32 devices in a mesh: orbits: 4 (over z), rows: 2 (over x), cols: 4 (over y, core).
Axes of the slice: x: 2, y: 2, z: 4, core: 2. Of those that a mesh axis runs over, the one named last changes fastest.
Arguments:
- obs_feat: bfloat16 [131072, 128], P(('orbits', 'rows', 'cols')), may hold values from -6 to 6
- obs_offset: bfloat16 [2, 131072], P(None, ('orbits', 'rows', 'cols')), may hold values from -0.5 to 0.5
- obs_cells: int32 [16, 131072], P(None, ('orbits', 'rows', 'cols')), may hold values from 0 to 255, as said below
- block_tile: int32 [1024], P(('orbits', 'rows', 'cols')), may hold values from 0 to 7, as said below
- block_patch: int32 [1024], P(('orbits', 'rows', 'cols')), may hold values from 0 to 31
- w_embed: bfloat16 [128, 128], replicated, may hold values from -0.5 to 0.5
- b_embed: float32 [128], replicated, may hold values from -3 to 3
- w_proj: bfloat16 [128, 128], replicated, may hold values from -0.5 to 0.5
- b_proj: float32 [128], replicated, may hold values from -3 to 3
- density_weight: float32 [128], replicated, may hold values from -4 to 4
- w_first: bfloat16 [3, 3, 128, 128], replicated, may hold values from -0.1875 to 0.1875
- b_first: float32 [128], replicated, may hold values from -3 to 3
- w_second: bfloat16 [3, 3, 128, 128], replicated, may hold values from -0.1875 to 0.1875
- b_second: float32 [128], replicated, may hold values from -3 to 3
Outputs:
- obs_out: bfloat16 [131072, 128], P(('orbits', 'rows', 'cols'))
- grid_out: bfloat16 [128, 512, 128], P(('orbits', 'rows'), 'cols')
The draws below stay inside these ranges and needn't reach their ends.
Inputs may be any that keep to these rules, and one draw needn't show every extreme that they name: `obs_cells`: column o is a 4 by 4 window of cells of a 8 by 32 patch: entry k is (a + k // 4) * 32 + b + k % 4 with 0 <= a <= 4 and 0 <= b <= 28. `block_tile`: tile t is the grid block of the devices with rows index t // 4 and cols index t % 4. Of the 32 blocks of one device, at most 8 name one tile, so one tile gets at most 64 blocks from the devices of one orbits index.
All inputs are finite; a program needn't handle non-finite values.
Results may differ from the reference program's by a relative error of at most 0.013.
Values may be sent and summed in bfloat16 or wider, within the bound.
No kernel may reach another device: no remote copies, remote signals or barrier semaphores. Data moves between devices by JAX's collectives and lax.ppermute only.
A program may use at most 64 MiB of HBM per device.

```python
import jax
import jax.numpy as jnp

C = 128
BLK = 128
KN = 16
PH = 8
PW = 32
NBLK_DEV = 32
SR = 16
TC = 128
TILES = 8
MOST = 8
PATCHES = 32
NBLK = 1024
OBS = 131072
GRID_ROWS = 128
GRID_COLS = 512
N_ROWS = 2


def draw_obs_cells(key, part):
    row_key, col_key = jax.random.split(key)
    anchor_row = jax.random.randint(row_key, (OBS,), 0, PH - 3)
    anchor_col = jax.random.randint(col_key, (OBS,), 0, PW - 3)
    tap_ids = jnp.arange(KN)
    cells = (anchor_row[None, :] + tap_ids[:, None] // 4) * PW + anchor_col[None, :] + tap_ids[:, None] % 4
    return cells.astype(jnp.int32)


def draw_block_tile(key, part):
    devices = NBLK // NBLK_DEV
    groups = devices // TILES
    busiest = jax.random.randint(jax.random.fold_in(key, 11), (groups,), 0, TILES)

    def one_device(device):
        device_key = jax.random.fold_in(key, 1000 + device)
        perm_key, shift_key, shuffle_key = jax.random.split(device_key, 3)
        centre = busiest[device // TILES]
        shuffled = jax.random.permutation(perm_key, TILES - 1)
        others = (centre + 1 + shuffled) % TILES
        shift_count = jax.random.randint(shift_key, (), 0, MOST)
        position = jnp.arange(NBLK_DEV - MOST)
        remaining = others[(position + shift_count) // MOST]
        chosen = jnp.concatenate([jnp.full((MOST,), centre, jnp.int32), remaining.astype(jnp.int32)])
        return chosen[jax.random.permutation(shuffle_key, NBLK_DEV)]
    return jax.vmap(one_device)(jnp.arange(devices)).reshape(NBLK).astype(jnp.int32)


def set_ends(result, own_key, smallest, top_value):
    longest = result.shape.index(max(result.shape))
    spots = []
    for shift in (0, 1):
        where = [jax.random.randint(jax.random.fold_in(own_key, axis), (), 0, length) for axis, length in enumerate(result.shape)]
        where[longest] = (where[longest] + shift) % result.shape[longest]
        spots.append(tuple(where))
    return result.at[spots[0]].set(smallest).at[spots[1]].set(top_value)


def level_of(stream_key, dims, cuts, smallest, high):
    factor_of, own = 1.0, jax.random.fold_in(stream_key, 6)
    for axis_at, blocks in cuts:
        draws = jnp.exp(jax.random.uniform(jax.random.fold_in(own, axis_at), (blocks,), jnp.float32, smallest / len(cuts), high / len(cuts)))
        factor_of = factor_of * jnp.repeat(draws, dims[axis_at] // blocks).reshape([-1 if axis == axis_at else 1 for axis in range(len(dims))])
    return factor_of


def scatter_about(rng, dims, scale, reach, shards=(), kind=jnp.bfloat16):
    array = scale * jax.random.normal(rng, dims, jnp.float32)
    if shards:
        array = array * level_of(rng, dims, shards, -0.22, 0.18)
    return jnp.clip(array, -reach, reach).astype(kind)


def setup_inputs(seed: int = 0) -> dict:
    key_of = jax.random.split(jax.random.key(seed), 15)
    obs_feat = scatter_about(key_of[0], (OBS, C), 1.0, 6.0, ((0, 32),))
    obs_offset = jnp.clip(jax.random.uniform(key_of[1], (2, OBS), jnp.float32, -0.5, 0.5) * level_of(key_of[1], (2, OBS), ((1, 32),), -0.4, 0.0), -0.5, 0.5).astype(jnp.bfloat16)
    obs_cells = draw_obs_cells(jax.random.fold_in(key_of[14], 71), 0)
    block_tile = draw_block_tile(jax.random.fold_in(key_of[14], 71), 0)
    block_patch = set_ends(jax.random.randint(key_of[4], (NBLK,), 0, PATCHES), jax.random.fold_in(key_of[4], 1), 0, PATCHES - 1).astype(jnp.int32)
    w_embed = scatter_about(key_of[5], (C, C), C ** -0.5, 0.5)
    b_embed = scatter_about(key_of[6], (C,), 0.5, 3.0, (), jnp.float32)
    w_proj = scatter_about(key_of[7], (C, C), C ** -0.5, 0.5)
    b_proj = scatter_about(key_of[8], (C,), 0.5, 3.0, (), jnp.float32)
    density_weight = scatter_about(key_of[9], (C,), 1.0, 4.0, (), jnp.float32)
    w_first = scatter_about(key_of[10], (3, 3, C, C), (9 * C) ** -0.5, 0.1875)
    b_first = scatter_about(key_of[11], (C,), 0.5, 3.0, (), jnp.float32)
    w_second = scatter_about(key_of[12], (3, 3, C, C), (9 * C) ** -0.5, 0.1875)
    b_second = scatter_about(key_of[13], (C,), 0.5, 3.0, (), jnp.float32)
    return dict(obs_feat=obs_feat, obs_offset=obs_offset, obs_cells=obs_cells, block_tile=block_tile, block_patch=block_patch, w_embed=w_embed, b_embed=b_embed, w_proj=w_proj, b_proj=b_proj, density_weight=density_weight, w_first=w_first, b_first=b_first, w_second=w_second, b_second=b_second)


inverse_width = 0.5


def kernel_taps(obs_offset):
    offsets = obs_offset.astype(jnp.float32)
    tap_ids = jnp.arange(KN)
    tap_row = (tap_ids // 4).astype(jnp.float32)
    tap_col = (tap_ids % 4).astype(jnp.float32)
    delta_row = tap_row[:, None] - 1.5 - offsets[0][None, :]
    delta_col = tap_col[:, None] - 1.5 - offsets[1][None, :]
    return jnp.exp(-(delta_row * delta_row + delta_col * delta_col) * inverse_width).astype(jnp.bfloat16)


def convolve(padded, weight, bias_vec):
    height = padded.shape[-3] - 2
    breadth = padded.shape[-2] - 2
    channels = padded.shape[-1]
    leading = padded.shape[:-3]
    summed = None
    for row_shift in range(3):
        rows_part = padded[..., row_shift:row_shift + height, :, :]
        stacked = jnp.concatenate([rows_part[..., col_shift:col_shift + breadth, :] for col_shift in range(3)], axis=-1)
        product_term = jnp.dot(stacked.reshape(-1, 3 * channels), weight[row_shift].reshape(3 * channels, channels), preferred_element_type=jnp.float32)
        summed = product_term if summed is None else summed + product_term
    return summed.reshape(leading + (height, breadth, channels)) + bias_vec


def reference(obs_feat, obs_offset, obs_cells, block_tile, block_patch, w_embed, b_embed, w_proj, b_proj, density_weight, w_first, b_first, w_second, b_second):
    hidden = jax.nn.silu(jnp.dot(obs_feat, w_embed, preferred_element_type=jnp.float32) + b_embed).astype(jnp.bfloat16)
    features = (jnp.dot(hidden, w_proj, preferred_element_type=jnp.float32) + b_proj).astype(jnp.bfloat16)
    features_wide = features.astype(jnp.float32)
    kernel = kernel_taps(obs_offset).astype(jnp.float32)
    tile_obs = jnp.repeat(block_tile, BLK).astype(jnp.int32)
    patch_obs = jnp.repeat(block_patch, BLK).astype(jnp.int32)
    tiles_across = GRID_COLS // TC
    patches_across = TC // PW
    tile_row = tile_obs // tiles_across
    tile_col = tile_obs % tiles_across
    patch_row = patch_obs // patches_across
    patch_col = patch_obs % patches_across
    local_row = patch_row[None, :] * PH + obs_cells // PW
    grid_row = ((local_row // SR) * N_ROWS + tile_row[None, :]) * SR + local_row % SR
    grid_col = tile_col[None, :] * TC + patch_col[None, :] * PW + obs_cells % PW
    flat_cell = (grid_row * GRID_COLS + grid_col).astype(jnp.int32)
    spread = jnp.zeros((GRID_ROWS * GRID_COLS, C), jnp.float32)
    density = jnp.zeros((GRID_ROWS * GRID_COLS,), jnp.float32)
    for tap in range(KN):
        spread = spread.at[flat_cell[tap]].add(kernel[tap][:, None] * features_wide)
        density = density.at[flat_cell[tap]].add(kernel[tap])
    grid_in = (spread / jnp.maximum(density, 1.0)[:, None] + density_weight[None, :] * (density / (1.0 + density))[:, None]).astype(jnp.bfloat16)
    grid_in = grid_in.reshape(GRID_ROWS, GRID_COLS, C)
    pads = ((1, 1), (1, 1), (0, 0))
    first = jax.nn.silu(convolve(jnp.pad(grid_in, pads), w_first, b_first)).astype(jnp.bfloat16)
    grid_out = (grid_in.astype(jnp.float32) + convolve(jnp.pad(first, pads), w_second, b_second)).astype(jnp.bfloat16)
    values = grid_out.reshape(GRID_ROWS * GRID_COLS, C)
    reading = jnp.zeros((OBS, C), jnp.float32)
    for tap in range(KN):
        reading = reading + kernel[tap][:, None] * values[flat_cell[tap]].astype(jnp.float32)
    reading = (reading / jnp.sum(kernel, axis=0)[:, None]).astype(jnp.bfloat16)
    obs_out = (features_wide + reading.astype(jnp.float32)).astype(jnp.bfloat16)
    return obs_out, grid_out
```

```python
import functools

import jax
import jax.numpy as jnp
from jax import lax
from jax.experimental import pallas as pl
from jax.experimental.pallas import tpu as pltpu
from jax.sharding import PartitionSpec as P

KN = 16
PH = 8
PW = 32
SR = 16
TC = 128
SIDE = 4
PAD = 8
META = 4
F32 = jnp.float32
BF16 = jnp.bfloat16

VMEM = pl.BlockSpec(memory_space=pltpu.VMEM)
SMEM = pl.BlockSpec(memory_space=pltpu.SMEM)
LIMIT = 48 * 1024 * 1024


def call(kernel, out_shape, in_specs, scratch, flops, moved):
    single = not isinstance(out_shape, (tuple, list))
    return pl.pallas_call(
        kernel,
        out_shape=out_shape,
        in_specs=in_specs,
        out_specs=VMEM if single else [VMEM] * len(out_shape),
        scratch_shapes=scratch,
        compiler_params=pltpu.CompilerParams(vmem_limit_bytes=LIMIT),
        cost_estimate=pl.CostEstimate(flops=flops, bytes_accessed=moved, transcendentals=0),
    )


def silu(v):
    half = 0.5 * v
    return half + half * jnp.tanh(half)


def each_slot(tile_ref, count_ref, most, body):
    for t in range(count_ref.shape[0]):
        count_ref[t] = 0
    for b in range(tile_ref.shape[0]):
        t = tile_ref[b]
        n = count_ref[t]
        count_ref[t] = n + 1
        body(b, t * most + n)


def meta_kernel(most, tile_ref, patch_ref, offset_ref, cells_ref, out_ref, count_ref):
    size = out_ref.shape[1]
    row = lax.broadcasted_iota(jnp.int32, out_ref.shape, 0) % META
    out_ref[...] = jnp.where(row == META - 1, 0.0, jnp.where(row == META - 2, -65536.0, 0.0))

    def put(b, slot):
        part = slice(b * size, (b + 1) * size)
        out_ref[pl.ds(slot * META, 2), :] = offset_ref[:, part].astype(F32)
        out_ref[pl.ds(slot * META + 2, 1), :] = cells_ref[0:1, part].astype(F32)
        out_ref[pl.ds(slot * META + 3, 1), :] = jnp.full((1, size), patch_ref[b], jnp.int32).astype(F32)

    each_slot(tile_ref, count_ref, most, put)


def embed_kernel(most, tile_ref, x_ref, we_ref, be_ref, wp_ref, bp_ref, feat_ref, send_ref, count_ref):
    blocks, size, channels = feat_ref.shape
    send_ref[...] = jnp.zeros(send_ref.shape, BF16)
    step = 4

    def some(i, unused):
        rows = pl.ds(pl.multiple_of(i * step * size, step * size), step * size)
        hidden = silu(jnp.dot(x_ref[rows, :], we_ref[...], preferred_element_type=F32) + be_ref[...])
        out = jnp.dot(hidden.astype(BF16), wp_ref[...], preferred_element_type=F32) + bp_ref[...]
        feat_ref[pl.ds(i * step, step)] = out.astype(BF16).reshape(step, size, channels)
        return unused

    lax.fori_loop(0, blocks // step, some, 0)

    def put(b, slot):
        send_ref[slot] = feat_ref[b]

    each_slot(tile_ref, count_ref, most, put)


def factors(meta, normal):
    off_row, off_col, corner = meta[0:1, :], meta[1:2, :], meta[2:3, :]
    first_row = jnp.floor(corner * (1.0 / PW))
    first_col = corner - first_row * PW

    def factor(count, start, off):
        at = lax.broadcasted_iota(jnp.int32, (count, meta.shape[1]), 0).astype(F32) - start
        delta = at - 1.5 - off
        value = jnp.exp(delta * delta * -0.5)
        return jnp.where((at >= 0.0) & (at < SIDE), value, 0.0)

    def total(off):
        at = lax.broadcasted_iota(jnp.int32, (SIDE, meta.shape[1]), 0).astype(F32)
        delta = at - 1.5 - off
        return jnp.sum(jnp.exp(delta * delta * -0.5), axis=0, keepdims=True)

    rows, cols = factor(PH, first_row, off_row), factor(PW, first_col, off_col)
    if normal:
        rows = rows / (total(off_row) * total(off_col))
    return rows, cols


def outer(rows, cols):
    return (rows[:, None, :] * cols[None, :, :]).reshape(PH * PW, rows.shape[1]).astype(BF16)


def spread_kernel(patch_ref, meta_ref, feat_ref, out_ref, acc_ref, dens_ref):
    slots = feat_ref.shape[0]
    across = TC // PW
    orbits = out_ref.shape[0]
    acc_ref[...] = jnp.zeros(acc_ref.shape, F32)
    dens_ref[...] = jnp.zeros(dens_ref.shape, F32)

    def pair(i, unused):
        metas = meta_ref[pl.ds(pl.multiple_of(i * 2 * META, 2 * META), 2 * META), :]
        for k in range(2):
            slot = i * 2 + k
            rows, cols = factors(metas[k * META : (k + 1) * META], False)
            matrix = outer(rows, cols)
            patch = patch_ref[slot]
            part = jnp.dot(matrix, feat_ref[slot], preferred_element_type=F32)
            at = (
                pl.ds(pl.multiple_of(patch // across * PH, PH), PH),
                pl.ds(pl.multiple_of(patch % across * PW, PW), PW),
            )
            acc_ref[at] += part.reshape(PH, PW, part.shape[1])
            dens_ref[patch] += lax.dot_general(
                rows.astype(BF16), cols.astype(BF16), (((1,), (1,)), ((), ())), preferred_element_type=F32
            )
        return unused

    lax.fori_loop(0, slots // 2, pair, 0)
    channels = acc_ref.shape[2]
    for z in range(orbits):
        out_ref[z, 0 : SR * TC, :] = acc_ref[z * SR : (z + 1) * SR].reshape(SR * TC, channels).astype(BF16)
        bands = []
        for band in range(SR // PH):
            first = (z * (SR // PH) + band) * across
            bands.append(jnp.concatenate([dens_ref[first + c] for c in range(across)], axis=1))
        out_ref[z, SR * TC :, :] = jnp.concatenate(bands, axis=0).astype(BF16)


def grid_kernel(part_ref, weight_ref, out_ref):
    density = part_ref[SR * TC :, :].astype(F32).T
    for i in range(SR):
        d = jnp.broadcast_to(density[:, i : i + 1], (TC, out_ref.shape[2]))
        spread = part_ref[i * TC : (i + 1) * TC, :].astype(F32)
        out_ref[i] = (spread / jnp.maximum(d, 1.0) + weight_ref[...] * (d / (1.0 + d))).astype(BF16)


def conv_kernel(
    edge_ref, x_ref, up_ref, down_ref, left_ref, right_ref, w1_ref, b1_ref, w2_ref, b2_ref,
    out_ref, wide_ref, x16_ref, first_ref, wc1_ref, wc2_ref,
):
    channels = out_ref.shape[2]
    width = x16_ref.shape[1]
    for a in range(3):
        for b in range(3):
            at = (slice(a * channels, (a + 1) * channels), slice(b * channels, (b + 1) * channels))
            wc1_ref[at] = w1_ref[a, b]
            wc2_ref[at] = w2_ref[a, b]
    body = slice(PAD, PAD + TC)
    wide_ref[...] = jnp.zeros(wide_ref.shape, F32)
    wide_ref[0:2, body] = up_ref[...].astype(F32)
    wide_ref[2 : 2 + SR, body] = x_ref[...].astype(F32)
    wide_ref[2 + SR :, body] = down_ref[...].astype(F32)
    wide_ref[:, PAD - 2 : PAD] = left_ref[...].astype(F32)
    wide_ref[:, PAD + TC : PAD + TC + 2] = right_ref[...].astype(F32)
    x16_ref[...] = wide_ref[...].astype(BF16)

    def taps(source, i, weights):
        rows = jnp.concatenate([source[i], source[i + 1], source[i + 2]], axis=1)
        all_taps = jnp.dot(rows, weights[...], preferred_element_type=F32)
        return (
            pltpu.roll(all_taps[:, :channels], 1, 0)
            + all_taps[:, channels : 2 * channels]
            + pltpu.roll(all_taps[:, 2 * channels :], width - 1, 0)
        )

    col = lax.broadcasted_iota(jnp.int32, (width, channels), 0)
    inside = (col >= PAD - edge_ref[2]) & (col < PAD + TC + edge_ref[3])

    def first_row(i, unused):
        value = silu(taps(x16_ref, i, wc1_ref) + b1_ref[...])
        low = jnp.where(edge_ref[0] == 1, 0, 1)
        high = jnp.where(edge_ref[1] == 1, SR + 2, SR + 1)
        keep = inside & (i >= low) & (i < high)
        first_ref[i] = jnp.where(keep, value, 0.0).astype(BF16)
        return unused

    lax.fori_loop(0, SR + 2, first_row, 0)

    def second_row(i, unused):
        value = taps(first_ref, i, wc2_ref) + b2_ref[...]
        out_ref[i] = (value[PAD : PAD + TC] + x_ref[i].astype(F32)).astype(BF16)
        return unused

    lax.fori_loop(0, SR, second_row, 0)


def read_kernel(patch_ref, meta_ref, grid_ref, out_ref):
    slots = out_ref.shape[0]
    across = TC // PW

    def pair(i, unused):
        metas = meta_ref[pl.ds(pl.multiple_of(i * 2 * META, 2 * META), 2 * META), :]
        for k in range(2):
            slot = i * 2 + k
            rows, cols = factors(metas[k * META : (k + 1) * META], True)
            matrix = outer(rows, cols)
            patch = patch_ref[slot]
            values = grid_ref[
                pl.ds(pl.multiple_of(patch // across * PH, PH), PH),
                pl.ds(pl.multiple_of(patch % across * PW, PW), PW),
            ].reshape(PH * PW, grid_ref.shape[2])
            out_ref[slot] = lax.dot_general(
                matrix, values, (((0,), (0,)), ((), ())), preferred_element_type=F32
            ).astype(BF16)
        return unused

    lax.fori_loop(0, slots // 2, pair, 0)


def final_kernel(most, tile_ref, feat_ref, got_ref, out_ref, count_ref):
    def put(b, slot):
        out_ref[b] = (feat_ref[b].astype(F32) + got_ref[slot].astype(F32)).astype(BF16)

    each_slot(tile_ref, count_ref, most, put)


def shifts(axis):
    size = lax.axis_size(axis)
    up = [(i, i + 1) for i in range(size - 1)]
    return up, [(j, i) for i, j in up]


def halo(x, axis, dim, width):
    up, down = shifts(axis)
    length = x.shape[dim]
    before = lax.ppermute(lax.slice_in_dim(x, length - width, length, axis=dim), axis, up)
    after = lax.ppermute(lax.slice_in_dim(x, 0, width, axis=dim), axis, down)
    return before, after


def local(
    obs_feat, obs_offset, obs_cells, block_tile, block_patch, w_embed, b_embed, w_proj, b_proj,
    density_weight, w_first, b_first, w_second, b_second,
):
    channels = obs_feat.shape[1]
    blocks = block_tile.shape[0]
    size = obs_feat.shape[0] // blocks
    plane = ("rows", "cols")
    tiles = lax.axis_size(plane)
    orbits = lax.axis_size("orbits")
    most = max(2, 2 * blocks // tiles)
    slots = tiles * most
    height = orbits * SR
    patches = height // PH * (TC // PW)
    counts = pltpu.SMEM((tiles,), jnp.int32)
    shape = jax.ShapeDtypeStruct
    bias = lambda b: b.reshape(1, channels)

    meta = call(
        functools.partial(meta_kernel, most),
        shape((slots * META, size), F32),
        [SMEM, SMEM, VMEM, VMEM],
        [counts],
        1000000,
        obs_cells.size * 4,
    )(block_tile, block_patch, obs_offset, obs_cells)
    got_meta = lax.all_to_all(
        meta.reshape(tiles, most * META, size), plane, split_axis=0, concat_axis=0, tiled=True
    ).reshape(slots * META, size)
    features, send = call(
        functools.partial(embed_kernel, most),
        (shape((blocks, size, channels), BF16), shape((slots, size, channels), BF16)),
        [SMEM, VMEM, VMEM, VMEM, VMEM, VMEM],
        [counts],
        4 * obs_feat.size * channels,
        8 * obs_feat.size,
    )(block_tile, obs_feat, w_embed, bias(b_embed), w_proj, bias(b_proj))
    got = lax.all_to_all(
        send.reshape(tiles, most, size, channels), plane, split_axis=0, concat_axis=0, tiled=True
    ).reshape(slots, size, channels)
    got_patch = got_meta.reshape(slots, META, size)[:, META - 1, 0].astype(jnp.int32)

    matmul_flops = 2 * slots * size * channels * PH * PW
    partial = call(
        spread_kernel,
        shape((orbits, SR * TC + SR, channels), BF16),
        [SMEM, VMEM, VMEM],
        [pltpu.VMEM((height, TC, channels), F32), pltpu.VMEM((patches, PH, PW), F32)],
        matmul_flops,
        8 * slots * size * channels,
    )(got_patch, got_meta, got)
    part = lax.psum_scatter(
        partial.reshape(orbits * (SR * TC + SR), channels), "orbits", scatter_dimension=0, tiled=True
    )
    grid_in = call(
        grid_kernel, shape((SR, TC, channels), BF16), [VMEM, VMEM], [], 10000000, 4 * part.size
    )(part, bias(density_weight))

    stripe = ("orbits", "rows")
    above, below = halo(grid_in, stripe, 0, 2)
    extended = jnp.concatenate(
        [jnp.concatenate([above[:, c], grid_in[:, c], below[:, c]], axis=0) for c in (slice(0, 2), slice(TC - 2, TC))],
        axis=1,
    )
    left, right = halo(extended, "cols", 1, 2)
    at_row, at_col = lax.axis_index(stripe), lax.axis_index("cols")
    edges = jnp.stack(
        [
            at_row > 0,
            at_row < lax.axis_size(stripe) - 1,
            at_col > 0,
            at_col < lax.axis_size("cols") - 1,
        ]
    ).astype(jnp.int32)
    width = TC + 2 * PAD
    grid_out = call(
        conv_kernel,
        shape((SR, TC, channels), BF16),
        [SMEM] + [VMEM] * 9,
        [
            pltpu.VMEM((SR + 4, width, channels), F32),
            pltpu.VMEM((SR + 4, width, channels), BF16),
            pltpu.VMEM((SR + 2, width, channels), BF16),
            pltpu.VMEM((3 * channels, 3 * channels), BF16),
            pltpu.VMEM((3 * channels, 3 * channels), BF16),
        ],
        4 * 9 * SR * TC * channels * channels,
        4 * grid_in.size,
    )(edges, grid_in, above, below, left, right, w_first, bias(b_first), w_second, bias(b_second))

    whole = lax.all_gather(grid_out, "orbits", axis=0, tiled=True)
    readings = call(
        read_kernel,
        shape((slots, size, channels), BF16),
        [SMEM, VMEM, VMEM],
        [],
        matmul_flops,
        8 * slots * size * channels,
    )(got_patch, got_meta, whole)
    returned = lax.all_to_all(
        readings.reshape(tiles, most, size, channels), plane, split_axis=0, concat_axis=0, tiled=True
    ).reshape(slots, size, channels)
    obs_out = call(
        functools.partial(final_kernel, most),
        shape((blocks, size, channels), BF16),
        [SMEM, VMEM, VMEM],
        [counts],
        1000000,
        8 * obs_feat.size,
    )(block_tile, features, returned)
    return obs_out.reshape(obs_feat.shape), grid_out


def solution(mesh):
    spread_out = ("orbits", "rows", "cols")
    in_specs = (
        P(spread_out, None),
        P(None, spread_out),
        P(None, spread_out),
        P(spread_out),
        P(spread_out),
    ) + (P(),) * 9
    out_specs = (P(spread_out, None), P(("orbits", "rows"), "cols", None))
    return jax.shard_map(local, mesh=mesh, in_specs=in_specs, out_specs=out_specs, check_vma=False)
```

```python
import functools

import jax
import jax.numpy as jnp
from jax import lax
from jax.experimental import pallas as pl
from jax.experimental.pallas import tpu as pltpu
from jax.sharding import PartitionSpec as P

KN = 16
PH = 8
PW = 32
SR = 16
TC = 128
SIDE = 4
PAD = 8
META = 4
ACROSS = TC // PW
F32 = jnp.float32
BF16 = jnp.bfloat16

SMEM = pl.BlockSpec(memory_space=pltpu.SMEM)
LIMIT = 48 * 1024 * 1024


def whole(shape):
    zeros = (0,) * len(shape)
    return pl.BlockSpec(tuple(shape), lambda i: zeros)


def part(shape, *rest):
    tail = rest or (0,) * (len(shape) - 1)
    return pl.BlockSpec(tuple(shape), lambda i: (i,) + tuple(tail))


def call(kernel, grid, in_specs, out_specs, out_shape, scratch, flops, moved, *args):
    return pl.pallas_call(
        kernel,
        grid=(grid,),
        in_specs=in_specs,
        out_specs=out_specs,
        out_shape=out_shape,
        scratch_shapes=scratch,
        compiler_params=pltpu.CompilerParams(vmem_limit_bytes=LIMIT),
        cost_estimate=pl.CostEstimate(flops=flops, bytes_accessed=moved, transcendentals=0),
    )(*args)


def silu(v):
    half = 0.5 * v
    return half + half * jnp.tanh(half)


def swap(x):
    axis = x.ndim - 1
    return pltpu.roll(x.astype(F32), x.shape[axis] // 2, axis).astype(x.dtype)


def lanes(shape):
    return lax.broadcasted_iota(jnp.int32, shape, len(shape) - 1) // (shape[-1] // 2)


def next_slot(tile_ref, count_ref, b):
    t = tile_ref[b]
    n = count_ref[t]
    count_ref[t] = n + 1
    return t, n


def clear(count_ref):
    for t in range(count_ref.shape[0]):
        count_ref[t] = 0


def embed_kernel(
    tile_ref, patch_ref, offset_ref, cells_ref, x_ref, we_ref, be_ref, wp_ref, bp_ref,
    feat_ref, send0_ref, send1_ref, count_ref, meta_ref, wide_ref, bias_ref,
):
    step = pl.program_id(0)
    per, size, channels = feat_ref.shape
    tiles = send0_ref.shape[0]
    meta_rows = meta_ref.shape[0] // tiles

    @pl.when(step == 0)
    def _():
        clear(count_ref)
        send0_ref[...] = jnp.zeros(send0_ref.shape, BF16)
        send1_ref[...] = jnp.zeros(send1_ref.shape, BF16)
        row = lax.broadcasted_iota(jnp.int32, meta_ref.shape, 0) % META
        meta_ref[...] = jnp.where(row == 2, -65536.0, 0.0)
        wide_ref[:, :channels] = wp_ref[...]
        wide_ref[:, channels:] = swap(wp_ref[...])
        bias_ref[:, :channels] = bp_ref[...]
        bias_ref[:, channels:] = swap(bp_ref[...])

    hidden = silu(jnp.dot(x_ref[...], we_ref[...], preferred_element_type=F32) + be_ref[...])
    both = jnp.dot(hidden.astype(BF16), wide_ref[...], preferred_element_type=F32) + bias_ref[...]
    feat_ref[...] = both[:, :channels].astype(BF16).reshape(feat_ref.shape)
    group = lanes((size, channels))
    for k in range(per):
        b = step * per + k
        t, n = next_slot(tile_ref, count_ref, b)
        odd = lax.rem(n, 2)
        at = pl.ds(pl.multiple_of(n // 2 * size, size), size)
        straight = both[k * size : (k + 1) * size, :channels]
        turned = both[k * size : (k + 1) * size, channels:]
        keep = group == odd
        low = jnp.where(keep, jnp.where(odd == 0, straight, turned), 0.0).astype(BF16)
        high = jnp.where(keep, jnp.where(odd == 0, turned, straight), 0.0).astype(BF16)
        send0_ref[t, at, :] += low
        send1_ref[t, at, :] += high
        first = t * meta_rows + n * META
        obs = pl.ds(pl.multiple_of(b * size, size), size)
        meta_ref[pl.ds(first, 2), :] = offset_ref[:, obs].astype(F32)
        meta_ref[pl.ds(first + 2, 1), :] = cells_ref[0:1, obs].astype(F32)
        meta_ref[pl.ds(first + 3, 1), :] = jnp.full((1, size), patch_ref[b], jnp.int32).astype(F32)

    @pl.when(step == pl.num_programs(0) - 1)
    def _():
        base = send1_ref.shape[1]
        extra = send0_ref.shape[1] - base - meta_rows
        for t in range(tiles):
            rows = meta_ref[t * meta_rows : (t + 1) * meta_rows, :]
            if extra:
                rows = jnp.concatenate([rows, jnp.zeros((extra, size), F32)], axis=0)
            send0_ref[t, base:, :] = rows.astype(BF16)


def factors(meta, normal):
    off_row, off_col, corner = meta[0:1, :], meta[1:2, :], meta[2:3, :]
    first_row = jnp.floor(corner * (1.0 / PW))
    first_col = corner - first_row * PW

    def factor(count, start, off):
        at = lax.broadcasted_iota(jnp.int32, (count, meta.shape[1]), 0).astype(F32) - start
        delta = at - 1.5 - off
        value = jnp.exp(delta * delta * -0.5)
        return jnp.where((at >= 0.0) & (at < SIDE), value, 0.0)

    def total(off):
        at = lax.broadcasted_iota(jnp.int32, (SIDE, meta.shape[1]), 0).astype(F32)
        delta = at - 1.5 - off
        return jnp.sum(jnp.exp(delta * delta * -0.5), axis=0, keepdims=True)

    rows, cols = factor(PH, first_row, off_row), factor(PW, first_col, off_col)
    if normal:
        rows = rows / (total(off_row) * total(off_col))
    return rows, cols


def outer(rows, cols):
    return (rows[:, None, :] * cols[None, :, :]).reshape(PH * PW, rows.shape[1])


def place(patch):
    row, col = patch // ACROSS, lax.rem(patch, ACROSS)
    halves = ACROSS // 2
    return (
        pl.ds(pl.multiple_of(row * PH, PH), PH),
        pl.ds(pl.multiple_of(lax.rem(col, halves) * PW, PW), PW),
        col // halves,
    )


def add_slot(acc_ref, matrix, packed, turned, odd, patch):
    at_row, at_col, half = place(patch)
    keep = lanes((1, packed.shape[1])) == half
    values = jnp.where(half == odd, packed, turned) * jnp.where(keep, 1.0, 0.0).astype(BF16)
    result = jnp.dot(matrix, values, preferred_element_type=F32)
    acc_ref[at_row, at_col, :] += result.reshape(PH, PW, result.shape[1])


def write_stripes(ring_ref, acc_ref, outs):
    for k, out_ref in enumerate(outs):
        z = ring_ref[k]
        stripe = acc_ref[pl.ds(z * SR, SR)].astype(BF16)
        out_ref[0 : SR * TC // 2, :] = stripe.reshape(SR * TC // 2, stripe.shape[2])


def spread0_kernel(orbits, most, ring_ref, got_ref, *refs):
    outs, (matrix_ref, patch_ref, acc_ref, dens_ref) = refs[:orbits], refs[orbits:]
    t = pl.program_id(0)
    size = got_ref.shape[2]

    @pl.when(t == 0)
    def _():
        acc_ref[...] = jnp.zeros(acc_ref.shape, F32)
        dens_ref[...] = jnp.zeros(dens_ref.shape, F32)

    base = most // 2 * size
    metas = got_ref[0, base:, :].astype(F32)
    patches = [jnp.max(metas[n * META + 3 : n * META + 4, :]).astype(jnp.int32) for n in range(most)]
    for pair in range(most // 2):
        packed = got_ref[0, pair * size : (pair + 1) * size, :]
        turned = swap(packed)
        for odd in range(2):
            n = pair * 2 + odd
            patch = patches[n]
            patch_ref[t * most + n] = patch
            rows, cols = factors(metas[n * META : (n + 1) * META], False)
            matrix = outer(rows, cols).astype(BF16)
            matrix_ref[n] = matrix
            add_slot(acc_ref, matrix, packed, turned, odd, patch)
            dens_ref[patch] += lax.dot_general(
                rows.astype(BF16), cols.astype(BF16), (((1,), (1,)), ((), ())), preferred_element_type=F32
            )

    @pl.when(t == pl.num_programs(0) - 1)
    def _():
        write_stripes(ring_ref, acc_ref, outs)
        for k, out_ref in enumerate(outs):
            bands = []
            for band in range(SR // PH):
                first = (ring_ref[k] * (SR // PH) + band) * ACROSS
                bands.append(jnp.concatenate([dens_ref[first + c] for c in range(ACROSS)], axis=1))
            out_ref[SR * TC // 2 :, :] = jnp.concatenate(bands, axis=0).astype(BF16)


def spread1_kernel(orbits, most, ring_ref, patch_ref, matrix_ref, got_ref, *refs):
    outs, (acc_ref,) = refs[:orbits], refs[orbits:]
    t = pl.program_id(0)
    size = got_ref.shape[2]

    @pl.when(t == 0)
    def _():
        acc_ref[...] = jnp.zeros(acc_ref.shape, F32)

    for pair in range(most // 2):
        packed = got_ref[0, pair * size : (pair + 1) * size, :]
        turned = swap(packed)
        for odd in range(2):
            n = pair * 2 + odd
            add_slot(acc_ref, matrix_ref[n], packed, turned, odd, patch_ref[t * most + n])

    @pl.when(t == pl.num_programs(0) - 1)
    def _():
        write_stripes(ring_ref, acc_ref, outs)


def weights_kernel(most, meta_ref, out_ref):
    metas = meta_ref[0].astype(F32)
    for n in range(most):
        rows, cols = factors(metas[n * META : (n + 1) * META], True)
        out_ref[n] = outer(rows, cols).T.astype(BF16)


def grid_kernel(own0_ref, sum0_ref, own1_ref, sum1_ref, weight_ref, out_ref):
    half = TC // 2
    channels = out_ref.shape[2]
    tail = slice(SR * half, SR * half + SR)
    density = (own0_ref[tail, :].astype(F32) + sum0_ref[tail, :].astype(F32)).T
    low = lanes((half, channels)) == 0
    for i in range(SR):
        at = slice(i * half, (i + 1) * half)
        a = own0_ref[at, :].astype(F32) + sum0_ref[at, :].astype(F32)
        b = own1_ref[at, :].astype(F32) + sum1_ref[at, :].astype(F32)
        spread = jnp.concatenate([jnp.where(low, a, swap(b)), jnp.where(low, swap(a), b)], axis=0)
        d = jnp.broadcast_to(density[:, i : i + 1], (TC, channels))
        out_ref[i] = (spread / jnp.maximum(d, 1.0) + weight_ref[...] * (d / (1.0 + d))).astype(BF16)


def conv_kernel(
    edge_ref, x_ref, up_ref, down_ref, left_ref, right_ref, w1_ref, b1_ref, w2_ref, b2_ref,
    out_ref, out0_ref, out1_ref, wide_ref, x16_ref, first_ref, wc1_ref, wc2_ref,
):
    channels = out_ref.shape[2]
    width = x16_ref.shape[1]
    half = TC // 2
    for a in range(3):
        for b in range(3):
            at = (slice(a * channels, (a + 1) * channels), slice(b * channels, (b + 1) * channels))
            wc1_ref[at] = w1_ref[a, b]
            wc2_ref[at] = w2_ref[a, b]
    body = slice(PAD, PAD + TC)
    wide_ref[...] = jnp.zeros(wide_ref.shape, F32)
    wide_ref[0:2, body] = up_ref[...].astype(F32)
    wide_ref[2 : 2 + SR, body] = x_ref[...].astype(F32)
    wide_ref[2 + SR :, body] = down_ref[...].astype(F32)
    wide_ref[:, PAD - 2 : PAD] = left_ref[...].astype(F32)
    wide_ref[:, PAD + TC : PAD + TC + 2] = right_ref[...].astype(F32)
    x16_ref[...] = wide_ref[...].astype(BF16)

    def taps(source, i, weights):
        rows = jnp.concatenate([source[i], source[i + 1], source[i + 2]], axis=1)
        all_taps = jnp.dot(rows, weights[...], preferred_element_type=F32)
        return (
            pltpu.roll(all_taps[:, :channels], 1, 0)
            + all_taps[:, channels : 2 * channels]
            + pltpu.roll(all_taps[:, 2 * channels :], width - 1, 0)
        )

    col = lax.broadcasted_iota(jnp.int32, (width, channels), 0)
    inside = (col >= PAD - edge_ref[2]) & (col < PAD + TC + edge_ref[3])

    def first_row(i, unused):
        value = silu(taps(x16_ref, i, wc1_ref) + b1_ref[...])
        low = jnp.where(edge_ref[0] == 1, 0, 1)
        high = jnp.where(edge_ref[1] == 1, SR + 2, SR + 1)
        keep = inside & (i >= low) & (i < high)
        first_ref[i] = jnp.where(keep, value, 0.0).astype(BF16)
        return unused

    lax.fori_loop(0, SR + 2, first_row, 0)
    group = lanes((half, channels)) == 0

    def second_row(i, unused):
        value = taps(first_ref, i, wc2_ref) + b2_ref[...]
        value = value[PAD : PAD + TC] + x_ref[i].astype(F32)
        left, right = value[:half], value[half:]
        out_ref[i] = value.astype(BF16)
        out0_ref[i] = jnp.where(group, left, swap(right)).astype(BF16)
        out1_ref[i] = jnp.where(group, swap(left), right).astype(BF16)
        return unused

    lax.fori_loop(0, SR, second_row, 0)


def read_kernel(orbits, most, ring_ref, patch_ref, weights_ref, *refs):
    pieces, (out_ref, grid_ref) = refs[:orbits], refs[orbits:]
    t = pl.program_id(0)
    size = out_ref.shape[2]

    @pl.when(t == 0)
    def _():
        for k, piece_ref in enumerate(pieces):
            at = pl.ds(ring_ref[k] * SR, SR)
            grid_ref[0, at] = piece_ref[...]
            grid_ref[1, at] = swap(piece_ref[...])

    low = lanes((size, out_ref.shape[2])) == 0
    for pair in range(most // 2):
        sums = []
        for odd in range(2):
            n = pair * 2 + odd
            at_row, at_col, half = place(patch_ref[t * most + n])
            turn = jnp.where(half == odd, 0, 1)
            values = grid_ref[turn, at_row, at_col, :].reshape(PH * PW, grid_ref.shape[3])
            sums.append(jnp.dot(weights_ref[n], values, preferred_element_type=F32))
        out_ref[0, pair * size : (pair + 1) * size, :] = jnp.where(low, sums[0], sums[1]).astype(BF16)


def final_kernel(tile_ref, feat_ref, got0_ref, got1_ref, out_ref, count_ref):
    step = pl.program_id(0)
    per, size, channels = feat_ref.shape

    @pl.when(step == 0)
    def _():
        clear(count_ref)

    low = lanes((size, channels)) == 0
    for k in range(per):
        t, n = next_slot(tile_ref, count_ref, step * per + k)
        odd = lax.rem(n, 2)
        at = pl.ds(pl.multiple_of(n // 2 * size, size), size)
        a, b = got0_ref[t, at, :].astype(F32), got1_ref[t, at, :].astype(F32)
        turn = swap(jnp.where(odd == 0, b, a))
        mine = jnp.where(odd == 0, jnp.where(low, a, turn), jnp.where(low, turn, b))
        out_ref[k] = (feat_ref[k].astype(F32) + mine).astype(BF16)


def shifts(axis):
    size = lax.axis_size(axis)
    up = [(i, i + 1) for i in range(size - 1)]
    return up, [(j, i) for i, j in up]


def halo(x, axis, dim, width):
    up, down = shifts(axis)
    length = x.shape[dim]
    before = lax.ppermute(lax.slice_in_dim(x, length - width, length, axis=dim), axis, up)
    after = lax.ppermute(lax.slice_in_dim(x, 0, width, axis=dim), axis, down)
    return before, after


def turn(x, way):
    size = lax.axis_size("orbits")
    return lax.ppermute(x, "orbits", [(i, (i + way) % size) for i in range(size)])


def ring_sum(stripes, way):
    total = None
    for stripe in stripes[:-1]:
        total = turn(stripe if total is None else stripe + total, way)
    return total


def ring_gather(x, way):
    pieces = [x]
    for _ in range(lax.axis_size("orbits") - 1):
        pieces.append(turn(pieces[-1], way))
    return pieces


def local(
    obs_feat, obs_offset, obs_cells, block_tile, block_patch, w_embed, b_embed, w_proj, b_proj,
    density_weight, w_first, b_first, w_second, b_second,
):
    channels = obs_feat.shape[1]
    blocks = block_tile.shape[0]
    size = obs_feat.shape[0] // blocks
    plane = ("rows", "cols")
    tiles = lax.axis_size(plane)
    orbits = lax.axis_size("orbits")
    most = max(2, 2 * blocks // tiles)
    slots = tiles * most
    height = orbits * SR
    patches = height // PH * ACROSS
    half = TC // 2
    pairs = most // 2 * size
    meta_rows = max(16, most * META)
    per = 4
    counts = pltpu.SMEM((tiles,), jnp.int32)
    shape = jax.ShapeDtypeStruct
    bias = lambda b: b.reshape(1, channels)
    me = lax.axis_index("orbits")
    order = jnp.arange(orbits, dtype=jnp.int32)
    exchange = lambda x: lax.all_to_all(x, plane, split_axis=0, concat_axis=0, tiled=True)

    features, send0, send1 = call(
        embed_kernel,
        blocks // per,
        [SMEM, SMEM, whole(obs_offset.shape), whole((8, obs_cells.shape[1])), part((per * size, channels))]
        + [whole((channels, channels)), whole((1, channels))] * 2,
        [
            part((per, size, channels)),
            whole((tiles, pairs + meta_rows, channels)),
            whole((tiles, pairs, channels)),
        ],
        (
            shape((blocks, size, channels), BF16),
            shape((tiles, pairs + meta_rows, channels), BF16),
            shape((tiles, pairs, channels), BF16),
        ),
        [
            counts,
            pltpu.VMEM((slots * META, size), F32),
            pltpu.VMEM((channels, 2 * channels), BF16),
            pltpu.VMEM((1, 2 * channels), F32),
        ],
        6 * obs_feat.size * channels,
        8 * obs_feat.size,
        block_tile, block_patch, obs_offset, obs_cells, obs_feat, w_embed, bias(b_embed), w_proj, bias(b_proj),
    )
    got0 = exchange(send0)
    got1 = exchange(send1)

    flops = 2 * slots * size * channels * PH * PW
    stripe_shape = shape((SR * half, channels), BF16)
    dense_shape = shape((SR * half + SR, channels), BF16)
    acc = pltpu.VMEM((height, half, channels), F32)
    *out0, matrices, patch_of = call(
        functools.partial(spread0_kernel, orbits, most),
        tiles,
        [SMEM, part((1, pairs + meta_rows, channels))],
        [whole(dense_shape.shape)] * orbits + [part((most, PH * PW, size)), SMEM],
        [dense_shape] * orbits + [shape((slots, PH * PW, size), BF16), shape((slots,), jnp.int32)],
        [acc, pltpu.VMEM((patches, PH, PW), F32)],
        flops,
        12 * slots * size * channels,
        (me - 1 - order) % orbits, got0,
    )
    sum0 = ring_sum(out0, 1)
    out1 = call(
        functools.partial(spread1_kernel, orbits, most),
        tiles,
        [SMEM, SMEM, part((most, PH * PW, size)), part((1, pairs, channels))],
        [whole(stripe_shape.shape)] * orbits,
        [stripe_shape] * orbits,
        [acc],
        flops,
        8 * slots * size * channels,
        (me + 1 + order) % orbits, patch_of, matrices, got1,
    )
    sum1 = ring_sum(out1, -1)
    weights = call(
        functools.partial(weights_kernel, most),
        tiles,
        [part((1, meta_rows, channels), pairs // meta_rows, 0)],
        part((most, size, PH * PW)),
        shape((slots, size, PH * PW), BF16),
        [],
        flops,
        4 * slots * size * channels,
        got0,
    )
    grid_in = call(
        grid_kernel,
        1,
        [whole(dense_shape.shape)] * 2 + [whole(stripe_shape.shape)] * 2 + [whole((1, channels))],
        whole((SR, TC, channels)),
        shape((SR, TC, channels), BF16),
        [],
        10000000,
        8 * SR * TC * channels,
        out0[-1], sum0, out1[-1], sum1, bias(density_weight),
    )

    stripe = ("orbits", "rows")
    above, below = halo(grid_in, stripe, 0, 2)
    extended = jnp.concatenate(
        [
            jnp.concatenate([above[:, c], grid_in[:, c], below[:, c]], axis=0)
            for c in (slice(0, 2), slice(TC - 2, TC))
        ],
        axis=1,
    )
    left, right = halo(extended, "cols", 1, 2)
    at_row, at_col = lax.axis_index(stripe), lax.axis_index("cols")
    edges = jnp.stack(
        [
            at_row > 0,
            at_row < lax.axis_size(stripe) - 1,
            at_col > 0,
            at_col < lax.axis_size("cols") - 1,
        ]
    ).astype(jnp.int32)
    width = TC + 2 * PAD
    weight_spec = whole(w_first.shape)
    grid_out, half0, half1 = call(
        conv_kernel,
        1,
        [SMEM]
        + [whole(a.shape) for a in (grid_in, above, below, left, right)]
        + [weight_spec, whole((1, channels))] * 2,
        [whole((SR, TC, channels)), whole((SR, half, channels)), whole((SR, half, channels))],
        [shape((SR, TC, channels), BF16)] + [shape((SR, half, channels), BF16)] * 2,
        [
            pltpu.VMEM((SR + 4, width, channels), F32),
            pltpu.VMEM((SR + 4, width, channels), BF16),
            pltpu.VMEM((SR + 2, width, channels), BF16),
            pltpu.VMEM((3 * channels, 3 * channels), BF16),
            pltpu.VMEM((3 * channels, 3 * channels), BF16),
        ],
        4 * 9 * SR * TC * channels * channels,
        8 * grid_in.size,
        edges, grid_in, above, below, left, right, w_first, bias(b_first), w_second, bias(b_second),
    )

    def readings(pieces, ring):
        return call(
            functools.partial(read_kernel, orbits, most),
            tiles,
            [SMEM, SMEM, part((most, size, PH * PW))] + [whole((SR, half, channels))] * orbits,
            part((1, pairs, channels)),
            shape((tiles, pairs, channels), BF16),
            [pltpu.VMEM((2, height, half, channels), BF16)],
            flops,
            8 * slots * size * channels,
            ring, patch_of, weights, *pieces,
        )

    back0 = exchange(readings(ring_gather(half0, 1), (me - order) % orbits))
    back1 = exchange(readings(ring_gather(half1, -1), (me + order) % orbits))
    block = part((per, size, channels))
    obs_out = call(
        final_kernel,
        blocks // per,
        [SMEM, block] + [whole((tiles, pairs, channels))] * 2,
        block,
        shape((blocks, size, channels), BF16),
        [counts],
        1000000,
        8 * obs_feat.size,
        block_tile, features, back0, back1,
    )
    return obs_out.reshape(obs_feat.shape), grid_out


def solution(mesh):
    spread_out = ("orbits", "rows", "cols")
    in_specs = (
        P(spread_out, None),
        P(None, spread_out),
        P(None, spread_out),
        P(spread_out),
        P(spread_out),
    ) + (P(),) * 9
    out_specs = (P(spread_out, None), P(("orbits", "rows"), "cols", None))
    return jax.shard_map(local, mesh=mesh, in_specs=in_specs, out_specs=out_specs, check_vma=False)
```

```python
import functools

import jax
import jax.numpy as jnp
from jax import lax
from jax.experimental import pallas as pl
from jax.experimental.pallas import tpu as pltpu
from jax.sharding import PartitionSpec as P

KN = 16
PH = 8
PW = 32
SR = 16
TC = 128
SIDE = 4
PAD = 8
META = 4
ACROSS = TC // PW
F32 = jnp.float32
BF16 = jnp.bfloat16

VMEM = pl.BlockSpec(memory_space=pltpu.VMEM)
SMEM = pl.BlockSpec(memory_space=pltpu.SMEM)
HBM = pl.BlockSpec(memory_space=pltpu.HBM)
LIMIT = 56 * 1024 * 1024


def call(kernel, in_specs, out_specs, out_shape, scratch, flops, moved, *args):
    return pl.pallas_call(
        kernel,
        in_specs=in_specs,
        out_specs=out_specs,
        out_shape=out_shape,
        scratch_shapes=scratch,
        compiler_params=pltpu.CompilerParams(vmem_limit_bytes=LIMIT),
        cost_estimate=pl.CostEstimate(flops=flops, bytes_accessed=moved, transcendentals=0),
    )(*args)


def silu(v):
    half = 0.5 * v
    return half + half * jnp.tanh(half)


def swap(x):
    axis = x.ndim - 1
    return pltpu.roll(x.astype(F32), x.shape[axis] // 2, axis).astype(x.dtype)


def lanes(shape):
    return lax.broadcasted_iota(jnp.int32, shape, len(shape) - 1) // (shape[-1] // 2)


def next_slot(tile_ref, count_ref, b):
    t = tile_ref[b]
    n = count_ref[t]
    count_ref[t] = n + 1
    return t, n


def clear(count_ref):
    for t in range(count_ref.shape[0]):
        count_ref[t] = 0


def embed_kernel(
    tile_hbm, patch_hbm, offset_hbm, cells_hbm, x_hbm, we_hbm, be_hbm, wp_hbm, bp_hbm,
    feat_ref, send0_ref, send1_ref,
    tile_ref, patch_ref, offset_ref, cells_ref, x_ref, we_ref, be_ref, wp_ref, bp_ref,
    count_ref, meta_ref, wide_ref, bias_ref, sems, x_sems,
):
    blocks, size, channels = feat_ref.shape
    chunks = x_sems.shape[0]
    per = blocks // chunks
    tiles = send0_ref.shape[0]
    meta_rows = meta_ref.shape[0] // tiles
    pairs = (
        (we_hbm, we_ref), (be_hbm, be_ref), (wp_hbm, wp_ref), (bp_hbm, bp_ref), (tile_hbm, tile_ref),
        (patch_hbm, patch_ref), (offset_hbm, offset_ref), (cells_hbm.at[0:8], cells_ref),
    )
    copies = [pltpu.make_async_copy(a, b, sems.at[i]) for i, (a, b) in enumerate(pairs)]

    def fetch(c):
        rows = pl.ds(pl.multiple_of(c * per * size, per * size), per * size)
        return pltpu.make_async_copy(x_hbm.at[rows], x_ref.at[rows], x_sems.at[c])

    for copy in copies:
        copy.start()
    for c in range(chunks):
        fetch(c).start()
    clear(count_ref)
    send0_ref[...] = jnp.zeros(send0_ref.shape, BF16)
    send1_ref[...] = jnp.zeros(send1_ref.shape, BF16)
    row = lax.broadcasted_iota(jnp.int32, meta_ref.shape, 0) % META
    meta_ref[...] = jnp.where(row == 2, -65536.0, 0.0)
    for copy in copies:
        copy.wait()
    wide_ref[:, :channels] = wp_ref[...]
    wide_ref[:, channels:] = swap(wp_ref[...])
    bias_ref[:, :channels] = bp_ref[...]
    bias_ref[:, channels:] = swap(bp_ref[...])
    group = lanes((size, channels))

    def chunk(c, unused):
        fetch(c).wait()
        rows = pl.ds(pl.multiple_of(c * per * size, per * size), per * size)
        hidden = silu(jnp.dot(x_ref[rows, :], we_ref[...], preferred_element_type=F32) + be_ref[...])
        both = jnp.dot(hidden.astype(BF16), wide_ref[...], preferred_element_type=F32) + bias_ref[...]
        feat_ref[pl.ds(c * per, per)] = both[:, :channels].astype(BF16).reshape(per, size, channels)
        for k in range(per):
            b = c * per + k
            t, n = next_slot(tile_ref, count_ref, b)
            odd = lax.rem(n, 2)
            at = pl.ds(pl.multiple_of(n // 2 * size, size), size)
            straight = both[k * size : (k + 1) * size, :channels]
            turned = both[k * size : (k + 1) * size, channels:]
            keep = group == odd
            low = jnp.where(keep, jnp.where(odd == 0, straight, turned), 0.0).astype(BF16)
            high = jnp.where(keep, jnp.where(odd == 0, turned, straight), 0.0).astype(BF16)
            send0_ref[t, at, :] += low
            send1_ref[t, at, :] += high
            first = t * meta_rows + n * META
            obs = pl.ds(pl.multiple_of(b * size, size), size)
            meta_ref[pl.ds(first, 2), :] = offset_ref[:, obs].astype(F32)
            meta_ref[pl.ds(first + 2, 1), :] = cells_ref[0:1, obs].astype(F32)
            meta_ref[pl.ds(first + 3, 1), :] = jnp.full((1, size), patch_ref[b], jnp.int32).astype(F32)
        return unused

    lax.fori_loop(0, chunks, chunk, 0)
    base = send1_ref.shape[1]
    extra = send0_ref.shape[1] - base - meta_rows
    for t in range(tiles):
        rows = meta_ref[t * meta_rows : (t + 1) * meta_rows, :]
        if extra:
            rows = jnp.concatenate([rows, jnp.zeros((extra, size), F32)], axis=0)
        send0_ref[t, base:, :] = rows.astype(BF16)


def factors(meta, normal):
    off_row, off_col, corner = meta[0:1, :], meta[1:2, :], meta[2:3, :]
    first_row = jnp.floor(corner * (1.0 / PW))
    first_col = corner - first_row * PW

    def factor(count, start, off):
        at = lax.broadcasted_iota(jnp.int32, (count, meta.shape[1]), 0).astype(F32) - start
        delta = at - 1.5 - off
        value = jnp.exp(delta * delta * -0.5)
        return jnp.where((at >= 0.0) & (at < SIDE), value, 0.0)

    def total(off):
        at = lax.broadcasted_iota(jnp.int32, (SIDE, meta.shape[1]), 0).astype(F32)
        delta = at - 1.5 - off
        return jnp.sum(jnp.exp(delta * delta * -0.5), axis=0, keepdims=True)

    rows, cols = factor(PH, first_row, off_row), factor(PW, first_col, off_col)
    if normal:
        rows = rows / (total(off_row) * total(off_col))
    return rows, cols


def outer(rows, cols):
    return (rows[:, None, :] * cols[None, :, :]).reshape(PH * PW, rows.shape[1])


def place(patch):
    row, col = patch // ACROSS, lax.rem(patch, ACROSS)
    halves = ACROSS // 2
    return (
        pl.ds(pl.multiple_of(row * PH, PH), PH),
        pl.ds(pl.multiple_of(lax.rem(col, halves) * PW, PW), PW),
        col // halves,
    )


def add_slot(acc_ref, matrix, packed, turned, odd, patch):
    at_row, at_col, half = place(patch)
    keep = lanes((1, packed.shape[1])) == half
    values = jnp.where(half == odd, packed, turned) * jnp.where(keep, 1.0, 0.0).astype(BF16)
    result = jnp.dot(matrix, values, preferred_element_type=F32)
    acc_ref[at_row, at_col, :] += result.reshape(PH, PW, result.shape[1])


def stripe_at(k, way):
    orbits = lax.axis_size("orbits")
    return lax.rem(lax.axis_index("orbits") + way * (orbits - 1 - k) + orbits * orbits, orbits)


def write_stripes(acc_ref, outs, way):
    for k, out_ref in enumerate(outs):
        stripe = acc_ref[pl.ds(stripe_at(k, way) * SR, SR)].astype(BF16)
        out_ref[0 : SR * TC // 2, :] = stripe.reshape(SR * TC // 2, stripe.shape[2])


def spread0_kernel(orbits, most, got_ref, *refs):
    outs, (matrix_ref, patch_ref, acc_ref, dens_ref) = refs[:orbits], refs[orbits:]
    size = got_ref.shape[2]
    acc_ref[...] = jnp.zeros(acc_ref.shape, F32)
    dens_ref[...] = jnp.zeros(dens_ref.shape, F32)
    base = most // 2 * size

    def tile(t, unused):
        metas = got_ref[t, base:, :].astype(F32)
        patches = [jnp.max(metas[n * META + 3 : n * META + 4, :]).astype(jnp.int32) for n in range(most)]
        for pair in range(most // 2):
            packed = got_ref[t, pair * size : (pair + 1) * size, :]
            turned = swap(packed)
            for odd in range(2):
                n = pair * 2 + odd
                patch = patches[n]
                patch_ref[t * most + n] = patch
                rows, cols = factors(metas[n * META : (n + 1) * META], False)
                matrix = outer(rows, cols).astype(BF16)
                matrix_ref[t * most + n] = matrix
                add_slot(acc_ref, matrix, packed, turned, odd, patch)
                dens_ref[patch] += lax.dot_general(
                    rows.astype(BF16), cols.astype(BF16), (((1,), (1,)), ((), ())), preferred_element_type=F32
                )
        return unused

    lax.fori_loop(0, got_ref.shape[0], tile, 0)
    write_stripes(acc_ref, outs, 1)
    for k, out_ref in enumerate(outs):
        bands = []
        for band in range(SR // PH):
            first = (stripe_at(k, 1) * (SR // PH) + band) * ACROSS
            bands.append(jnp.concatenate([dens_ref[first + c] for c in range(ACROSS)], axis=1))
        out_ref[SR * TC // 2 :, :] = jnp.concatenate(bands, axis=0).astype(BF16)


def spread1_kernel(orbits, most, patch_ref, matrix_ref, got_ref, *refs):
    outs, (acc_ref,) = refs[:orbits], refs[orbits:]
    size = got_ref.shape[2]
    acc_ref[...] = jnp.zeros(acc_ref.shape, F32)

    def tile(t, unused):
        for pair in range(most // 2):
            packed = got_ref[t, pair * size : (pair + 1) * size, :]
            turned = swap(packed)
            for odd in range(2):
                slot = t * most + pair * 2 + odd
                add_slot(acc_ref, matrix_ref[slot], packed, turned, odd, patch_ref[slot])
        return unused

    lax.fori_loop(0, got_ref.shape[0], tile, 0)
    write_stripes(acc_ref, outs, -1)


def weights_kernel(most, got_ref, out_ref):
    base = most // 2 * got_ref.shape[2]

    def tile(t, unused):
        metas = got_ref[t, base:, :].astype(F32)
        for n in range(most):
            rows, cols = factors(metas[n * META : (n + 1) * META], True)
            out_ref[t * most + n] = outer(rows, cols).T.astype(BF16)
        return unused

    lax.fori_loop(0, got_ref.shape[0], tile, 0)


def grid_kernel(own0_ref, sum0_ref, own1_ref, sum1_ref, weight_ref, out_ref):
    half = TC // 2
    channels = out_ref.shape[2]
    tail = slice(SR * half, SR * half + SR)
    density = (own0_ref[tail, :].astype(F32) + sum0_ref[tail, :].astype(F32)).T
    low = lanes((half, channels)) == 0
    for i in range(SR):
        at = slice(i * half, (i + 1) * half)
        a = own0_ref[at, :].astype(F32) + sum0_ref[at, :].astype(F32)
        b = own1_ref[at, :].astype(F32) + sum1_ref[at, :].astype(F32)
        spread = jnp.concatenate([jnp.where(low, a, swap(b)), jnp.where(low, swap(a), b)], axis=0)
        d = jnp.broadcast_to(density[:, i : i + 1], (TC, channels))
        out_ref[i] = (spread / jnp.maximum(d, 1.0) + weight_ref[...] * (d / (1.0 + d))).astype(BF16)


def conv_kernel(
    x_ref, up_ref, down_ref, left_ref, right_ref, w1_ref, b1_ref, w2_ref, b2_ref,
    out_ref, out0_ref, out1_ref, wide_ref, x16_ref, first_ref, wc1_ref, wc2_ref,
):
    channels = out_ref.shape[2]
    width = x16_ref.shape[1]
    half = TC // 2
    for a in range(3):
        for b in range(3):
            at = (slice(a * channels, (a + 1) * channels), slice(b * channels, (b + 1) * channels))
            wc1_ref[at] = w1_ref[a, b]
            wc2_ref[at] = w2_ref[a, b]
    body = slice(PAD, PAD + TC)
    wide_ref[...] = jnp.zeros(wide_ref.shape, F32)
    wide_ref[0:2, body] = up_ref[...].astype(F32)
    wide_ref[2 : 2 + SR, body] = x_ref[...].astype(F32)
    wide_ref[2 + SR :, body] = down_ref[...].astype(F32)
    wide_ref[:, PAD - 2 : PAD] = left_ref[...].astype(F32)
    wide_ref[:, PAD + TC : PAD + TC + 2] = right_ref[...].astype(F32)
    x16_ref[...] = wide_ref[...].astype(BF16)

    def taps(source, first, count, weights):
        rows = [source[pl.ds(first + a, count)].reshape(count * width, channels) for a in range(3)]
        all_taps = jnp.dot(jnp.concatenate(rows, axis=1), weights[...], preferred_element_type=F32)
        return (
            pltpu.roll(all_taps[:, :channels], 1, 0)
            + all_taps[:, channels : 2 * channels]
            + pltpu.roll(all_taps[:, 2 * channels :], count * width - 1, 0)
        )

    at_row, at_col = lax.axis_index(("orbits", "rows")), lax.axis_index("cols")
    col = lax.broadcasted_iota(jnp.int32, (width, channels), 0)
    first_col = jnp.where(at_col > 0, PAD - 1, PAD)
    last_col = jnp.where(at_col < lax.axis_size("cols") - 1, PAD + TC, PAD + TC - 1)
    inside = (col >= first_col) & (col <= last_col)
    first_row = jnp.where(at_row > 0, 0, 1)
    last_row = jnp.where(at_row < lax.axis_size(("orbits", "rows")) - 1, SR + 1, SR)
    count = (SR + 2) // 3

    def first_rows(i, unused):
        value = silu(taps(x16_ref, i * count, count, wc1_ref) + b1_ref[...])
        for r in range(count):
            row = i * count + r
            keep = inside & (row >= first_row) & (row <= last_row)
            first_ref[row] = jnp.where(keep, value[r * width : (r + 1) * width], 0.0).astype(BF16)
        return unused

    lax.fori_loop(0, 3, first_rows, 0)
    group = lanes((half, channels)) == 0
    again = SR // 2

    def second_rows(i, unused):
        values = taps(first_ref, i * again, again, wc2_ref) + b2_ref[...]
        for r in range(again):
            row = i * again + r
            value = values[r * width + PAD : r * width + PAD + TC] + x_ref[row].astype(F32)
            left, right = value[:half], value[half:]
            out_ref[row] = value.astype(BF16)
            out0_ref[row] = jnp.where(group, left, swap(right)).astype(BF16)
            out1_ref[row] = jnp.where(group, swap(left), right).astype(BF16)
        return unused

    lax.fori_loop(0, 2, second_rows, 0)


def read_kernel(orbits, most, way, patch_ref, weights_ref, *refs):
    pieces, (out_ref, grid_ref) = refs[:orbits], refs[orbits:]
    size = out_ref.shape[2]
    for k, piece_ref in enumerate(pieces):
        at = pl.ds(stripe_at(orbits - 1 - k, -way) * SR, SR)
        grid_ref[0, at] = piece_ref[...]
        grid_ref[1, at] = swap(piece_ref[...])
    low = lanes((size, out_ref.shape[2])) == 0

    def tile(t, unused):
        for pair in range(most // 2):
            sums = []
            for odd in range(2):
                slot = t * most + pair * 2 + odd
                at_row, at_col, half = place(patch_ref[slot])
                turn = jnp.where(half == odd, 0, 1)
                values = grid_ref[turn, at_row, at_col, :].reshape(PH * PW, grid_ref.shape[3])
                sums.append(jnp.dot(weights_ref[slot], values, preferred_element_type=F32))
            out_ref[t, pair * size : (pair + 1) * size, :] = jnp.where(low, sums[0], sums[1]).astype(BF16)
        return unused

    lax.fori_loop(0, out_ref.shape[0], tile, 0)


def final_kernel(tile_ref, feat_ref, got0_ref, got1_ref, out_ref, count_ref):
    blocks, size, channels = feat_ref.shape
    clear(count_ref)
    low = lanes((size, channels)) == 0
    per = 4

    def chunk(c, unused):
        for k in range(per):
            b = c * per + k
            t, n = next_slot(tile_ref, count_ref, b)
            odd = lax.rem(n, 2)
            at = pl.ds(pl.multiple_of(n // 2 * size, size), size)
            a, b2 = got0_ref[t, at, :].astype(F32), got1_ref[t, at, :].astype(F32)
            turned = swap(jnp.where(odd == 0, b2, a))
            mine = jnp.where(odd == 0, jnp.where(low, a, turned), jnp.where(low, turned, b2))
            out_ref[b] = (feat_ref[b].astype(F32) + mine).astype(BF16)
        return unused

    lax.fori_loop(0, blocks // per, chunk, 0)


def shifts(axis):
    size = lax.axis_size(axis)
    up = [(i, i + 1) for i in range(size - 1)]
    return up, [(j, i) for i, j in up]


def halo(x, axis, dim, width):
    up, down = shifts(axis)
    length = x.shape[dim]
    before = lax.ppermute(lax.slice_in_dim(x, length - width, length, axis=dim), axis, up)
    after = lax.ppermute(lax.slice_in_dim(x, 0, width, axis=dim), axis, down)
    return before, after


def turn(x, way):
    size = lax.axis_size("orbits")
    return lax.ppermute(x, "orbits", [(i, (i + way) % size) for i in range(size)])


together = lax.optimization_barrier


def local(
    obs_feat, obs_offset, obs_cells, block_tile, block_patch, w_embed, b_embed, w_proj, b_proj,
    density_weight, w_first, b_first, w_second, b_second,
):
    channels = obs_feat.shape[1]
    blocks = block_tile.shape[0]
    size = obs_feat.shape[0] // blocks
    plane = ("rows", "cols")
    tiles = lax.axis_size(plane)
    orbits = lax.axis_size("orbits")
    most = max(2, 2 * blocks // tiles)
    slots = tiles * most
    height = orbits * SR
    patches = height // PH * ACROSS
    half = TC // 2
    pairs = most // 2 * size
    meta_rows = max(16, most * META)
    chunks = blocks // 4
    counts = pltpu.SMEM((tiles,), jnp.int32)
    shape = jax.ShapeDtypeStruct
    bias = lambda b: b.reshape(1, channels)
    exchange = lambda x: lax.all_to_all(x, plane, split_axis=0, concat_axis=0, tiled=True)
    vmem = lambda a: pltpu.VMEM(a.shape, a.dtype)

    b_embed, b_proj = bias(b_embed), bias(b_proj)
    features, send0, send1 = call(
        embed_kernel,
        [HBM] * 9,
        [VMEM] * 3,
        (
            shape((blocks, size, channels), BF16),
            shape((tiles, pairs + meta_rows, channels), BF16),
            shape((tiles, pairs, channels), BF16),
        ),
        [
            pltpu.SMEM((blocks,), jnp.int32),
            pltpu.SMEM((blocks,), jnp.int32),
            vmem(obs_offset),
            pltpu.VMEM((8, obs_cells.shape[1]), jnp.int32),
            vmem(obs_feat),
            vmem(w_embed),
            vmem(b_embed),
            vmem(w_proj),
            vmem(b_proj),
            counts,
            pltpu.VMEM((slots * META, size), F32),
            pltpu.VMEM((channels, 2 * channels), BF16),
            pltpu.VMEM((1, 2 * channels), F32),
            pltpu.SemaphoreType.DMA((8,)),
            pltpu.SemaphoreType.DMA((chunks,)),
        ],
        6 * obs_feat.size * channels,
        8 * obs_feat.size,
        block_tile, block_patch, obs_offset, obs_cells, obs_feat, w_embed, b_embed, w_proj, b_proj,
    )
    got0 = exchange(send0)
    got1 = exchange(send1)

    flops = 2 * slots * size * channels * PH * PW
    stripe_shape = shape((SR * half, channels), BF16)
    dense_shape = shape((SR * half + SR, channels), BF16)
    acc = pltpu.VMEM((height, half, channels), F32)
    *out0, matrices, patch_of = call(
        functools.partial(spread0_kernel, orbits, most),
        [VMEM],
        [VMEM] * (orbits + 1) + [SMEM],
        [dense_shape] * orbits + [shape((slots, PH * PW, size), BF16), shape((slots,), jnp.int32)],
        [acc, pltpu.VMEM((patches, PH, PW), F32)],
        flops,
        12 * slots * size * channels,
        got0,
    )
    sum0 = out0[0]
    for k in range(1, orbits):
        sum0 = turn(sum0, 1)
        if k < orbits - 1:
            sum0 = sum0 + out0[k]
        if k == 1:
            sum0, got1 = together((sum0, got1))
    out1 = call(
        functools.partial(spread1_kernel, orbits, most),
        [SMEM, VMEM, VMEM],
        [VMEM] * orbits,
        [stripe_shape] * orbits,
        [acc],
        flops,
        8 * slots * size * channels,
        patch_of, matrices, got1,
    )
    sum1 = out1[0]
    for k in range(1, orbits):
        sum1 = turn(sum1, -1)
        if k < orbits - 1:
            sum1 = sum1 + out1[k]
    weights = call(
        functools.partial(weights_kernel, most),
        [VMEM],
        VMEM,
        shape((slots, size, PH * PW), BF16),
        [],
        flops,
        4 * slots * size * channels,
        got0,
    )
    grid_in = call(
        grid_kernel,
        [VMEM] * 5,
        VMEM,
        shape((SR, TC, channels), BF16),
        [],
        10000000,
        8 * SR * TC * channels,
        out0[-1], sum0, out1[-1], sum1, bias(density_weight),
    )

    above, below = halo(grid_in, ("orbits", "rows"), 0, 2)
    extended = jnp.concatenate(
        [
            jnp.concatenate([above[:, c], grid_in[:, c], below[:, c]], axis=0)
            for c in (slice(0, 2), slice(TC - 2, TC))
        ],
        axis=1,
    )
    left, right = halo(extended, "cols", 1, 2)
    width = TC + 2 * PAD
    grid_out, half0, half1 = call(
        conv_kernel,
        [VMEM] * 9,
        [VMEM] * 3,
        [shape((SR, TC, channels), BF16)] + [shape((SR, half, channels), BF16)] * 2,
        [
            pltpu.VMEM((SR + 4, width, channels), F32),
            pltpu.VMEM((SR + 4, width, channels), BF16),
            pltpu.VMEM((SR + 2, width, channels), BF16),
            pltpu.VMEM((3 * channels, 3 * channels), BF16),
            pltpu.VMEM((3 * channels, 3 * channels), BF16),
        ],
        4 * 9 * SR * TC * channels * channels,
        8 * grid_in.size,
        grid_in, above, below, left, right, w_first, bias(b_first), w_second, bias(b_second),
    )

    def readings(pieces, way):
        return call(
            functools.partial(read_kernel, orbits, most, way),
            [SMEM, VMEM] + [VMEM] * orbits,
            VMEM,
            shape((tiles, pairs, channels), BF16),
            [pltpu.VMEM((2, height, half, channels), BF16)],
            flops,
            8 * slots * size * channels,
            patch_of, weights, *pieces,
        )

    pieces0, pieces1 = [half0, turn(half0, 1)], [half1]
    for k in range(2, orbits):
        both = together((turn(pieces0[-1], 1), turn(pieces1[-1], -1)))
        pieces0.append(both[0])
        pieces1.append(both[1])
    while len(pieces1) < orbits:
        pieces1.append(turn(pieces1[-1], -1))
    back0 = exchange(readings(pieces0, 1))
    back1 = exchange(readings(pieces1, -1))
    obs_out = call(
        final_kernel,
        [SMEM] + [VMEM] * 3,
        VMEM,
        shape((blocks, size, channels), BF16),
        [counts],
        1000000,
        8 * obs_feat.size,
        block_tile, features, back0, back1,
    )
    return obs_out.reshape(obs_feat.shape), grid_out


def solution(mesh):
    spread_out = ("orbits", "rows", "cols")
    in_specs = (
        P(spread_out, None),
        P(None, spread_out),
        P(None, spread_out),
        P(spread_out),
        P(spread_out),
    ) + (P(),) * 9
    out_specs = (P(spread_out, None), P(("orbits", "rows"), "cols", None))
    return jax.shard_map(local, mesh=mesh, in_specs=in_specs, out_specs=out_specs, check_vma=False)
```

```python
import functools

import jax
import jax.numpy as jnp
from jax import lax
from jax.experimental import pallas as pl
from jax.experimental.pallas import tpu as pltpu
from jax.sharding import PartitionSpec as P

KN = 16
PH = 8
PW = 32
SR = 16
TC = 128
SIDE = 4
PAD = 8
META = 4
ACROSS = TC // PW
F32 = jnp.float32
BF16 = jnp.bfloat16

VMEM = pl.BlockSpec(memory_space=pltpu.VMEM)
SMEM = pl.BlockSpec(memory_space=pltpu.SMEM)
HBM = pl.BlockSpec(memory_space=pltpu.HBM)
LIMIT = 20 * 1024 * 1024
LARGE = 56 * 1024 * 1024


def call(kernel, in_specs, out_specs, out_shape, scratch, flops, moved, *args, limit=LIMIT):
    return pl.pallas_call(
        kernel,
        in_specs=in_specs,
        out_specs=out_specs,
        out_shape=out_shape,
        scratch_shapes=scratch,
        compiler_params=pltpu.CompilerParams(vmem_limit_bytes=limit),
        cost_estimate=pl.CostEstimate(flops=flops, bytes_accessed=moved, transcendentals=0),
    )(*args)


def silu(v):
    half = 0.5 * v
    return half + half * jnp.tanh(half)


def next_slot(tile_ref, count_ref, b):
    t = tile_ref[b]
    n = count_ref[t]
    count_ref[t] = n + 1
    return t, n


def clear(count_ref):
    for t in range(count_ref.shape[0]):
        count_ref[t] = 0


def embed_kernel(
    tile_hbm, patch_hbm, offset_hbm, cells_hbm, x_hbm, we_hbm, be_hbm, wp_hbm, bp_hbm,
    feat_ref, send_ref,
    tile_ref, patch_ref, offset_ref, cells_ref, x_ref, we_ref, be_ref, wp_ref, bp_ref,
    count_ref, meta_ref, sems, x_sems,
):
    blocks, size, channels = feat_ref.shape
    chunks = x_sems.shape[0]
    per = blocks // chunks
    tiles = send_ref.shape[0]
    meta_rows = meta_ref.shape[0] // tiles
    base = meta_rows // META * size
    pairs = (
        (we_hbm, we_ref), (be_hbm, be_ref), (wp_hbm, wp_ref), (bp_hbm, bp_ref), (tile_hbm, tile_ref),
        (patch_hbm, patch_ref), (offset_hbm, offset_ref), (cells_hbm.at[0:8], cells_ref),
    )
    copies = [pltpu.make_async_copy(a, b, sems.at[i]) for i, (a, b) in enumerate(pairs)]

    def fetch(c):
        rows = pl.ds(pl.multiple_of(c * per * size, per * size), per * size)
        return pltpu.make_async_copy(x_hbm.at[rows], x_ref.at[rows], x_sems.at[c])

    for copy in copies:
        copy.start()
    for c in range(chunks):
        fetch(c).start()
    clear(count_ref)
    send_ref[...] = jnp.zeros(send_ref.shape, BF16)
    row = lax.broadcasted_iota(jnp.int32, meta_ref.shape, 0) % META
    meta_ref[...] = jnp.where(row == 2, -65536.0, 0.0)
    for copy in copies:
        copy.wait()

    def chunk(c, unused):
        fetch(c).wait()
        rows = pl.ds(pl.multiple_of(c * per * size, per * size), per * size)
        hidden = silu(jnp.dot(x_ref[rows, :], we_ref[...], preferred_element_type=F32) + be_ref[...])
        out = jnp.dot(hidden.astype(BF16), wp_ref[...], preferred_element_type=F32) + bp_ref[...]
        out = out.astype(BF16)
        feat_ref[pl.ds(c * per, per)] = out.reshape(per, size, channels)
        for k in range(per):
            b = c * per + k
            t, n = next_slot(tile_ref, count_ref, b)
            send_ref[t, pl.ds(pl.multiple_of(n * size, size), size), :] = out[k * size : (k + 1) * size]
            first = t * meta_rows + n * META
            obs = pl.ds(pl.multiple_of(b * size, size), size)
            meta_ref[pl.ds(first, 2), :] = offset_ref[:, obs].astype(F32)
            meta_ref[pl.ds(first + 2, 1), :] = cells_ref[0:1, obs].astype(F32)
            meta_ref[pl.ds(first + 3, 1), :] = jnp.full((1, size), patch_ref[b], jnp.int32).astype(F32)
        return unused

    lax.fori_loop(0, chunks, chunk, 0)
    extra = send_ref.shape[1] - base - meta_rows
    for t in range(tiles):
        rows = meta_ref[t * meta_rows : (t + 1) * meta_rows, :]
        if extra:
            rows = jnp.concatenate([rows, jnp.zeros((extra, size), F32)], axis=0)
        send_ref[t, base:, :] = rows.astype(BF16)


def factors(meta, normal):
    off_row, off_col, corner = meta[0:1, :], meta[1:2, :], meta[2:3, :]
    first_row = jnp.floor(corner * (1.0 / PW))
    first_col = corner - first_row * PW

    def factor(count, start, off):
        at = lax.broadcasted_iota(jnp.int32, (count, meta.shape[1]), 0).astype(F32) - start
        delta = at - 1.5 - off
        value = jnp.exp(delta * delta * -0.5)
        return jnp.where((at >= 0.0) & (at < SIDE), value, 0.0)

    def total(off):
        at = lax.broadcasted_iota(jnp.int32, (SIDE, meta.shape[1]), 0).astype(F32)
        delta = at - 1.5 - off
        return jnp.sum(jnp.exp(delta * delta * -0.5), axis=0, keepdims=True)

    rows, cols = factor(PH, first_row, off_row), factor(PW, first_col, off_col)
    if normal:
        rows = rows / (total(off_row) * total(off_col))
    return rows, cols


def outer(rows, cols):
    return (rows[:, None, :] * cols[None, :, :]).reshape(PH * PW, rows.shape[1])


def place(patch):
    row, col = patch // ACROSS, lax.rem(patch, ACROSS)
    return pl.ds(pl.multiple_of(row * PH, PH), PH), pl.ds(pl.multiple_of(col * PW, PW), PW)


def stripe_at(k, way):
    orbits = lax.axis_size("orbits")
    return lax.rem(lax.axis_index("orbits") + way * (orbits - 1 - k) + orbits * orbits, orbits)


def spread_kernel(orbits, most, got_ref, *refs):
    up, down, (patch_ref, acc_ref, dens_ref) = refs[:orbits], refs[orbits : 2 * orbits], refs[2 * orbits :]
    size, channels = got_ref.shape[2], acc_ref.shape[2]
    acc_ref[...] = jnp.zeros(acc_ref.shape, F32)
    dens_ref[...] = jnp.zeros(dens_ref.shape, F32)
    base = most * size

    def tile(t, unused):
        metas = got_ref[t, base:, :].astype(F32)
        patches = [jnp.max(metas[n * META + 3 : n * META + 4, :]).astype(jnp.int32) for n in range(most)]
        for n in range(most):
            patch = patches[n]
            patch_ref[t * most + n] = patch
            rows, cols = factors(metas[n * META : (n + 1) * META], False)
            values = got_ref[t, n * size : (n + 1) * size, :]
            result = jnp.dot(outer(rows, cols).astype(BF16), values, preferred_element_type=F32)
            at_row, at_col = place(patch)
            acc_ref[at_row, at_col, :] += result.reshape(PH, PW, channels)
            dens_ref[patch] += lax.dot_general(
                rows.astype(BF16), cols.astype(BF16), (((1,), (1,)), ((), ())), preferred_element_type=F32
            )
        return unused

    lax.fori_loop(0, got_ref.shape[0], tile, 0)
    for k in range(orbits):
        for out_ref, way, band in ((up[k], 1, 0), (down[k], -1, 1)):
            rows = acc_ref[pl.ds(stripe_at(k, way) * SR + band * PH, PH)].astype(BF16)
            out_ref[0 : PH * TC, :] = rows.reshape(PH * TC, channels)
        bands = []
        for band in range(SR // PH):
            first = (stripe_at(k, 1) * (SR // PH) + band) * ACROSS
            bands.append(jnp.concatenate([dens_ref[first + c] for c in range(ACROSS)], axis=1))
        up[k][PH * TC :, :] = jnp.concatenate(bands, axis=0).astype(BF16)


def weights_kernel(most, got_ref, out_ref):
    base = most * got_ref.shape[2]

    def tile(t, unused):
        metas = got_ref[t, base:, :].astype(F32)
        for n in range(most):
            rows, cols = factors(metas[n * META : (n + 1) * META], True)
            out_ref[t * most + n] = outer(rows, cols).T.astype(BF16)
        return unused

    lax.fori_loop(0, got_ref.shape[0], tile, 0)


def grid_kernel(own0_ref, sum0_ref, own1_ref, sum1_ref, weight_ref, out_ref):
    channels = out_ref.shape[2]
    tail = slice(PH * TC, PH * TC + SR)
    density = (own0_ref[tail, :].astype(F32) + sum0_ref[tail, :].astype(F32)).T
    for i in range(SR):
        own_ref, sum_ref = (own0_ref, sum0_ref) if i < PH else (own1_ref, sum1_ref)
        at = slice(i % PH * TC, (i % PH + 1) * TC)
        spread = own_ref[at, :].astype(F32) + sum_ref[at, :].astype(F32)
        d = jnp.broadcast_to(density[:, i : i + 1], (TC, channels))
        out_ref[i] = (spread / jnp.maximum(d, 1.0) + weight_ref[...] * (d / (1.0 + d))).astype(BF16)


def conv_kernel(
    x_ref, up_ref, down_ref, left_ref, right_ref, w1_ref, b1_ref, w2_ref, b2_ref,
    out_ref, out0_ref, out1_ref, wide_ref, x16_ref, first_ref, wc1_ref, wc2_ref,
):
    channels = out_ref.shape[2]
    width = x16_ref.shape[1]
    for a in range(3):
        for b in range(3):
            at = (slice(a * channels, (a + 1) * channels), slice(b * channels, (b + 1) * channels))
            wc1_ref[at] = w1_ref[a, b]
            wc2_ref[at] = w2_ref[a, b]
    body = slice(PAD, PAD + TC)
    wide_ref[...] = jnp.zeros(wide_ref.shape, F32)
    wide_ref[0:2, body] = up_ref[...].astype(F32)
    wide_ref[2 : 2 + SR, body] = x_ref[...].astype(F32)
    wide_ref[2 + SR :, body] = down_ref[...].astype(F32)
    wide_ref[:, PAD - 2 : PAD] = left_ref[...].astype(F32)
    wide_ref[:, PAD + TC : PAD + TC + 2] = right_ref[...].astype(F32)
    x16_ref[...] = wide_ref[...].astype(BF16)

    def taps(source, first, count, weights):
        rows = [source[pl.ds(first + a, count)].reshape(count * width, channels) for a in range(3)]
        all_taps = jnp.dot(jnp.concatenate(rows, axis=1), weights[...], preferred_element_type=F32)
        return (
            pltpu.roll(all_taps[:, :channels], 1, 0)
            + all_taps[:, channels : 2 * channels]
            + pltpu.roll(all_taps[:, 2 * channels :], count * width - 1, 0)
        )

    at_row, at_col = lax.axis_index(("orbits", "rows")), lax.axis_index("cols")
    col = lax.broadcasted_iota(jnp.int32, (width, channels), 0)
    first_col = jnp.where(at_col > 0, PAD - 1, PAD)
    last_col = jnp.where(at_col < lax.axis_size("cols") - 1, PAD + TC, PAD + TC - 1)
    inside = (col >= first_col) & (col <= last_col)
    first_row = jnp.where(at_row > 0, 0, 1)
    last_row = jnp.where(at_row < lax.axis_size(("orbits", "rows")) - 1, SR + 1, SR)
    count = (SR + 2) // 3

    def first_rows(i, unused):
        value = silu(taps(x16_ref, i * count, count, wc1_ref) + b1_ref[...])
        for r in range(count):
            row = i * count + r
            keep = inside & (row >= first_row) & (row <= last_row)
            first_ref[row] = jnp.where(keep, value[r * width : (r + 1) * width], 0.0).astype(BF16)
        return unused

    lax.fori_loop(0, 3, first_rows, 0)
    again = PH

    def second_rows(i, band_ref):
        values = taps(first_ref, i * again, again, wc2_ref) + b2_ref[...]
        for r in range(again):
            row = i * again + r
            value = values[r * width + PAD : r * width + PAD + TC] + x_ref[row].astype(F32)
            out_ref[row] = value.astype(BF16)
            band_ref[r] = value.astype(BF16)

    second_rows(0, out0_ref)
    second_rows(1, out1_ref)


def read_kernel(orbits, most, patch_ref, weights_ref, *refs):
    up, down, (out_ref, grid_ref) = refs[:orbits], refs[orbits : 2 * orbits], refs[2 * orbits :]
    size = out_ref.shape[2]
    for k in range(orbits):
        for piece_ref, way, band in ((up[k], 1, 0), (down[k], -1, 1)):
            grid_ref[pl.ds(stripe_at(orbits - 1 - k, -way) * SR + band * PH, PH)] = piece_ref[...]

    def tile(t, unused):
        for n in range(most):
            at_row, at_col = place(patch_ref[t * most + n])
            values = grid_ref[at_row, at_col, :].reshape(PH * PW, grid_ref.shape[2])
            result = jnp.dot(weights_ref[t * most + n], values, preferred_element_type=F32)
            out_ref[t, n * size : (n + 1) * size, :] = result.astype(BF16)
        return unused

    lax.fori_loop(0, out_ref.shape[0], tile, 0)


def final_kernel(tile_ref, feat_ref, got_ref, out_ref, count_ref):
    blocks, size, _ = feat_ref.shape
    clear(count_ref)
    per = 4

    def chunk(c, unused):
        for k in range(per):
            b = c * per + k
            t, n = next_slot(tile_ref, count_ref, b)
            mine = got_ref[t, pl.ds(pl.multiple_of(n * size, size), size), :]
            out_ref[b] = (feat_ref[b].astype(F32) + mine.astype(F32)).astype(BF16)
        return unused

    lax.fori_loop(0, blocks // per, chunk, 0)


def shifts(axis):
    size = lax.axis_size(axis)
    up = [(i, i + 1) for i in range(size - 1)]
    return up, [(j, i) for i, j in up]


def halo(x, axis, dim, width):
    up, down = shifts(axis)
    length = x.shape[dim]
    before = lax.ppermute(lax.slice_in_dim(x, length - width, length, axis=dim), axis, up)
    after = lax.ppermute(lax.slice_in_dim(x, 0, width, axis=dim), axis, down)
    return before, after


def turn(x, way):
    size = lax.axis_size("orbits")
    return lax.ppermute(x, "orbits", [(i, (i + way) % size) for i in range(size)])


def ring_sum(stripes, way):
    total = stripes[0]
    for k in range(1, len(stripes)):
        total = turn(total, way)
        if k < len(stripes) - 1:
            total = total + stripes[k]
    return total


def ring_gather(x, way):
    pieces = [x]
    for _ in range(lax.axis_size("orbits") - 1):
        pieces.append(turn(pieces[-1], way))
    return pieces


def local(
    obs_feat, obs_offset, obs_cells, block_tile, block_patch, w_embed, b_embed, w_proj, b_proj,
    density_weight, w_first, b_first, w_second, b_second,
):
    channels = obs_feat.shape[1]
    blocks = block_tile.shape[0]
    size = obs_feat.shape[0] // blocks
    plane = ("rows", "cols")
    tiles = lax.axis_size(plane)
    orbits = lax.axis_size("orbits")
    most = max(2, 2 * blocks // tiles)
    slots = tiles * most
    height = orbits * SR
    patches = height // PH * ACROSS
    length = most * size
    meta_rows = max(16, most * META)
    chunks = blocks // 4
    counts = pltpu.SMEM((tiles,), jnp.int32)
    shape = jax.ShapeDtypeStruct
    bias = lambda b: b.reshape(1, channels)
    exchange = lambda x: lax.all_to_all(x, plane, split_axis=0, concat_axis=0, tiled=True)
    vmem = lambda a: pltpu.VMEM(a.shape, a.dtype)

    b_embed, b_proj = bias(b_embed), bias(b_proj)
    features, send = call(
        embed_kernel,
        [HBM] * 9,
        [VMEM] * 2,
        (shape((blocks, size, channels), BF16), shape((tiles, length + meta_rows, channels), BF16)),
        [
            pltpu.SMEM((blocks,), jnp.int32),
            pltpu.SMEM((blocks,), jnp.int32),
            vmem(obs_offset),
            pltpu.VMEM((8, obs_cells.shape[1]), jnp.int32),
            vmem(obs_feat),
            vmem(w_embed),
            vmem(b_embed),
            vmem(w_proj),
            vmem(b_proj),
            counts,
            pltpu.VMEM((slots * META, size), F32),
            pltpu.SemaphoreType.DMA((8,)),
            pltpu.SemaphoreType.DMA((chunks,)),
        ],
        6 * obs_feat.size * channels,
        8 * obs_feat.size,
        block_tile, block_patch, obs_offset, obs_cells, obs_feat, w_embed, b_embed, w_proj, b_proj,
        limit=LARGE,
    )
    got = exchange(send)

    flops = 2 * slots * size * channels * PH * PW
    band_shape = shape((PH * TC, channels), BF16)
    dense_shape = shape((PH * TC + SR, channels), BF16)
    *bands, patch_of = call(
        functools.partial(spread_kernel, orbits, most),
        [VMEM],
        [VMEM] * (2 * orbits) + [SMEM],
        [dense_shape] * orbits + [band_shape] * orbits + [shape((slots,), jnp.int32)],
        [pltpu.VMEM((height, TC, channels), F32), pltpu.VMEM((patches, PH, PW), F32)],
        flops,
        8 * slots * size * channels,
        got,
    )
    bands0, bands1 = bands[:orbits], bands[orbits:]
    sum0, sum1 = ring_sum(bands0, 1), ring_sum(bands1, -1)
    weights = call(
        functools.partial(weights_kernel, most),
        [VMEM],
        VMEM,
        shape((slots, size, PH * PW), BF16),
        [],
        flops,
        4 * slots * size * channels,
        got,
    )
    grid_in = call(
        grid_kernel,
        [VMEM] * 5,
        VMEM,
        shape((SR, TC, channels), BF16),
        [],
        10000000,
        8 * SR * TC * channels,
        bands0[-1], sum0, bands1[-1], sum1, bias(density_weight),
    )

    above, below = halo(grid_in, ("orbits", "rows"), 0, 2)
    extended = jnp.concatenate(
        [
            jnp.concatenate([above[:, c], grid_in[:, c], below[:, c]], axis=0)
            for c in (slice(0, 2), slice(TC - 2, TC))
        ],
        axis=1,
    )
    left, right = halo(extended, "cols", 1, 2)
    width = TC + 2 * PAD
    grid_out, band0, band1 = call(
        conv_kernel,
        [VMEM] * 9,
        [VMEM] * 3,
        [shape((SR, TC, channels), BF16)] + [shape((PH, TC, channels), BF16)] * 2,
        [
            pltpu.VMEM((SR + 4, width, channels), F32),
            pltpu.VMEM((SR + 4, width, channels), BF16),
            pltpu.VMEM((SR + 2, width, channels), BF16),
            pltpu.VMEM((3 * channels, 3 * channels), BF16),
            pltpu.VMEM((3 * channels, 3 * channels), BF16),
        ],
        4 * 9 * SR * TC * channels * channels,
        8 * grid_in.size,
        grid_in, above, below, left, right, w_first, bias(b_first), w_second, bias(b_second),
    )

    readings = call(
        functools.partial(read_kernel, orbits, most),
        [SMEM, VMEM] + [VMEM] * (2 * orbits),
        VMEM,
        shape((tiles, length, channels), BF16),
        [pltpu.VMEM((height, TC, channels), BF16)],
        flops,
        8 * slots * size * channels,
        patch_of, weights, *ring_gather(band0, 1), *ring_gather(band1, -1),
    )
    back = exchange(readings)
    obs_out = call(
        final_kernel,
        [SMEM] + [VMEM] * 2,
        VMEM,
        shape((blocks, size, channels), BF16),
        [counts],
        1000000,
        8 * obs_feat.size,
        block_tile, features, back,
    )
    return obs_out.reshape(obs_feat.shape), grid_out


def solution(mesh):
    spread_out = ("orbits", "rows", "cols")
    in_specs = (
        P(spread_out, None),
        P(None, spread_out),
        P(None, spread_out),
        P(spread_out),
        P(spread_out),
    ) + (P(),) * 9
    out_specs = (P(spread_out, None), P(("orbits", "rows"), "cols", None))
    return jax.shard_map(local, mesh=mesh, in_specs=in_specs, out_specs=out_specs, check_vma=False)
```

```python
import functools

import jax
import jax.numpy as jnp
from jax import lax
from jax.experimental import pallas as pl
from jax.experimental.pallas import tpu as pltpu
from jax.sharding import PartitionSpec as P

KN = 16
PH = 8
PW = 32
SR = 16
TC = 128
SIDE = 4
PAD = 8
META = 4
EDGE = 2
EARLY = (0, 1, SR - 2, SR - 1)
LATE = tuple(r for r in range(SR) if r not in EARLY)
FULL = len(EARLY) * TC
CELLS = -(-len(LATE) * 2 * EDGE // 16) * 16
ACROSS = TC // PW
F32 = jnp.float32
BF16 = jnp.bfloat16

VMEM = pl.BlockSpec(memory_space=pltpu.VMEM)
SMEM = pl.BlockSpec(memory_space=pltpu.SMEM)
HBM = pl.BlockSpec(memory_space=pltpu.HBM)
LIMIT = 20 * 1024 * 1024
LARGE = 56 * 1024 * 1024


def call(kernel, in_specs, out_specs, out_shape, scratch, flops, moved, *args, limit=LIMIT):
    return pl.pallas_call(
        kernel,
        in_specs=in_specs,
        out_specs=out_specs,
        out_shape=out_shape,
        scratch_shapes=scratch,
        compiler_params=pltpu.CompilerParams(vmem_limit_bytes=limit),
        cost_estimate=pl.CostEstimate(flops=flops, bytes_accessed=moved, transcendentals=0),
    )(*args)


def silu(v):
    half = 0.5 * v
    return half + half * jnp.tanh(half)


def next_slot(tile_ref, count_ref, b):
    t = tile_ref[b]
    n = count_ref[t]
    count_ref[t] = n + 1
    return t, n


def clear(count_ref):
    for t in range(count_ref.shape[0]):
        count_ref[t] = 0


def embed_kernel(
    tile_hbm, patch_hbm, offset_hbm, cells_hbm, x_hbm, we_hbm, be_hbm, wp_hbm, bp_hbm,
    feat_ref, send_ref,
    tile_ref, patch_ref, offset_ref, cells_ref, x_ref, we_ref, be_ref, wp_ref, bp_ref,
    count_ref, meta_ref, sems, x_sems,
):
    blocks, size, channels = feat_ref.shape
    chunks = x_sems.shape[0]
    per = blocks // chunks
    tiles = send_ref.shape[0]
    meta_rows = meta_ref.shape[0] // tiles
    base = meta_rows // META * size
    pairs = (
        (we_hbm, we_ref), (be_hbm, be_ref), (wp_hbm, wp_ref), (bp_hbm, bp_ref), (tile_hbm, tile_ref),
        (patch_hbm, patch_ref), (offset_hbm, offset_ref), (cells_hbm.at[0:8], cells_ref),
    )
    copies = [pltpu.make_async_copy(a, b, sems.at[i]) for i, (a, b) in enumerate(pairs)]

    def fetch(c):
        rows = pl.ds(pl.multiple_of(c * per * size, per * size), per * size)
        return pltpu.make_async_copy(x_hbm.at[rows], x_ref.at[rows], x_sems.at[c])

    for copy in copies:
        copy.start()
    for c in range(chunks):
        fetch(c).start()
    clear(count_ref)
    send_ref[...] = jnp.zeros(send_ref.shape, BF16)
    row = lax.broadcasted_iota(jnp.int32, meta_ref.shape, 0) % META
    meta_ref[...] = jnp.where(row == 2, -65536.0, 0.0)
    for copy in copies:
        copy.wait()

    def chunk(c, unused):
        fetch(c).wait()
        rows = pl.ds(pl.multiple_of(c * per * size, per * size), per * size)
        hidden = silu(jnp.dot(x_ref[rows, :], we_ref[...], preferred_element_type=F32) + be_ref[...])
        out = jnp.dot(hidden.astype(BF16), wp_ref[...], preferred_element_type=F32) + bp_ref[...]
        out = out.astype(BF16)
        feat_ref[pl.ds(c * per, per)] = out.reshape(per, size, channels)
        for k in range(per):
            b = c * per + k
            t, n = next_slot(tile_ref, count_ref, b)
            send_ref[t, pl.ds(pl.multiple_of(n * size, size), size), :] = out[k * size : (k + 1) * size]
            first = t * meta_rows + n * META
            obs = pl.ds(pl.multiple_of(b * size, size), size)
            meta_ref[pl.ds(first, 2), :] = offset_ref[:, obs].astype(F32)
            meta_ref[pl.ds(first + 2, 1), :] = cells_ref[0:1, obs].astype(F32)
            meta_ref[pl.ds(first + 3, 1), :] = jnp.full((1, size), patch_ref[b], jnp.int32).astype(F32)
        return unused

    lax.fori_loop(0, chunks, chunk, 0)
    extra = send_ref.shape[1] - base - meta_rows
    for t in range(tiles):
        rows = meta_ref[t * meta_rows : (t + 1) * meta_rows, :]
        if extra:
            rows = jnp.concatenate([rows, jnp.zeros((extra, size), F32)], axis=0)
        send_ref[t, base:, :] = rows.astype(BF16)


def factors(meta, normal):
    off_row, off_col, corner = meta[0:1, :], meta[1:2, :], meta[2:3, :]
    first_row = jnp.floor(corner * (1.0 / PW))
    first_col = corner - first_row * PW

    def factor(count, start, off):
        at = lax.broadcasted_iota(jnp.int32, (count, meta.shape[1]), 0).astype(F32) - start
        delta = at - 1.5 - off
        value = jnp.exp(delta * delta * -0.5)
        return jnp.where((at >= 0.0) & (at < SIDE), value, 0.0)

    def total(off):
        at = lax.broadcasted_iota(jnp.int32, (SIDE, meta.shape[1]), 0).astype(F32)
        delta = at - 1.5 - off
        return jnp.sum(jnp.exp(delta * delta * -0.5), axis=0, keepdims=True)

    rows, cols = factor(PH, first_row, off_row), factor(PW, first_col, off_col)
    if normal:
        rows = rows / (total(off_row) * total(off_col))
    return rows, cols


def outer(rows, cols):
    return (rows[:, None, :] * cols[None, :, :]).reshape(PH * PW, rows.shape[1])


def place(patch):
    row, col = patch // ACROSS, lax.rem(patch, ACROSS)
    return pl.ds(pl.multiple_of(row * PH, PH), PH), pl.ds(pl.multiple_of(col * PW, PW), PW)


def stripe_at(k, way):
    orbits = lax.axis_size("orbits")
    return lax.rem(lax.axis_index("orbits") + way * (orbits - 1 - k) + orbits * orbits, orbits)


def spread_kernel(orbits, most, got_ref, *refs):
    up, down, (patch_ref, acc_ref, dens_ref) = refs[:orbits], refs[orbits : 2 * orbits], refs[2 * orbits :]
    size, channels = got_ref.shape[2], acc_ref.shape[2]
    acc_ref[...] = jnp.zeros(acc_ref.shape, F32)
    dens_ref[...] = jnp.zeros(dens_ref.shape, F32)
    base = most * size

    def tile(t, unused):
        metas = got_ref[t, base:, :].astype(F32)
        patches = [jnp.max(metas[n * META + 3 : n * META + 4, :]).astype(jnp.int32) for n in range(most)]
        for n in range(most):
            patch = patches[n]
            patch_ref[t * most + n] = patch
            rows, cols = factors(metas[n * META : (n + 1) * META], False)
            values = got_ref[t, n * size : (n + 1) * size, :]
            result = jnp.dot(outer(rows, cols).astype(BF16), values, preferred_element_type=F32)
            at_row, at_col = place(patch)
            acc_ref[at_row, at_col, :] += result.reshape(PH, PW, channels)
            dens_ref[patch] += lax.dot_general(
                rows.astype(BF16), cols.astype(BF16), (((1,), (1,)), ((), ())), preferred_element_type=F32
            )
        return unused

    lax.fori_loop(0, got_ref.shape[0], tile, 0)
    for k in range(orbits):
        for out_ref, way, rows in ((up[k], 1, EARLY), (down[k], -1, LATE)):
            first = stripe_at(k, way) * SR
            for i, r in enumerate(rows):
                out_ref[i * TC : (i + 1) * TC, :] = acc_ref[first + r].astype(BF16)
        first = stripe_at(k, 1) * SR
        bands = []
        for band in range(SR // PH):
            at = (stripe_at(k, 1) * (SR // PH) + band) * ACROSS
            bands.append(jnp.concatenate([dens_ref[at + c] for c in range(ACROSS)], axis=1))
        up[k][FULL : FULL + SR, :] = jnp.concatenate(bands, axis=0).astype(BF16)
        cells = [acc_ref[first + r, at] for r in LATE for at in (slice(0, EDGE), slice(TC - EDGE, TC))]
        spare = CELLS - len(LATE) * 2 * EDGE
        if spare:
            cells.append(jnp.zeros((spare, channels), F32))
        up[k][FULL + SR :, :] = jnp.concatenate(cells, axis=0).astype(BF16)


def weights_kernel(most, got_ref, out_ref):
    base = most * got_ref.shape[2]

    def tile(t, unused):
        metas = got_ref[t, base:, :].astype(F32)
        for n in range(most):
            rows, cols = factors(metas[n * META : (n + 1) * META], True)
            out_ref[t * most + n] = outer(rows, cols).T.astype(BF16)
        return unused

    lax.fori_loop(0, got_ref.shape[0], tile, 0)


def grid_values(spread, density, weight):
    return (spread / jnp.maximum(density, 1.0) + weight * (density / (1.0 + density))).astype(BF16)


def densities(own_ref, sum_ref):
    tail = slice(FULL, FULL + SR)
    columns = (own_ref[tail, :].astype(F32) + sum_ref[tail, :].astype(F32)).T
    return lambda r: jnp.broadcast_to(columns[:, r : r + 1], (TC, own_ref.shape[1]))


def edge_kernel(own_ref, sum_ref, weight_ref, top_ref, bottom_ref, left_ref, right_ref):
    density = densities(own_ref, sum_ref)
    weight = weight_ref[...]
    low, high = slice(0, EDGE), slice(TC - EDGE, TC)
    cells = own_ref[FULL + SR :, :].astype(F32) + sum_ref[FULL + SR :, :].astype(F32)
    for r in range(SR):
        d = density(r)
        if r in EARLY:
            at = slice(EARLY.index(r) * TC, (EARLY.index(r) + 1) * TC)
            spread = own_ref[at, :].astype(F32) + sum_ref[at, :].astype(F32)
            row = grid_values(spread, d, weight)
            if r < EDGE:
                top_ref[r] = row
            if r >= SR - EDGE:
                bottom_ref[r - (SR - EDGE)] = row
            left_ref[r], right_ref[r] = row[low], row[high]
        else:
            at = LATE.index(r) * 2 * EDGE
            left_ref[r] = grid_values(cells[at : at + EDGE], d[low], weight)
            right_ref[r] = grid_values(cells[at + EDGE : at + 2 * EDGE], d[high], weight)


def grid_kernel(own0_ref, sum0_ref, own1_ref, sum1_ref, weight_ref, out_ref):
    density = densities(own0_ref, sum0_ref)
    for own_ref, sum_ref, rows in ((own0_ref, sum0_ref, EARLY), (own1_ref, sum1_ref, LATE)):
        for i, r in enumerate(rows):
            at = slice(i * TC, (i + 1) * TC)
            spread = own_ref[at, :].astype(F32) + sum_ref[at, :].astype(F32)
            out_ref[r] = grid_values(spread, density(r), weight_ref[...])


def conv_kernel(
    x_ref, up_ref, down_ref, left_ref, right_ref, w1_ref, b1_ref, w2_ref, b2_ref,
    out_ref, out0_ref, out1_ref, wide_ref, x16_ref, first_ref, wc1_ref, wc2_ref,
):
    channels = out_ref.shape[2]
    width = x16_ref.shape[1]
    for a in range(3):
        for b in range(3):
            at = (slice(a * channels, (a + 1) * channels), slice(b * channels, (b + 1) * channels))
            wc1_ref[at] = w1_ref[a, b]
            wc2_ref[at] = w2_ref[a, b]
    body = slice(PAD, PAD + TC)
    wide_ref[...] = jnp.zeros(wide_ref.shape, F32)
    wide_ref[0:2, body] = up_ref[...].astype(F32)
    wide_ref[2 : 2 + SR, body] = x_ref[...].astype(F32)
    wide_ref[2 + SR :, body] = down_ref[...].astype(F32)
    wide_ref[:, PAD - 2 : PAD] = left_ref[...].astype(F32)
    wide_ref[:, PAD + TC : PAD + TC + 2] = right_ref[...].astype(F32)
    x16_ref[...] = wide_ref[...].astype(BF16)

    def taps(source, first, count, weights):
        rows = [source[pl.ds(first + a, count)].reshape(count * width, channels) for a in range(3)]
        all_taps = jnp.dot(jnp.concatenate(rows, axis=1), weights[...], preferred_element_type=F32)
        return (
            pltpu.roll(all_taps[:, :channels], 1, 0)
            + all_taps[:, channels : 2 * channels]
            + pltpu.roll(all_taps[:, 2 * channels :], count * width - 1, 0)
        )

    at_row, at_col = lax.axis_index(("orbits", "rows")), lax.axis_index("cols")
    col = lax.broadcasted_iota(jnp.int32, (width, channels), 0)
    first_col = jnp.where(at_col > 0, PAD - 1, PAD)
    last_col = jnp.where(at_col < lax.axis_size("cols") - 1, PAD + TC, PAD + TC - 1)
    inside = (col >= first_col) & (col <= last_col)
    first_row = jnp.where(at_row > 0, 0, 1)
    last_row = jnp.where(at_row < lax.axis_size(("orbits", "rows")) - 1, SR + 1, SR)
    count = (SR + 2) // 3

    def first_rows(i, unused):
        value = silu(taps(x16_ref, i * count, count, wc1_ref) + b1_ref[...])
        for r in range(count):
            row = i * count + r
            keep = inside & (row >= first_row) & (row <= last_row)
            first_ref[row] = jnp.where(keep, value[r * width : (r + 1) * width], 0.0).astype(BF16)
        return unused

    lax.fori_loop(0, 3, first_rows, 0)
    again = PH

    def second_rows(i, band_ref):
        values = taps(first_ref, i * again, again, wc2_ref) + b2_ref[...]
        for r in range(again):
            row = i * again + r
            value = values[r * width + PAD : r * width + PAD + TC] + x_ref[row].astype(F32)
            out_ref[row] = value.astype(BF16)
            band_ref[r] = value.astype(BF16)

    second_rows(0, out0_ref)
    second_rows(1, out1_ref)


def read_kernel(orbits, most, patch_ref, weights_ref, *refs):
    up, down, (out_ref, grid_ref) = refs[:orbits], refs[orbits : 2 * orbits], refs[2 * orbits :]
    size = out_ref.shape[2]
    for k in range(orbits):
        for piece_ref, way, band in ((up[k], 1, 0), (down[k], -1, 1)):
            grid_ref[pl.ds(stripe_at(orbits - 1 - k, -way) * SR + band * PH, PH)] = piece_ref[...]

    def tile(t, unused):
        for n in range(most):
            at_row, at_col = place(patch_ref[t * most + n])
            values = grid_ref[at_row, at_col, :].reshape(PH * PW, grid_ref.shape[2])
            result = jnp.dot(weights_ref[t * most + n], values, preferred_element_type=F32)
            out_ref[t, n * size : (n + 1) * size, :] = result.astype(BF16)
        return unused

    lax.fori_loop(0, out_ref.shape[0], tile, 0)


def final_kernel(tile_ref, feat_ref, got_ref, out_ref, count_ref):
    blocks, size, _ = feat_ref.shape
    clear(count_ref)
    per = 4

    def chunk(c, unused):
        for k in range(per):
            b = c * per + k
            t, n = next_slot(tile_ref, count_ref, b)
            mine = got_ref[t, pl.ds(pl.multiple_of(n * size, size), size), :]
            out_ref[b] = (feat_ref[b].astype(F32) + mine.astype(F32)).astype(BF16)
        return unused

    lax.fori_loop(0, blocks // per, chunk, 0)


def shifts(axis):
    size = lax.axis_size(axis)
    up = [(i, i + 1) for i in range(size - 1)]
    return up, [(j, i) for i, j in up]


def halo(first, last, axis):
    up, down = shifts(axis)
    return lax.ppermute(last, axis, up), lax.ppermute(first, axis, down)


def turn(x, way):
    size = lax.axis_size("orbits")
    return lax.ppermute(x, "orbits", [(i, (i + way) % size) for i in range(size)])


def ring_sum(stripes, way):
    total = stripes[0]
    for k in range(1, len(stripes)):
        total = turn(total, way)
        if k < len(stripes) - 1:
            total = total + stripes[k]
    return total


def ring_gather(x, way):
    pieces = [x]
    for _ in range(lax.axis_size("orbits") - 1):
        pieces.append(turn(pieces[-1], way))
    return pieces


def local(
    obs_feat, obs_offset, obs_cells, block_tile, block_patch, w_embed, b_embed, w_proj, b_proj,
    density_weight, w_first, b_first, w_second, b_second,
):
    channels = obs_feat.shape[1]
    blocks = block_tile.shape[0]
    size = obs_feat.shape[0] // blocks
    plane = ("rows", "cols")
    tiles = lax.axis_size(plane)
    orbits = lax.axis_size("orbits")
    most = max(2, 2 * blocks // tiles)
    slots = tiles * most
    height = orbits * SR
    patches = height // PH * ACROSS
    length = most * size
    meta_rows = max(16, most * META)
    chunks = blocks // 4
    counts = pltpu.SMEM((tiles,), jnp.int32)
    shape = jax.ShapeDtypeStruct
    bias = lambda b: b.reshape(1, channels)
    exchange = lambda x: lax.all_to_all(x, plane, split_axis=0, concat_axis=0, tiled=True)
    vmem = lambda a: pltpu.VMEM(a.shape, a.dtype)

    b_embed, b_proj = bias(b_embed), bias(b_proj)
    features, send = call(
        embed_kernel,
        [HBM] * 9,
        [VMEM] * 2,
        (shape((blocks, size, channels), BF16), shape((tiles, length + meta_rows, channels), BF16)),
        [
            pltpu.SMEM((blocks,), jnp.int32),
            pltpu.SMEM((blocks,), jnp.int32),
            vmem(obs_offset),
            pltpu.VMEM((8, obs_cells.shape[1]), jnp.int32),
            vmem(obs_feat),
            vmem(w_embed),
            vmem(b_embed),
            vmem(w_proj),
            vmem(b_proj),
            counts,
            pltpu.VMEM((slots * META, size), F32),
            pltpu.SemaphoreType.DMA((8,)),
            pltpu.SemaphoreType.DMA((chunks,)),
        ],
        6 * obs_feat.size * channels,
        8 * obs_feat.size,
        block_tile, block_patch, obs_offset, obs_cells, obs_feat, w_embed, b_embed, w_proj, b_proj,
        limit=LARGE,
    )
    got = exchange(send)

    flops = 2 * slots * size * channels * PH * PW
    early_shape = shape((FULL + SR + CELLS, channels), BF16)
    late_shape = shape((len(LATE) * TC, channels), BF16)
    *bands, patch_of = call(
        functools.partial(spread_kernel, orbits, most),
        [VMEM],
        [VMEM] * (2 * orbits) + [SMEM],
        [early_shape] * orbits + [late_shape] * orbits + [shape((slots,), jnp.int32)],
        [pltpu.VMEM((height, TC, channels), F32), pltpu.VMEM((patches, PH, PW), F32)],
        flops,
        8 * slots * size * channels,
        got,
    )
    bands0, bands1 = bands[:orbits], bands[orbits:]
    sum0, sum1 = ring_sum(bands0, 1), ring_sum(bands1, -1)
    weights = call(
        functools.partial(weights_kernel, most),
        [VMEM],
        VMEM,
        shape((slots, size, PH * PW), BF16),
        [],
        flops,
        4 * slots * size * channels,
        got,
    )
    density_weight = bias(density_weight)
    rows_shape, cols_shape = shape((EDGE, TC, channels), BF16), shape((SR, EDGE, channels), BF16)
    top, bottom, left, right = call(
        edge_kernel,
        [VMEM] * 3,
        [VMEM] * 4,
        [rows_shape] * 2 + [cols_shape] * 2,
        [],
        10000000,
        4 * SR * TC * channels,
        bands0[-1], sum0, density_weight,
    )
    above, below = halo(top, bottom, ("orbits", "rows"))
    left = jnp.concatenate([above[:, :EDGE], left, below[:, :EDGE]], axis=0)
    right = jnp.concatenate([above[:, TC - EDGE :], right, below[:, TC - EDGE :]], axis=0)
    left, right = halo(left, right, "cols")
    grid_in = call(
        grid_kernel,
        [VMEM] * 5,
        VMEM,
        shape((SR, TC, channels), BF16),
        [],
        10000000,
        8 * SR * TC * channels,
        bands0[-1], sum0, bands1[-1], sum1, density_weight,
    )

    width = TC + 2 * PAD
    grid_out, band0, band1 = call(
        conv_kernel,
        [VMEM] * 9,
        [VMEM] * 3,
        [shape((SR, TC, channels), BF16)] + [shape((PH, TC, channels), BF16)] * 2,
        [
            pltpu.VMEM((SR + 4, width, channels), F32),
            pltpu.VMEM((SR + 4, width, channels), BF16),
            pltpu.VMEM((SR + 2, width, channels), BF16),
            pltpu.VMEM((3 * channels, 3 * channels), BF16),
            pltpu.VMEM((3 * channels, 3 * channels), BF16),
        ],
        4 * 9 * SR * TC * channels * channels,
        8 * grid_in.size,
        grid_in, above, below, left, right, w_first, bias(b_first), w_second, bias(b_second),
    )

    readings = call(
        functools.partial(read_kernel, orbits, most),
        [SMEM, VMEM] + [VMEM] * (2 * orbits),
        VMEM,
        shape((tiles, length, channels), BF16),
        [pltpu.VMEM((height, TC, channels), BF16)],
        flops,
        8 * slots * size * channels,
        patch_of, weights, *ring_gather(band0, 1), *ring_gather(band1, -1),
    )
    back = exchange(readings)
    obs_out = call(
        final_kernel,
        [SMEM] + [VMEM] * 2,
        VMEM,
        shape((blocks, size, channels), BF16),
        [counts],
        1000000,
        8 * obs_feat.size,
        block_tile, features, back,
    )
    return obs_out.reshape(obs_feat.shape), grid_out


def solution(mesh):
    spread_out = ("orbits", "rows", "cols")
    in_specs = (
        P(spread_out, None),
        P(None, spread_out),
        P(None, spread_out),
        P(spread_out),
        P(spread_out),
    ) + (P(),) * 9
    out_specs = (P(spread_out, None), P(("orbits", "rows"), "cols", None))
    return jax.shard_map(local, mesh=mesh, in_specs=in_specs, out_specs=out_specs, check_vma=False)
```

```python
import functools

import jax
import jax.numpy as jnp
from jax import lax
from jax.experimental import pallas as pl
from jax.experimental.pallas import tpu as pltpu
from jax.sharding import PartitionSpec as P

KN = 16
PH = 8
PW = 32
SR = 16
TC = 128
SIDE = 4
PAD = 8
META = 4
EDGE = 2
EARLY = (0, 1, SR - 2, SR - 1)
LATE = tuple(r for r in range(SR) if r not in EARLY)
FULL = len(EARLY) * TC
CELLS = -(-len(LATE) * 2 * EDGE // 16) * 16
ACROSS = TC // PW
F32 = jnp.float32
BF16 = jnp.bfloat16

VMEM = pl.BlockSpec(memory_space=pltpu.VMEM)
SMEM = pl.BlockSpec(memory_space=pltpu.SMEM)
HBM = pl.BlockSpec(memory_space=pltpu.HBM)
LIMIT = 20 * 1024 * 1024
LARGE = 56 * 1024 * 1024


def call(kernel, in_specs, out_specs, out_shape, scratch, flops, moved, *args, limit=LIMIT):
    return pl.pallas_call(
        kernel,
        in_specs=in_specs,
        out_specs=out_specs,
        out_shape=out_shape,
        scratch_shapes=scratch,
        compiler_params=pltpu.CompilerParams(vmem_limit_bytes=limit),
        cost_estimate=pl.CostEstimate(flops=flops, bytes_accessed=moved, transcendentals=0),
    )(*args)


def silu(v):
    half = 0.5 * v
    return half + half * jnp.tanh(half)


def next_slot(tile_ref, count_ref, b):
    t = tile_ref[b]
    n = count_ref[t]
    count_ref[t] = n + 1
    return t, n


def clear(count_ref):
    for t in range(count_ref.shape[0]):
        count_ref[t] = 0


def embed_kernel(
    tile_hbm, patch_hbm, offset_hbm, cells_hbm, x_hbm, we_hbm, be_hbm, wp_hbm, bp_hbm,
    feat_hbm, send_hbm,
    tile_ref, patch_ref, offset_ref, cells_ref, x_ref, we_ref, be_ref, wp_ref, bp_ref, feat_ref,
    zero_ref, count_ref, slot_ref, meta_ref, meta16_ref, sems, x_sems, feat_sems, send_sems,
):
    blocks, size, channels = feat_ref.shape
    chunks = x_sems.shape[0]
    per = blocks // chunks
    tiles, meta_rows = meta16_ref.shape[0], meta_ref.shape[0] // meta16_ref.shape[0]
    most = meta_rows // META
    base = most * size
    pairs = (
        (tile_hbm, tile_ref), (patch_hbm, patch_ref), (offset_hbm, offset_ref), (cells_hbm.at[0:8], cells_ref),
        (we_hbm, we_ref), (be_hbm, be_ref), (wp_hbm, wp_ref), (bp_hbm, bp_ref),
    )
    copies = [pltpu.make_async_copy(a, b, sems.at[i]) for i, (a, b) in enumerate(pairs)]

    def rows_of(c):
        return pl.ds(pl.multiple_of(c * per * size, per * size), per * size)

    def fetch(c):
        return pltpu.make_async_copy(x_hbm.at[rows_of(c)], x_ref.at[rows_of(c)], x_sems.at[c])

    def keep(c):
        at = pl.ds(c * per, per)
        return pltpu.make_async_copy(feat_ref.at[at], feat_hbm.at[at], feat_sems.at[c])

    def send(source, slot):
        rows = pl.ds(pl.multiple_of(lax.rem(slot, most) * size, size), size)
        return pltpu.make_async_copy(source, send_hbm.at[slot // most, rows], send_sems.at[slot])

    for copy in copies:
        copy.start()
    for c in range(chunks):
        fetch(c).start()
    zero_ref[...] = jnp.zeros(zero_ref.shape, BF16)
    clear(count_ref)
    row = lax.broadcasted_iota(jnp.int32, meta_ref.shape, 0) % META
    meta_ref[...] = jnp.where(row == 2, -65536.0, 0.0)
    copies[0].wait()
    for b in range(blocks):
        t, n = next_slot(tile_ref, count_ref, b)
        slot_ref[b] = t * most + n
    for t in range(tiles):
        for n in range(most):

            @pl.when(n >= count_ref[t])
            def _():
                send(zero_ref, t * most + n).start()

    for copy in copies[4:]:
        copy.wait()

    def chunk(c, unused):
        fetch(c).wait()
        hidden = silu(jnp.dot(x_ref[rows_of(c), :], we_ref[...], preferred_element_type=F32) + be_ref[...])
        out = jnp.dot(hidden.astype(BF16), wp_ref[...], preferred_element_type=F32) + bp_ref[...]
        feat_ref[pl.ds(c * per, per)] = out.astype(BF16).reshape(per, size, channels)
        keep(c).start()
        for k in range(per):
            b = c * per + k
            send(feat_ref.at[b], slot_ref[b]).start()
        return unused

    lax.fori_loop(0, chunks, chunk, 0)
    for copy in copies[1:4]:
        copy.wait()
    for b in range(blocks):
        first = slot_ref[b] * META
        obs = slice(b * size, (b + 1) * size)
        meta_ref[pl.ds(first, 2), :] = offset_ref[:, obs].astype(F32)
        meta_ref[pl.ds(first + 2, 1), :] = cells_ref[0:1, obs].astype(F32)
        meta_ref[pl.ds(first + 3, 1), :] = jnp.full((1, size), patch_ref[b], jnp.int32).astype(F32)
    extra = meta16_ref.shape[1] - meta_rows
    for t in range(tiles):
        rows = meta_ref[t * meta_rows : (t + 1) * meta_rows, :]
        if extra:
            rows = jnp.concatenate([rows, jnp.zeros((extra, size), F32)], axis=0)
        meta16_ref[t] = rows.astype(BF16)
    described = pltpu.make_async_copy(
        meta16_ref, send_hbm.at[:, pl.ds(base, meta16_ref.shape[1])], sems.at[len(copies)]
    )
    described.start()

    def finish(c, unused):
        keep(c).wait()
        return unused

    lax.fori_loop(0, chunks, finish, 0)
    for slot in range(tiles * most):
        send(zero_ref, slot).wait()
    described.wait()


def factors(meta, normal):
    off_row, off_col, corner = meta[0:1, :], meta[1:2, :], meta[2:3, :]
    first_row = jnp.floor(corner * (1.0 / PW))
    first_col = corner - first_row * PW

    def factor(count, start, off):
        at = lax.broadcasted_iota(jnp.int32, (count, meta.shape[1]), 0).astype(F32) - start
        delta = at - 1.5 - off
        value = jnp.exp(delta * delta * -0.5)
        return jnp.where((at >= 0.0) & (at < SIDE), value, 0.0)

    def total(off):
        at = lax.broadcasted_iota(jnp.int32, (SIDE, meta.shape[1]), 0).astype(F32)
        delta = at - 1.5 - off
        return jnp.sum(jnp.exp(delta * delta * -0.5), axis=0, keepdims=True)

    rows, cols = factor(PH, first_row, off_row), factor(PW, first_col, off_col)
    if normal:
        rows = rows / (total(off_row) * total(off_col))
    return rows, cols


def outer(rows, cols):
    return (rows[:, None, :] * cols[None, :, :]).reshape(PH * PW, rows.shape[1])


def place(patch):
    row, col = patch // ACROSS, lax.rem(patch, ACROSS)
    return pl.ds(pl.multiple_of(row * PH, PH), PH), pl.ds(pl.multiple_of(col * PW, PW), PW)


def stripe_at(k, way):
    orbits = lax.axis_size("orbits")
    return lax.rem(lax.axis_index("orbits") + way * (orbits - 1 - k) + orbits * orbits, orbits)


def spread_kernel(orbits, most, got_ref, *refs):
    up, down, (patch_ref, acc_ref, dens_ref) = refs[:orbits], refs[orbits : 2 * orbits], refs[2 * orbits :]
    size, channels = got_ref.shape[2], acc_ref.shape[2]
    acc_ref[...] = jnp.zeros(acc_ref.shape, F32)
    dens_ref[...] = jnp.zeros(dens_ref.shape, F32)
    base = most * size

    def tile(t, unused):
        metas = got_ref[t, base:, :].astype(F32)
        patches = [jnp.max(metas[n * META + 3 : n * META + 4, :]).astype(jnp.int32) for n in range(most)]
        for n in range(most):
            patch = patches[n]
            patch_ref[t * most + n] = patch
            rows, cols = factors(metas[n * META : (n + 1) * META], False)
            values = got_ref[t, n * size : (n + 1) * size, :]
            result = jnp.dot(outer(rows, cols).astype(BF16), values, preferred_element_type=F32)
            at_row, at_col = place(patch)
            acc_ref[at_row, at_col, :] += result.reshape(PH, PW, channels)
            dens_ref[patch] += lax.dot_general(
                rows.astype(BF16), cols.astype(BF16), (((1,), (1,)), ((), ())), preferred_element_type=F32
            )
        return unused

    lax.fori_loop(0, got_ref.shape[0], tile, 0)
    for k in range(orbits):
        for out_ref, way, rows in ((up[k], 1, EARLY), (down[k], -1, LATE)):
            first = stripe_at(k, way) * SR
            for i, r in enumerate(rows):
                out_ref[i * TC : (i + 1) * TC, :] = acc_ref[first + r].astype(BF16)
        first = stripe_at(k, 1) * SR
        bands = []
        for band in range(SR // PH):
            at = (stripe_at(k, 1) * (SR // PH) + band) * ACROSS
            bands.append(jnp.concatenate([dens_ref[at + c] for c in range(ACROSS)], axis=1))
        up[k][FULL : FULL + SR, :] = jnp.concatenate(bands, axis=0).astype(BF16)
        cells = [acc_ref[first + r, at] for r in LATE for at in (slice(0, EDGE), slice(TC - EDGE, TC))]
        spare = CELLS - len(LATE) * 2 * EDGE
        if spare:
            cells.append(jnp.zeros((spare, channels), F32))
        up[k][FULL + SR :, :] = jnp.concatenate(cells, axis=0).astype(BF16)


def weights_kernel(most, got_ref, out_ref):
    base = most * got_ref.shape[2]

    def tile(t, unused):
        metas = got_ref[t, base:, :].astype(F32)
        for n in range(most):
            rows, cols = factors(metas[n * META : (n + 1) * META], True)
            out_ref[t * most + n] = outer(rows, cols).T.astype(BF16)
        return unused

    lax.fori_loop(0, got_ref.shape[0], tile, 0)


def grid_values(spread, density, weight):
    return (spread / jnp.maximum(density, 1.0) + weight * (density / (1.0 + density))).astype(BF16)


def densities(own_ref, sum_ref):
    tail = slice(FULL, FULL + SR)
    columns = (own_ref[tail, :].astype(F32) + sum_ref[tail, :].astype(F32)).T
    return lambda r: jnp.broadcast_to(columns[:, r : r + 1], (TC, own_ref.shape[1]))


def edge_kernel(own_ref, sum_ref, weight_ref, top_ref, bottom_ref, left_ref, right_ref):
    density = densities(own_ref, sum_ref)
    weight = weight_ref[...]
    low, high = slice(0, EDGE), slice(TC - EDGE, TC)
    cells = own_ref[FULL + SR :, :].astype(F32) + sum_ref[FULL + SR :, :].astype(F32)
    for r in range(SR):
        d = density(r)
        if r in EARLY:
            at = slice(EARLY.index(r) * TC, (EARLY.index(r) + 1) * TC)
            spread = own_ref[at, :].astype(F32) + sum_ref[at, :].astype(F32)
            row = grid_values(spread, d, weight)
            if r < EDGE:
                top_ref[r] = row
            if r >= SR - EDGE:
                bottom_ref[r - (SR - EDGE)] = row
            left_ref[r], right_ref[r] = row[low], row[high]
        else:
            at = LATE.index(r) * 2 * EDGE
            left_ref[r] = grid_values(cells[at : at + EDGE], d[low], weight)
            right_ref[r] = grid_values(cells[at + EDGE : at + 2 * EDGE], d[high], weight)


def grid_kernel(own0_ref, sum0_ref, own1_ref, sum1_ref, weight_ref, out_ref):
    density = densities(own0_ref, sum0_ref)
    for own_ref, sum_ref, rows in ((own0_ref, sum0_ref, EARLY), (own1_ref, sum1_ref, LATE)):
        for i, r in enumerate(rows):
            at = slice(i * TC, (i + 1) * TC)
            spread = own_ref[at, :].astype(F32) + sum_ref[at, :].astype(F32)
            out_ref[r] = grid_values(spread, density(r), weight_ref[...])


def conv_kernel(
    x_ref, up_ref, down_ref, left_ref, right_ref, w1_ref, b1_ref, w2_ref, b2_ref,
    out_ref, out0_ref, out1_ref, wide_ref, x16_ref, first_ref, wc1_ref, wc2_ref,
):
    channels = out_ref.shape[2]
    width = x16_ref.shape[1]
    for a in range(3):
        for b in range(3):
            at = (slice(a * channels, (a + 1) * channels), slice(b * channels, (b + 1) * channels))
            wc1_ref[at] = w1_ref[a, b]
            wc2_ref[at] = w2_ref[a, b]
    body = slice(PAD, PAD + TC)
    wide_ref[...] = jnp.zeros(wide_ref.shape, F32)
    wide_ref[0:2, body] = up_ref[...].astype(F32)
    wide_ref[2 : 2 + SR, body] = x_ref[...].astype(F32)
    wide_ref[2 + SR :, body] = down_ref[...].astype(F32)
    wide_ref[:, PAD - 2 : PAD] = left_ref[...].astype(F32)
    wide_ref[:, PAD + TC : PAD + TC + 2] = right_ref[...].astype(F32)
    x16_ref[...] = wide_ref[...].astype(BF16)

    def taps(source, first, count, weights):
        rows = [source[pl.ds(first + a, count)].reshape(count * width, channels) for a in range(3)]
        all_taps = jnp.dot(jnp.concatenate(rows, axis=1), weights[...], preferred_element_type=F32)
        return (
            pltpu.roll(all_taps[:, :channels], 1, 0)
            + all_taps[:, channels : 2 * channels]
            + pltpu.roll(all_taps[:, 2 * channels :], count * width - 1, 0)
        )

    at_row, at_col = lax.axis_index(("orbits", "rows")), lax.axis_index("cols")
    col = lax.broadcasted_iota(jnp.int32, (width, channels), 0)
    first_col = jnp.where(at_col > 0, PAD - 1, PAD)
    last_col = jnp.where(at_col < lax.axis_size("cols") - 1, PAD + TC, PAD + TC - 1)
    inside = (col >= first_col) & (col <= last_col)
    first_row = jnp.where(at_row > 0, 0, 1)
    last_row = jnp.where(at_row < lax.axis_size(("orbits", "rows")) - 1, SR + 1, SR)
    count = (SR + 2) // 3

    def first_rows(i, unused):
        value = silu(taps(x16_ref, i * count, count, wc1_ref) + b1_ref[...])
        for r in range(count):
            row = i * count + r
            keep = inside & (row >= first_row) & (row <= last_row)
            first_ref[row] = jnp.where(keep, value[r * width : (r + 1) * width], 0.0).astype(BF16)
        return unused

    lax.fori_loop(0, 3, first_rows, 0)
    again = PH

    def second_rows(i, band_ref):
        values = taps(first_ref, i * again, again, wc2_ref) + b2_ref[...]
        for r in range(again):
            row = i * again + r
            value = values[r * width + PAD : r * width + PAD + TC] + x_ref[row].astype(F32)
            out_ref[row] = value.astype(BF16)
            band_ref[r] = value.astype(BF16)

    second_rows(0, out0_ref)
    second_rows(1, out1_ref)


def read_kernel(orbits, most, patch_ref, weights_ref, *refs):
    up, down, (out_ref, grid_ref) = refs[:orbits], refs[orbits : 2 * orbits], refs[2 * orbits :]
    size = out_ref.shape[2]
    for k in range(orbits):
        for piece_ref, way, band in ((up[k], 1, 0), (down[k], -1, 1)):
            grid_ref[pl.ds(stripe_at(orbits - 1 - k, -way) * SR + band * PH, PH)] = piece_ref[...]

    def tile(t, unused):
        for n in range(most):
            at_row, at_col = place(patch_ref[t * most + n])
            values = grid_ref[at_row, at_col, :].reshape(PH * PW, grid_ref.shape[2])
            result = jnp.dot(weights_ref[t * most + n], values, preferred_element_type=F32)
            out_ref[t, n * size : (n + 1) * size, :] = result.astype(BF16)
        return unused

    lax.fori_loop(0, out_ref.shape[0], tile, 0)


def final_kernel(tile_ref, feat_ref, got_ref, out_hbm, out_ref, count_ref, sems):
    blocks, size, _ = feat_ref.shape
    chunks = sems.shape[0]
    per = blocks // chunks
    clear(count_ref)

    def give(c):
        at = pl.ds(c * per, per)
        return pltpu.make_async_copy(out_ref.at[at], out_hbm.at[at], sems.at[c])

    def chunk(c, unused):
        for k in range(per):
            b = c * per + k
            t, n = next_slot(tile_ref, count_ref, b)
            mine = got_ref[t, pl.ds(pl.multiple_of(n * size, size), size), :]
            out_ref[b] = (feat_ref[b].astype(F32) + mine.astype(F32)).astype(BF16)
        give(c).start()
        return unused

    lax.fori_loop(0, chunks, chunk, 0)
    for c in range(chunks):
        give(c).wait()


def shifts(axis):
    size = lax.axis_size(axis)
    up = [(i, i + 1) for i in range(size - 1)]
    return up, [(j, i) for i, j in up]


def halo(first, last, axis):
    up, down = shifts(axis)
    return lax.ppermute(last, axis, up), lax.ppermute(first, axis, down)


def turn(x, way):
    size = lax.axis_size("orbits")
    return lax.ppermute(x, "orbits", [(i, (i + way) % size) for i in range(size)])


def ring_sum(stripes, way):
    total = stripes[0]
    for k in range(1, len(stripes)):
        total = turn(total, way)
        if k < len(stripes) - 1:
            total = total + stripes[k]
    return total


def ring_gather(x, way):
    pieces = [x]
    for _ in range(lax.axis_size("orbits") - 1):
        pieces.append(turn(pieces[-1], way))
    return pieces


def local(
    obs_feat, obs_offset, obs_cells, block_tile, block_patch, w_embed, b_embed, w_proj, b_proj,
    density_weight, w_first, b_first, w_second, b_second,
):
    channels = obs_feat.shape[1]
    blocks = block_tile.shape[0]
    size = obs_feat.shape[0] // blocks
    plane = ("rows", "cols")
    tiles = lax.axis_size(plane)
    orbits = lax.axis_size("orbits")
    most = max(2, 2 * blocks // tiles)
    slots = tiles * most
    height = orbits * SR
    patches = height // PH * ACROSS
    length = most * size
    meta_rows = max(16, most * META)
    chunks = blocks // 8
    counts = pltpu.SMEM((tiles,), jnp.int32)
    shape = jax.ShapeDtypeStruct
    bias = lambda b: b.reshape(1, channels)
    exchange = lambda x: lax.all_to_all(x, plane, split_axis=0, concat_axis=0, tiled=True)
    vmem = lambda a: pltpu.VMEM(a.shape, a.dtype)

    b_embed, b_proj = bias(b_embed), bias(b_proj)
    features, send = call(
        embed_kernel,
        [HBM] * 9,
        [HBM] * 2,
        (shape((blocks, size, channels), BF16), shape((tiles, length + meta_rows, channels), BF16)),
        [
            pltpu.SMEM((blocks,), jnp.int32),
            pltpu.SMEM((blocks,), jnp.int32),
            vmem(obs_offset),
            pltpu.VMEM((8, obs_cells.shape[1]), jnp.int32),
            vmem(obs_feat),
            vmem(w_embed),
            vmem(b_embed),
            vmem(w_proj),
            vmem(b_proj),
            pltpu.VMEM((blocks, size, channels), BF16),
            pltpu.VMEM((size, channels), BF16),
            counts,
            pltpu.SMEM((blocks,), jnp.int32),
            pltpu.VMEM((slots * META, size), F32),
            pltpu.VMEM((tiles, meta_rows, size), BF16),
            pltpu.SemaphoreType.DMA((9,)),
            pltpu.SemaphoreType.DMA((chunks,)),
            pltpu.SemaphoreType.DMA((chunks,)),
            pltpu.SemaphoreType.DMA((slots,)),
        ],
        6 * obs_feat.size * channels,
        8 * obs_feat.size,
        block_tile, block_patch, obs_offset, obs_cells, obs_feat, w_embed, b_embed, w_proj, b_proj,
        limit=LARGE,
    )
    got = exchange(send)

    flops = 2 * slots * size * channels * PH * PW
    early_shape = shape((FULL + SR + CELLS, channels), BF16)
    late_shape = shape((len(LATE) * TC, channels), BF16)
    *bands, patch_of = call(
        functools.partial(spread_kernel, orbits, most),
        [VMEM],
        [VMEM] * (2 * orbits) + [SMEM],
        [early_shape] * orbits + [late_shape] * orbits + [shape((slots,), jnp.int32)],
        [pltpu.VMEM((height, TC, channels), F32), pltpu.VMEM((patches, PH, PW), F32)],
        flops,
        8 * slots * size * channels,
        got,
    )
    bands0, bands1 = bands[:orbits], bands[orbits:]
    sum0, sum1 = ring_sum(bands0, 1), ring_sum(bands1, -1)
    weights = call(
        functools.partial(weights_kernel, most),
        [VMEM],
        VMEM,
        shape((slots, size, PH * PW), BF16),
        [],
        flops,
        4 * slots * size * channels,
        got,
    )
    density_weight = bias(density_weight)
    rows_shape, cols_shape = shape((EDGE, TC, channels), BF16), shape((SR, EDGE, channels), BF16)
    top, bottom, left, right = call(
        edge_kernel,
        [VMEM] * 3,
        [VMEM] * 4,
        [rows_shape] * 2 + [cols_shape] * 2,
        [],
        10000000,
        4 * SR * TC * channels,
        bands0[-1], sum0, density_weight,
    )
    above, below = halo(top, bottom, ("orbits", "rows"))
    left = jnp.concatenate([above[:, :EDGE], left, below[:, :EDGE]], axis=0)
    right = jnp.concatenate([above[:, TC - EDGE :], right, below[:, TC - EDGE :]], axis=0)
    left, right = halo(left, right, "cols")
    grid_in = call(
        grid_kernel,
        [VMEM] * 5,
        VMEM,
        shape((SR, TC, channels), BF16),
        [],
        10000000,
        8 * SR * TC * channels,
        bands0[-1], sum0, bands1[-1], sum1, density_weight,
    )

    width = TC + 2 * PAD
    grid_out, band0, band1 = call(
        conv_kernel,
        [VMEM] * 9,
        [VMEM] * 3,
        [shape((SR, TC, channels), BF16)] + [shape((PH, TC, channels), BF16)] * 2,
        [
            pltpu.VMEM((SR + 4, width, channels), F32),
            pltpu.VMEM((SR + 4, width, channels), BF16),
            pltpu.VMEM((SR + 2, width, channels), BF16),
            pltpu.VMEM((3 * channels, 3 * channels), BF16),
            pltpu.VMEM((3 * channels, 3 * channels), BF16),
        ],
        4 * 9 * SR * TC * channels * channels,
        8 * grid_in.size,
        grid_in, above, below, left, right, w_first, bias(b_first), w_second, bias(b_second),
    )

    readings = call(
        functools.partial(read_kernel, orbits, most),
        [SMEM, VMEM] + [VMEM] * (2 * orbits),
        VMEM,
        shape((tiles, length, channels), BF16),
        [pltpu.VMEM((height, TC, channels), BF16)],
        flops,
        8 * slots * size * channels,
        patch_of, weights, *ring_gather(band0, 1), *ring_gather(band1, -1),
    )
    back = exchange(readings)
    obs_out = call(
        final_kernel,
        [SMEM] + [VMEM] * 2,
        HBM,
        shape((blocks, size, channels), BF16),
        [pltpu.VMEM((blocks, size, channels), BF16), counts, pltpu.SemaphoreType.DMA((chunks,))],
        1000000,
        8 * obs_feat.size,
        block_tile, features, back,
    )
    return obs_out.reshape(obs_feat.shape), grid_out


def solution(mesh):
    spread_out = ("orbits", "rows", "cols")
    in_specs = (
        P(spread_out, None),
        P(None, spread_out),
        P(None, spread_out),
        P(spread_out),
        P(spread_out),
    ) + (P(),) * 9
    out_specs = (P(spread_out, None), P(("orbits", "rows"), "cols", None))
    return jax.shard_map(local, mesh=mesh, in_specs=in_specs, out_specs=out_specs, check_vma=False)
```

```python
import functools

import jax
import jax.numpy as jnp
from jax import lax
from jax.experimental import pallas as pl
from jax.experimental.pallas import tpu as pltpu
from jax.sharding import PartitionSpec as P

KN = 16
PH = 8
PW = 32
SR = 16
TC = 128
SIDE = 4
PAD = 8
META = 4
BANDS = SR // PH
GROUP = 4
EDGE = 2
EARLY = (0, 1, SR - 2, SR - 1)
LATE = tuple(r for r in range(SR) if r not in EARLY)
FULL = len(EARLY) * TC
CELLS = -(-len(LATE) * 2 * EDGE // 16) * 16
ACROSS = TC // PW
F32 = jnp.float32
BF16 = jnp.bfloat16

VMEM = pl.BlockSpec(memory_space=pltpu.VMEM)
SMEM = pl.BlockSpec(memory_space=pltpu.SMEM)
HBM = pl.BlockSpec(memory_space=pltpu.HBM)
LIMIT = 20 * 1024 * 1024
LARGE = 56 * 1024 * 1024


def call(kernel, in_specs, out_specs, out_shape, scratch, flops, moved, *args, limit=LIMIT):
    return pl.pallas_call(
        kernel,
        in_specs=in_specs,
        out_specs=out_specs,
        out_shape=out_shape,
        scratch_shapes=scratch,
        compiler_params=pltpu.CompilerParams(vmem_limit_bytes=limit),
        cost_estimate=pl.CostEstimate(flops=flops, bytes_accessed=moved, transcendentals=0),
    )(*args)


def silu(v):
    half = 0.5 * v
    return half + half * jnp.tanh(half)


def next_slot(tile_ref, count_ref, b):
    t = tile_ref[b]
    n = count_ref[t]
    count_ref[t] = n + 1
    return t, n


def clear(count_ref):
    for t in range(count_ref.shape[0]):
        count_ref[t] = 0


def embed_kernel(
    tile_hbm, patch_hbm, offset_hbm, cells_hbm, x_hbm, we_hbm, be_hbm, wp_hbm, bp_hbm,
    feat_hbm, send_hbm,
    tile_ref, patch_ref, offset_ref, cells_ref, x_ref, we_ref, be_ref, wp_ref, bp_ref, feat_ref,
    zero_ref, count_ref, slot_ref, meta_ref, meta16_ref, sems, x_sems, feat_sems, send_sems,
):
    blocks, size, channels = feat_ref.shape
    chunks = x_sems.shape[0]
    per = blocks // chunks
    tiles, meta_rows = meta16_ref.shape[0], meta_ref.shape[0] // meta16_ref.shape[0]
    most = meta_rows // META
    base = most * size
    pairs = (
        (tile_hbm, tile_ref), (patch_hbm, patch_ref), (offset_hbm, offset_ref), (cells_hbm.at[0:8], cells_ref),
        (we_hbm, we_ref), (be_hbm, be_ref), (wp_hbm, wp_ref), (bp_hbm, bp_ref),
    )
    copies = [pltpu.make_async_copy(a, b, sems.at[i]) for i, (a, b) in enumerate(pairs)]

    def rows_of(c):
        return pl.ds(pl.multiple_of(c * per * size, per * size), per * size)

    def fetch(c):
        return pltpu.make_async_copy(x_hbm.at[rows_of(c)], x_ref.at[rows_of(c)], x_sems.at[c])

    def keep(c):
        at = pl.ds(c * per, per)
        return pltpu.make_async_copy(feat_ref.at[at], feat_hbm.at[at], feat_sems.at[c])

    def send(source, slot):
        rows = pl.ds(pl.multiple_of(lax.rem(slot, most) * size, size), size)
        return pltpu.make_async_copy(source, send_hbm.at[slot // most, rows], send_sems.at[slot])

    for copy in copies:
        copy.start()
    for c in range(chunks):
        fetch(c).start()
    zero_ref[...] = jnp.zeros(zero_ref.shape, BF16)
    clear(count_ref)
    row = lax.broadcasted_iota(jnp.int32, meta_ref.shape, 0) % META
    meta_ref[...] = jnp.where(row == 2, -65536.0, jnp.where(row == 3, -1.0, 0.0))
    copies[0].wait()
    for b in range(blocks):
        t, n = next_slot(tile_ref, count_ref, b)
        slot_ref[b] = t * most + n
    for t in range(tiles):
        for n in range(most):

            @pl.when(n >= count_ref[t])
            def _():
                send(zero_ref, t * most + n).start()

    for copy in copies[4:]:
        copy.wait()

    def chunk(c, unused):
        fetch(c).wait()
        hidden = silu(jnp.dot(x_ref[rows_of(c), :], we_ref[...], preferred_element_type=F32) + be_ref[...])
        out = jnp.dot(hidden.astype(BF16), wp_ref[...], preferred_element_type=F32) + bp_ref[...]
        feat_ref[pl.ds(c * per, per)] = out.astype(BF16).reshape(per, size, channels)
        keep(c).start()
        for k in range(per):
            b = c * per + k
            send(feat_ref.at[b], slot_ref[b]).start()
        return unused

    lax.fori_loop(0, chunks, chunk, 0)
    for copy in copies[1:4]:
        copy.wait()
    for b in range(blocks):
        first = slot_ref[b] * META
        obs = slice(b * size, (b + 1) * size)
        meta_ref[pl.ds(first, 2), :] = offset_ref[:, obs].astype(F32)
        meta_ref[pl.ds(first + 2, 1), :] = cells_ref[0:1, obs].astype(F32)
        meta_ref[pl.ds(first + 3, 1), :] = jnp.full((1, size), patch_ref[b], jnp.int32).astype(F32)
    extra = meta16_ref.shape[1] - meta_rows
    for t in range(tiles):
        rows = meta_ref[t * meta_rows : (t + 1) * meta_rows, :]
        if extra:
            rows = jnp.concatenate([rows, jnp.zeros((extra, size), F32)], axis=0)
        meta16_ref[t] = rows.astype(BF16)
    described = pltpu.make_async_copy(
        meta16_ref, send_hbm.at[:, pl.ds(base, meta16_ref.shape[1])], sems.at[len(copies)]
    )
    described.start()

    def finish(c, unused):
        keep(c).wait()
        return unused

    lax.fori_loop(0, chunks, finish, 0)
    for slot in range(tiles * most):
        send(zero_ref, slot).wait()
    described.wait()


def factors(meta, normal):
    off_row, off_col, corner = meta[0:1, :], meta[1:2, :], meta[2:3, :]
    first_row = jnp.floor(corner * (1.0 / PW))
    first_col = corner - first_row * PW

    def factor(count, start, off):
        at = lax.broadcasted_iota(jnp.int32, (count, meta.shape[1]), 0).astype(F32) - start
        delta = at - 1.5 - off
        value = jnp.exp(delta * delta * -0.5)
        return jnp.where((at >= 0.0) & (at < SIDE), value, 0.0)

    def total(off):
        at = lax.broadcasted_iota(jnp.int32, (SIDE, meta.shape[1]), 0).astype(F32)
        delta = at - 1.5 - off
        return jnp.sum(jnp.exp(delta * delta * -0.5), axis=0, keepdims=True)

    rows, cols = factor(PH, first_row, off_row), factor(PW, first_col, off_col)
    if normal:
        rows = rows / (total(off_row) * total(off_col))
    return rows, cols


def outer(rows, cols):
    return (rows[:, None, :] * cols[None, :, :]).reshape(PH * PW, rows.shape[1])


def place(patch):
    row, col = patch // ACROSS, lax.rem(patch, ACROSS)
    return pl.ds(pl.multiple_of(row * PH, PH), PH), pl.ds(pl.multiple_of(col * PW, PW), PW)


def stripe_at(k, way):
    orbits = lax.axis_size("orbits")
    return lax.rem(lax.axis_index("orbits") + way * (orbits - 1 - k) + orbits * orbits, orbits)


def choose(list_ref, patch_ref, wanted):
    def look(slot, count):
        patch = patch_ref[slot]
        list_ref[count] = slot
        return count + jnp.where((patch >= 0) & wanted(jnp.maximum(patch, 0)), 1, 0)

    return lax.fori_loop(0, patch_ref.shape[0], look, 0, unroll=8)


def for_chosen(list_ref, count, spare, body):
    for j in range(GROUP):
        list_ref[count + j] = spare

    def some(i, unused):
        for j in range(GROUP):
            body(list_ref[i * GROUP + j])
        return unused

    lax.fori_loop(0, (count + GROUP - 1) // GROUP, some, 0)


def odd_distance(stripe):
    return lax.rem(stripe + lax.axis_index("orbits"), 2) == 1


def spread_kernel(orbits, most, leading, *refs):
    ks = range(0 if leading else 1, orbits, 2)
    if leading:
        got_ref, *refs = refs
    else:
        patch_ref, got_ref, *refs = refs
    outs, refs = refs[: 2 * len(ks)], refs[2 * len(ks) :]
    if leading:
        patch_ref, *refs = refs
    acc_ref, dens_ref, meta_ref, list_ref = refs
    size, channels = got_ref.shape[2], acc_ref.shape[2]
    tiles, slots = got_ref.shape[0], patch_ref.shape[0]
    base, rows_of = most * size, most * META
    acc_ref[...] = jnp.zeros(acc_ref.shape, F32)
    dens_ref[...] = jnp.zeros(dens_ref.shape, F32)
    for t in range(tiles):
        metas = got_ref[t, base:, :].astype(F32)[:rows_of]
        meta_ref[t * rows_of : (t + 1) * rows_of, :] = metas
        if leading:
            for n in range(most):
                patch_ref[t * most + n] = jnp.max(metas[n * META + 3 : n * META + 4, :]).astype(jnp.int32)
    meta_ref[slots * META :, :] = jnp.full((meta_ref.shape[0] - slots * META, size), -65536.0, F32)
    per = BANDS * ACROSS
    count = choose(list_ref, patch_ref, lambda patch: odd_distance(patch // per) == leading)

    def add(slot):
        real = jnp.minimum(slot, slots - 1)
        patch = jnp.maximum(patch_ref[real], 0)
        metas = meta_ref[pl.ds(slot * META, META), :]
        rows, cols = factors(metas, False)
        values = got_ref[real // most, pl.ds(pl.multiple_of(lax.rem(real, most) * size, size), size), :]
        result = jnp.dot(outer(rows, cols).astype(BF16), values, preferred_element_type=F32)
        band = patch // ACROSS
        at_row = band // BANDS // 2 * SR + lax.rem(band, BANDS) * PH
        at_col = pl.ds(pl.multiple_of(lax.rem(patch, ACROSS) * PW, PW), PW)
        acc_ref[pl.ds(at_row, PH), at_col, :] += result.reshape(PH, PW, channels)
        dens_ref[patch] += lax.dot_general(
            rows.astype(BF16), cols.astype(BF16), (((1,), (1,)), ((), ())), preferred_element_type=F32
        )

    for_chosen(list_ref, count, slots, add)
    for j, k in enumerate(ks):
        for out_ref, way, rows in ((outs[2 * j], 1, EARLY), (outs[2 * j + 1], -1, LATE)):
            first = stripe_at(k, way) // 2 * SR
            for i, r in enumerate(rows):
                out_ref[i * TC : (i + 1) * TC, :] = acc_ref[first + r].astype(BF16)
        out_ref = outs[2 * j]
        stripe = stripe_at(k, 1)
        first = stripe // 2 * SR
        bands = []
        for band in range(BANDS):
            at = (stripe * BANDS + band) * ACROSS
            bands.append(jnp.concatenate([dens_ref[at + c] for c in range(ACROSS)], axis=1))
        out_ref[FULL : FULL + SR, :] = jnp.concatenate(bands, axis=0).astype(BF16)
        cells = [acc_ref[first + r, at] for r in LATE for at in (slice(0, EDGE), slice(TC - EDGE, TC))]
        spare = CELLS - len(LATE) * 2 * EDGE
        if spare:
            cells.append(jnp.zeros((spare, channels), F32))
        out_ref[FULL + SR :, :] = jnp.concatenate(cells, axis=0).astype(BF16)


def weights_kernel(most, got_ref, out_ref):
    base = most * got_ref.shape[2]

    def tile(t, unused):
        metas = got_ref[t, base:, :].astype(F32)
        for n in range(most):
            rows, cols = factors(metas[n * META : (n + 1) * META], True)
            out_ref[t * most + n] = outer(rows, cols).T.astype(BF16)
        return unused

    lax.fori_loop(0, got_ref.shape[0], tile, 0)


def grid_values(spread, density, weight):
    return (spread / jnp.maximum(density, 1.0) + weight * (density / (1.0 + density))).astype(BF16)


def densities(own_ref, sum_ref):
    tail = slice(FULL, FULL + SR)
    columns = (own_ref[tail, :].astype(F32) + sum_ref[tail, :].astype(F32)).T
    return lambda r: jnp.broadcast_to(columns[:, r : r + 1], (TC, own_ref.shape[1]))


def edge_kernel(own_ref, sum_ref, weight_ref, top_ref, bottom_ref, left_ref, right_ref):
    density = densities(own_ref, sum_ref)
    weight = weight_ref[...]
    low, high = slice(0, EDGE), slice(TC - EDGE, TC)
    cells = own_ref[FULL + SR :, :].astype(F32) + sum_ref[FULL + SR :, :].astype(F32)
    for r in range(SR):
        d = density(r)
        if r in EARLY:
            at = slice(EARLY.index(r) * TC, (EARLY.index(r) + 1) * TC)
            spread = own_ref[at, :].astype(F32) + sum_ref[at, :].astype(F32)
            row = grid_values(spread, d, weight)
            if r < EDGE:
                top_ref[r] = row
            if r >= SR - EDGE:
                bottom_ref[r - (SR - EDGE)] = row
            left_ref[r], right_ref[r] = row[low], row[high]
        else:
            at = LATE.index(r) * 2 * EDGE
            left_ref[r] = grid_values(cells[at : at + EDGE], d[low], weight)
            right_ref[r] = grid_values(cells[at + EDGE : at + 2 * EDGE], d[high], weight)


def grid_kernel(own0_ref, sum0_ref, own1_ref, sum1_ref, weight_ref, out_ref):
    density = densities(own0_ref, sum0_ref)
    for own_ref, sum_ref, rows in ((own0_ref, sum0_ref, EARLY), (own1_ref, sum1_ref, LATE)):
        for i, r in enumerate(rows):
            at = slice(i * TC, (i + 1) * TC)
            spread = own_ref[at, :].astype(F32) + sum_ref[at, :].astype(F32)
            out_ref[r] = grid_values(spread, density(r), weight_ref[...])


def conv_kernel(upper, x_ref, halo_ref, left_ref, right_ref, w1_ref, b1_ref, w2_ref, b2_ref, *refs):
    if upper:
        band_ref, *refs = refs
    else:
        above_ref, out_ref, band_ref, *refs = refs
    wide_ref, x16_ref, first_ref, wc1_ref, wc2_ref = refs
    channels = x_ref.shape[2]
    width = x16_ref.shape[1]
    for a in range(3):
        for b in range(3):
            at = (slice(a * channels, (a + 1) * channels), slice(b * channels, (b + 1) * channels))
            wc1_ref[at] = w1_ref[a, b]
            wc2_ref[at] = w2_ref[a, b]
    body = slice(PAD, PAD + TC)
    start = 0 if upper else SR - PH
    outer_rows, inner_rows = (slice(0, EDGE), slice(EDGE, None)) if upper else (slice(PH + EDGE, None), slice(0, PH + EDGE))
    wide_ref[...] = jnp.zeros(wide_ref.shape, F32)
    wide_ref[outer_rows, body] = halo_ref[...].astype(F32)
    inner = x_ref[0 : PH + EDGE] if upper else x_ref[SR - PH - EDGE :]
    wide_ref[inner_rows, body] = inner.astype(F32)
    sides = slice(start, start + PH + 2 * EDGE)
    wide_ref[:, PAD - EDGE : PAD] = left_ref[sides].astype(F32)
    wide_ref[:, PAD + TC : PAD + TC + EDGE] = right_ref[sides].astype(F32)
    x16_ref[...] = wide_ref[...].astype(BF16)

    def taps(source, first, count, weights):
        rows = [source[first + a : first + a + count].reshape(count * width, channels) for a in range(3)]
        all_taps = jnp.dot(jnp.concatenate(rows, axis=1), weights[...], preferred_element_type=F32)
        return (
            pltpu.roll(all_taps[:, :channels], 1, 0)
            + all_taps[:, channels : 2 * channels]
            + pltpu.roll(all_taps[:, 2 * channels :], count * width - 1, 0)
        )

    at_row, at_col = lax.axis_index(("orbits", "rows")), lax.axis_index("cols")
    col = lax.broadcasted_iota(jnp.int32, (width, channels), 0)
    first_col = jnp.where(at_col > 0, PAD - 1, PAD)
    last_col = jnp.where(at_col < lax.axis_size("cols") - 1, PAD + TC, PAD + TC - 1)
    inside = (col >= first_col) & (col <= last_col)
    if upper:
        edge, has_edge = 0, at_row > 0
    else:
        edge, has_edge = PH + 1, at_row < lax.axis_size(("orbits", "rows")) - 1
    count = (PH + 2) // 2
    for i in range(2):
        value = silu(taps(x16_ref, i * count, count, wc1_ref) + b1_ref[...])
        for r in range(count):
            row = i * count + r
            keep = inside & has_edge if row == edge else inside
            first_ref[row] = jnp.where(keep, value[r * width : (r + 1) * width], 0.0).astype(BF16)
    values = taps(first_ref, 0, PH, wc2_ref) + b2_ref[...]
    for r in range(PH):
        value = values[r * width + PAD : r * width + PAD + TC] + x_ref[start + r].astype(F32)
        band_ref[r] = value.astype(BF16)
        if not upper:
            out_ref[start + r] = value.astype(BF16)
    if not upper:
        out_ref[:start] = above_ref[...]


def arrives_last(orbits, patch):
    band = patch // ACROSS
    stripe = band // BANDS
    return jnp.where(
        lax.rem(band, BANDS) == 0, stripe == stripe_at(0, -1), stripe == stripe_at(0, 1)
    )


def read_kernel(orbits, most, last, patch_ref, weights_ref, *refs):
    if last:
        up_ref, down_ref, before_ref, out_ref, grid_ref, list_ref = refs
        out_ref[...] = before_ref[...]
        grid_ref[0:PH], grid_ref[PH : 2 * PH] = up_ref[...], down_ref[...]
    else:
        count = orbits - 1
        up, down, (out_ref, grid_ref, list_ref) = refs[:count], refs[count : 2 * count], refs[2 * count :]
        for k in range(count):
            for piece_ref, way, band in ((up[k], 1, 0), (down[k], -1, 1)):
                grid_ref[pl.ds(stripe_at(orbits - 1 - k, -way) * SR + band * PH, PH)] = piece_ref[...]
        out_ref[...] = jnp.zeros(out_ref.shape, BF16)
    size = out_ref.shape[2]
    count = choose(list_ref, patch_ref, lambda patch: arrives_last(orbits, patch) == last)

    def read(slot):
        patch = jnp.maximum(patch_ref[slot], 0)
        at_row, at_col = place(lax.rem(patch, BANDS * ACROSS) if last else patch)
        values = grid_ref[at_row, at_col, :].reshape(PH * PW, grid_ref.shape[2])
        result = jnp.dot(weights_ref[slot], values, preferred_element_type=F32)
        at = pl.ds(pl.multiple_of(lax.rem(slot, most) * size, size), size)
        out_ref[slot // most, at, :] = result.astype(BF16)

    for_chosen(list_ref, count, list_ref[jnp.maximum(count - 1, 0)], read)


def final_kernel(tile_ref, feat_ref, got_ref, out_hbm, out_ref, count_ref, sems):
    blocks, size, _ = feat_ref.shape
    chunks = sems.shape[0]
    per = blocks // chunks
    clear(count_ref)

    def give(c):
        at = pl.ds(c * per, per)
        return pltpu.make_async_copy(out_ref.at[at], out_hbm.at[at], sems.at[c])

    def chunk(c, unused):
        for k in range(per):
            b = c * per + k
            t, n = next_slot(tile_ref, count_ref, b)
            mine = got_ref[t, pl.ds(pl.multiple_of(n * size, size), size), :]
            out_ref[b] = (feat_ref[b].astype(F32) + mine.astype(F32)).astype(BF16)
        give(c).start()
        return unused

    lax.fori_loop(0, chunks, chunk, 0)
    for c in range(chunks):
        give(c).wait()


def shifts(axis):
    size = lax.axis_size(axis)
    up = [(i, i + 1) for i in range(size - 1)]
    return up, [(j, i) for i, j in up]


def halo(first, last, axis):
    up, down = shifts(axis)
    return lax.ppermute(last, axis, up), lax.ppermute(first, axis, down)


def turn(x, way):
    size = lax.axis_size("orbits")
    return lax.ppermute(x, "orbits", [(i, (i + way) % size) for i in range(size)])


def ring_sum(stripes, way):
    total = stripes[0]
    for k in range(1, len(stripes)):
        total = turn(total, way)
        if k < len(stripes) - 1:
            total = total + stripes[k]
    return total


def ring_gather(x, way):
    pieces = [x]
    for _ in range(lax.axis_size("orbits") - 1):
        pieces.append(turn(pieces[-1], way))
    return pieces


def local(
    obs_feat, obs_offset, obs_cells, block_tile, block_patch, w_embed, b_embed, w_proj, b_proj,
    density_weight, w_first, b_first, w_second, b_second,
):
    channels = obs_feat.shape[1]
    blocks = block_tile.shape[0]
    size = obs_feat.shape[0] // blocks
    plane = ("rows", "cols")
    tiles = lax.axis_size(plane)
    orbits = lax.axis_size("orbits")
    most = max(2, 2 * blocks // tiles)
    slots = tiles * most
    height = orbits * SR
    patches = height // PH * ACROSS
    length = most * size
    meta_rows = max(16, most * META)
    chunks = blocks // 8
    counts = pltpu.SMEM((tiles,), jnp.int32)
    shape = jax.ShapeDtypeStruct
    bias = lambda b: b.reshape(1, channels)
    exchange = lambda x: lax.all_to_all(x, plane, split_axis=0, concat_axis=0, tiled=True)
    vmem = lambda a: pltpu.VMEM(a.shape, a.dtype)

    b_embed, b_proj = bias(b_embed), bias(b_proj)
    features, send = call(
        embed_kernel,
        [HBM] * 9,
        [HBM] * 2,
        (shape((blocks, size, channels), BF16), shape((tiles, length + meta_rows, channels), BF16)),
        [
            pltpu.SMEM((blocks,), jnp.int32),
            pltpu.SMEM((blocks,), jnp.int32),
            vmem(obs_offset),
            pltpu.VMEM((8, obs_cells.shape[1]), jnp.int32),
            vmem(obs_feat),
            vmem(w_embed),
            vmem(b_embed),
            vmem(w_proj),
            vmem(b_proj),
            pltpu.VMEM((blocks, size, channels), BF16),
            pltpu.VMEM((size, channels), BF16),
            counts,
            pltpu.SMEM((blocks,), jnp.int32),
            pltpu.VMEM((slots * META, size), F32),
            pltpu.VMEM((tiles, meta_rows, size), BF16),
            pltpu.SemaphoreType.DMA((9,)),
            pltpu.SemaphoreType.DMA((chunks,)),
            pltpu.SemaphoreType.DMA((chunks,)),
            pltpu.SemaphoreType.DMA((slots,)),
        ],
        6 * obs_feat.size * channels,
        8 * obs_feat.size,
        block_tile, block_patch, obs_offset, obs_cells, obs_feat, w_embed, b_embed, w_proj, b_proj,
        limit=LARGE,
    )
    got = exchange(send)

    flops = 2 * slots * size * channels * PH * PW
    early_shape = shape((FULL + SR + CELLS, channels), BF16)
    late_shape = shape((len(LATE) * TC, channels), BF16)
    steps = orbits // 2
    spread_shapes = [early_shape, late_shape] * steps
    spread_scratch = [
        pltpu.VMEM((steps * SR, TC, channels), F32),
        pltpu.VMEM((patches, PH, PW), F32),
        pltpu.VMEM((slots * META + 8, size), F32),
        pltpu.SMEM((slots + GROUP,), jnp.int32),
    ]
    *leading, patch_of = call(
        functools.partial(spread_kernel, orbits, most, True),
        [VMEM],
        [VMEM] * (2 * steps) + [SMEM],
        spread_shapes + [shape((slots,), jnp.int32)],
        spread_scratch,
        flops // 2,
        4 * slots * size * channels,
        got,
    )
    others = call(
        functools.partial(spread_kernel, orbits, most, False),
        [SMEM, VMEM],
        [VMEM] * (2 * steps),
        spread_shapes,
        spread_scratch,
        flops // 2,
        4 * slots * size * channels,
        patch_of, got,
    )
    bands0 = [a for pair in zip(leading[0::2], others[0::2]) for a in pair]
    bands1 = [a for pair in zip(leading[1::2], others[1::2]) for a in pair]
    sum0, sum1 = ring_sum(bands0, 1), ring_sum(bands1, -1)
    weights = call(
        functools.partial(weights_kernel, most),
        [VMEM],
        VMEM,
        shape((slots, size, PH * PW), BF16),
        [],
        flops,
        4 * slots * size * channels,
        got,
    )
    density_weight = bias(density_weight)
    rows_shape, cols_shape = shape((EDGE, TC, channels), BF16), shape((SR, EDGE, channels), BF16)
    top, bottom, left, right = call(
        edge_kernel,
        [VMEM] * 3,
        [VMEM] * 4,
        [rows_shape] * 2 + [cols_shape] * 2,
        [],
        10000000,
        4 * SR * TC * channels,
        bands0[-1], sum0, density_weight,
    )
    above, below = halo(top, bottom, ("orbits", "rows"))
    left = jnp.concatenate([above[:, :EDGE], left, below[:, :EDGE]], axis=0)
    right = jnp.concatenate([above[:, TC - EDGE :], right, below[:, TC - EDGE :]], axis=0)
    left, right = halo(left, right, "cols")
    grid_in = call(
        grid_kernel,
        [VMEM] * 5,
        VMEM,
        shape((SR, TC, channels), BF16),
        [],
        10000000,
        8 * SR * TC * channels,
        bands0[-1], sum0, bands1[-1], sum1, density_weight,
    )

    width = TC + 2 * PAD
    conv_args = (w_first, bias(b_first), w_second, bias(b_second))
    conv_scratch = [
        pltpu.VMEM((PH + 4, width, channels), F32),
        pltpu.VMEM((PH + 4, width, channels), BF16),
        pltpu.VMEM((PH + 2, width, channels), BF16),
        pltpu.VMEM((3 * channels, 3 * channels), BF16),
        pltpu.VMEM((3 * channels, 3 * channels), BF16),
    ]
    conv_flops = 2 * 9 * SR * TC * channels * channels
    band_shape = shape((PH, TC, channels), BF16)
    band0 = call(
        functools.partial(conv_kernel, True),
        [VMEM] * 8,
        VMEM,
        band_shape,
        conv_scratch,
        conv_flops,
        4 * grid_in.size,
        grid_in, above, left, right, *conv_args,
    )
    grid_out, band1 = call(
        functools.partial(conv_kernel, False),
        [VMEM] * 9,
        [VMEM] * 2,
        (shape((SR, TC, channels), BF16), band_shape),
        conv_scratch,
        conv_flops,
        4 * grid_in.size,
        grid_in, below, left, right, *conv_args, band0,
    )

    up, down = ring_gather(band0, 1), ring_gather(band1, -1)
    read_shape = shape((tiles, length, channels), BF16)
    slot_list = pltpu.SMEM((slots + GROUP,), jnp.int32)
    readings = call(
        functools.partial(read_kernel, orbits, most, False),
        [SMEM, VMEM] + [VMEM] * (2 * orbits - 2),
        VMEM,
        read_shape,
        [pltpu.VMEM((height, TC, channels), BF16), slot_list],
        flops,
        8 * slots * size * channels,
        patch_of, weights, *up[:-1], *down[:-1],
    )
    readings = call(
        functools.partial(read_kernel, orbits, most, True),
        [SMEM, VMEM, VMEM, VMEM, VMEM],
        VMEM,
        read_shape,
        [pltpu.VMEM((2 * PH, TC, channels), BF16), slot_list],
        flops // 4,
        2 * slots * size * channels,
        patch_of, weights, up[-1], down[-1], readings,
    )
    back = exchange(readings)
    obs_out = call(
        final_kernel,
        [SMEM] + [VMEM] * 2,
        HBM,
        shape((blocks, size, channels), BF16),
        [pltpu.VMEM((blocks, size, channels), BF16), counts, pltpu.SemaphoreType.DMA((chunks,))],
        1000000,
        8 * obs_feat.size,
        block_tile, features, back,
    )
    return obs_out.reshape(obs_feat.shape), grid_out


def solution(mesh):
    spread_out = ("orbits", "rows", "cols")
    in_specs = (
        P(spread_out, None),
        P(None, spread_out),
        P(None, spread_out),
        P(spread_out),
        P(spread_out),
    ) + (P(),) * 9
    out_specs = (P(spread_out, None), P(("orbits", "rows"), "cols", None))
    return jax.shard_map(local, mesh=mesh, in_specs=in_specs, out_specs=out_specs, check_vma=False)
```

```python
import functools

import jax
import jax.numpy as jnp
from jax import lax
from jax.experimental import pallas as pl
from jax.experimental.pallas import tpu as pltpu
from jax.sharding import PartitionSpec as P

KN = 16
PH = 8
PW = 32
SR = 16
TC = 128
SIDE = 4
PAD = 8
META = 4
BANDS = SR // PH
GROUP = 8
EDGE = 2
EARLY = (0, 1, SR - 2, SR - 1, 2, 3, 4)
LATE = tuple(r for r in range(SR) if r not in EARLY)
FULL = len(EARLY) * TC
CELLS = -(-len(LATE) * 2 * EDGE // 16) * 16
ACROSS = TC // PW
F32 = jnp.float32
BF16 = jnp.bfloat16

VMEM = pl.BlockSpec(memory_space=pltpu.VMEM)
SMEM = pl.BlockSpec(memory_space=pltpu.SMEM)
HBM = pl.BlockSpec(memory_space=pltpu.HBM)
LIMIT = 20 * 1024 * 1024
LARGE = 56 * 1024 * 1024


def call(kernel, in_specs, out_specs, out_shape, scratch, flops, moved, *args, limit=LIMIT, aliases={}):
    return pl.pallas_call(
        kernel,
        in_specs=in_specs,
        out_specs=out_specs,
        out_shape=out_shape,
        scratch_shapes=scratch,
        input_output_aliases=aliases,
        compiler_params=pltpu.CompilerParams(vmem_limit_bytes=limit),
        cost_estimate=pl.CostEstimate(flops=flops, bytes_accessed=moved, transcendentals=0),
    )(*args)


def silu(v):
    half = 0.5 * v
    return half + half * jnp.tanh(half)


def next_slot(tile_ref, count_ref, b):
    t = tile_ref[b]
    n = count_ref[t]
    count_ref[t] = n + 1
    return t, n


def clear(count_ref):
    for t in range(count_ref.shape[0]):
        count_ref[t] = 0


def embed_kernel(
    tile_hbm, patch_hbm, offset_hbm, cells_hbm, x_hbm, we_hbm, be_hbm, wp_hbm, bp_hbm,
    feat_hbm, send_hbm,
    tile_ref, patch_ref, offset_ref, cells_ref, x_ref, we_ref, be_ref, wp_ref, bp_ref, feat_ref,
    zero_ref, count_ref, slot_ref, meta_ref, meta16_ref, sems, x_sems, feat_sems, send_sems,
):
    blocks, size, channels = feat_ref.shape
    chunks = x_sems.shape[0]
    per = blocks // chunks
    tiles, meta_rows = meta16_ref.shape[0], meta_ref.shape[0] // meta16_ref.shape[0]
    most = meta_rows // META
    base = most * size
    pairs = (
        (tile_hbm, tile_ref), (patch_hbm, patch_ref), (offset_hbm, offset_ref), (cells_hbm.at[0:8], cells_ref),
        (we_hbm, we_ref), (be_hbm, be_ref), (wp_hbm, wp_ref), (bp_hbm, bp_ref),
    )
    copies = [pltpu.make_async_copy(a, b, sems.at[i]) for i, (a, b) in enumerate(pairs)]

    def rows_of(c):
        return pl.ds(pl.multiple_of(c * per * size, per * size), per * size)

    def fetch(c):
        return pltpu.make_async_copy(x_hbm.at[rows_of(c)], x_ref.at[rows_of(c)], x_sems.at[c])

    def keep(c):
        at = pl.ds(c * per, per)
        return pltpu.make_async_copy(feat_ref.at[at], feat_hbm.at[at], feat_sems.at[c])

    def send(source, slot):
        rows = pl.ds(pl.multiple_of(lax.rem(slot, most) * size, size), size)
        return pltpu.make_async_copy(source, send_hbm.at[slot // most, rows], send_sems.at[slot])

    for copy in copies:
        copy.start()
    for c in range(chunks):
        fetch(c).start()
    zero_ref[...] = jnp.zeros(zero_ref.shape, BF16)
    clear(count_ref)
    row = lax.broadcasted_iota(jnp.int32, meta_ref.shape, 0) % META
    meta_ref[...] = jnp.where(row == 2, -65536.0, jnp.where(row == 3, -1.0, 0.0))
    copies[0].wait()
    for b in range(blocks):
        t, n = next_slot(tile_ref, count_ref, b)
        slot_ref[b] = t * most + n
    for t in range(tiles):
        for n in range(most):

            @pl.when(n >= count_ref[t])
            def _():
                send(zero_ref, t * most + n).start()

    for copy in copies[4:]:
        copy.wait()

    def chunk(c, unused):
        fetch(c).wait()
        hidden = silu(jnp.dot(x_ref[rows_of(c), :], we_ref[...], preferred_element_type=F32) + be_ref[...])
        out = jnp.dot(hidden.astype(BF16), wp_ref[...], preferred_element_type=F32) + bp_ref[...]
        feat_ref[pl.ds(c * per, per)] = out.astype(BF16).reshape(per, size, channels)
        keep(c).start()
        for k in range(per):
            b = c * per + k
            send(feat_ref.at[b], slot_ref[b]).start()
        return unused

    lax.fori_loop(0, chunks, chunk, 0)
    for copy in copies[1:4]:
        copy.wait()
    for b in range(blocks):
        first = slot_ref[b] * META
        obs = slice(b * size, (b + 1) * size)
        meta_ref[pl.ds(first, 2), :] = offset_ref[:, obs].astype(F32)
        meta_ref[pl.ds(first + 2, 1), :] = cells_ref[0:1, obs].astype(F32)
        meta_ref[pl.ds(first + 3, 1), :] = jnp.full((1, size), patch_ref[b], jnp.int32).astype(F32)
    extra = meta16_ref.shape[1] - meta_rows
    for t in range(tiles):
        rows = meta_ref[t * meta_rows : (t + 1) * meta_rows, :]
        if extra:
            rows = jnp.concatenate([rows, jnp.zeros((extra, size), F32)], axis=0)
        meta16_ref[t] = rows.astype(BF16)
    described = pltpu.make_async_copy(
        meta16_ref, send_hbm.at[:, pl.ds(base, meta16_ref.shape[1])], sems.at[len(copies)]
    )
    described.start()

    def finish(c, unused):
        keep(c).wait()
        return unused

    lax.fori_loop(0, chunks, finish, 0)
    for slot in range(tiles * most):
        send(zero_ref, slot).wait()
    described.wait()


def factors(meta, normal):
    off_row, off_col, corner = meta[0:1, :], meta[1:2, :], meta[2:3, :]
    first_row = jnp.floor(corner * (1.0 / PW))
    first_col = corner - first_row * PW

    def factor(count, start, off):
        at = lax.broadcasted_iota(jnp.int32, (count, meta.shape[1]), 0).astype(F32) - start
        delta = at - 1.5 - off
        value = jnp.exp(delta * delta * -0.5)
        return jnp.where((at >= 0.0) & (at < SIDE), value, 0.0)

    def total(off):
        at = lax.broadcasted_iota(jnp.int32, (SIDE, meta.shape[1]), 0).astype(F32)
        delta = at - 1.5 - off
        return jnp.sum(jnp.exp(delta * delta * -0.5), axis=0, keepdims=True)

    rows, cols = factor(PH, first_row, off_row), factor(PW, first_col, off_col)
    if normal:
        rows = rows / (total(off_row) * total(off_col))
    return rows, cols


def outer(rows, cols):
    return (rows[:, None, :] * cols[None, :, :]).reshape(PH * PW, rows.shape[1])


def place(patch):
    row, col = patch // ACROSS, lax.rem(patch, ACROSS)
    return pl.ds(pl.multiple_of(row * PH, PH), PH), pl.ds(pl.multiple_of(col * PW, PW), PW)


def stripe_at(k, way):
    orbits = lax.axis_size("orbits")
    return lax.rem(lax.axis_index("orbits") + way * (orbits - 1 - k) + orbits * orbits, orbits)


def spread_kernel(orbits, most, got_ref, *refs):
    up, down, (patch_ref, acc_ref, dens_ref) = refs[:orbits], refs[orbits : 2 * orbits], refs[2 * orbits :]
    size, channels = got_ref.shape[2], acc_ref.shape[2]
    acc_ref[...] = jnp.zeros(acc_ref.shape, F32)
    dens_ref[...] = jnp.zeros(dens_ref.shape, F32)
    base = most * size

    def tile(t, unused):
        metas = got_ref[t, base:, :].astype(F32)
        patches = [jnp.max(metas[n * META + 3 : n * META + 4, :]).astype(jnp.int32) for n in range(most)]
        for n in range(most):
            patch_ref[t * most + n] = patches[n]
            patch = jnp.maximum(patches[n], 0)
            rows, cols = factors(metas[n * META : (n + 1) * META], False)
            values = got_ref[t, n * size : (n + 1) * size, :]
            result = jnp.dot(outer(rows, cols).astype(BF16), values, preferred_element_type=F32)
            at_row, at_col = place(patch)
            acc_ref[at_row, at_col, :] += result.reshape(PH, PW, channels)
            dens_ref[patch] += lax.dot_general(
                rows.astype(BF16), cols.astype(BF16), (((1,), (1,)), ((), ())), preferred_element_type=F32
            )
        return unused

    lax.fori_loop(0, got_ref.shape[0], tile, 0, unroll=4)
    for k in range(orbits):
        for out_ref, way, rows in ((up[k], 1, EARLY), (down[k], -1, LATE)):
            first = stripe_at(k, way) * SR
            for i, r in enumerate(rows):
                out_ref[i * TC : (i + 1) * TC, :] = acc_ref[first + r].astype(BF16)
        first = stripe_at(k, 1) * SR
        bands = []
        for band in range(SR // PH):
            at = (stripe_at(k, 1) * (SR // PH) + band) * ACROSS
            bands.append(jnp.concatenate([dens_ref[at + c] for c in range(ACROSS)], axis=1))
        up[k][FULL : FULL + SR, :] = jnp.concatenate(bands, axis=0).astype(BF16)
        cells = [acc_ref[first + r, at] for r in LATE for at in (slice(0, EDGE), slice(TC - EDGE, TC))]
        spare = CELLS - len(LATE) * 2 * EDGE
        if spare:
            cells.append(jnp.zeros((spare, channels), F32))
        up[k][FULL + SR :, :] = jnp.concatenate(cells, axis=0).astype(BF16)


def weights_kernel(most, got_ref, out_ref):
    base = most * got_ref.shape[2]

    def tile(t, unused):
        metas = got_ref[t, base:, :].astype(F32)
        for n in range(most):
            rows, cols = factors(metas[n * META : (n + 1) * META], True)
            out_ref[t * most + n] = outer(rows, cols).T.astype(BF16)
        return unused

    lax.fori_loop(0, got_ref.shape[0], tile, 0)


def grid_values(spread, density, weight):
    return (spread / jnp.maximum(density, 1.0) + weight * (density / (1.0 + density))).astype(BF16)


def densities(own_ref, sum_ref):
    tail = slice(FULL, FULL + SR)
    columns = (own_ref[tail, :].astype(F32) + sum_ref[tail, :].astype(F32)).T
    return lambda r: jnp.broadcast_to(columns[:, r : r + 1], (TC, own_ref.shape[1]))


def edge_kernel(own_ref, sum_ref, weight_ref, top_ref, bottom_ref, left_ref, right_ref):
    density = densities(own_ref, sum_ref)
    weight = weight_ref[...]
    low, high = slice(0, EDGE), slice(TC - EDGE, TC)
    cells = own_ref[FULL + SR :, :].astype(F32) + sum_ref[FULL + SR :, :].astype(F32)
    for r in range(SR):
        d = density(r)
        if r in EARLY:
            at = slice(EARLY.index(r) * TC, (EARLY.index(r) + 1) * TC)
            spread = own_ref[at, :].astype(F32) + sum_ref[at, :].astype(F32)
            row = grid_values(spread, d, weight)
            if r < EDGE:
                top_ref[r] = row
            if r >= SR - EDGE:
                bottom_ref[r - (SR - EDGE)] = row
            left_ref[r], right_ref[r] = row[low], row[high]
        else:
            at = LATE.index(r) * 2 * EDGE
            left_ref[r] = grid_values(cells[at : at + EDGE], d[low], weight)
            right_ref[r] = grid_values(cells[at + EDGE : at + 2 * EDGE], d[high], weight)


def conv_kernel(
    own0_ref, sum0_ref, own1_ref, sum1_ref, weight_ref, up_ref, down_ref, left_ref, right_ref,
    w1_ref, b1_ref, w2_ref, b2_ref,
    out_ref, out0_ref, out1_ref, wide_ref, x16_ref, first_ref, wc1_ref, wc2_ref,
):
    channels = out_ref.shape[2]
    width = x16_ref.shape[1]
    for a in range(3):
        for b in range(3):
            at = (slice(a * channels, (a + 1) * channels), slice(b * channels, (b + 1) * channels))
            if a == 2 and b == 2:
                at = (slice(channels, 2 * channels), slice(3 * channels, None))
            wc1_ref[at] = w1_ref[a, b]
            wc2_ref[at] = w2_ref[a, b]
    spare = (slice(0, channels), slice(3 * channels, None))
    wc1_ref[spare] = jnp.zeros((channels, channels), BF16)
    wc2_ref[spare] = jnp.zeros((channels, channels), BF16)
    body = slice(PAD, PAD + TC)
    wide_ref[:, :PAD] = jnp.zeros((wide_ref.shape[0], PAD, channels), F32)
    wide_ref[:, PAD + TC :] = jnp.zeros((wide_ref.shape[0], PAD, channels), F32)
    density = densities(own0_ref, sum0_ref)
    for own_ref, sum_ref, rows in ((own0_ref, sum0_ref, EARLY), (own1_ref, sum1_ref, LATE)):
        for i, r in enumerate(rows):
            at = slice(i * TC, (i + 1) * TC)
            spread = own_ref[at, :].astype(F32) + sum_ref[at, :].astype(F32)
            wide_ref[EDGE + r, body] = grid_values(spread, density(r), weight_ref[...]).astype(F32)
    wide_ref[0:EDGE, body] = up_ref[...].astype(F32)
    wide_ref[EDGE + SR :, body] = down_ref[...].astype(F32)
    wide_ref[:, PAD - EDGE : PAD] = left_ref[...].astype(F32)
    wide_ref[:, PAD + TC : PAD + TC + EDGE] = right_ref[...].astype(F32)
    x16_ref[...] = wide_ref[...].astype(BF16)

    def taps(source, first, count, weights):
        rows = [source[pl.ds(first + a, count)].reshape(count * width, channels) for a in range(3)]
        near = jnp.dot(jnp.concatenate(rows, axis=1), weights[:, : 2 * channels], preferred_element_type=F32)
        more = [source[pl.ds(first + a, count + 1)].reshape((count + 1) * width, channels) for a in range(2)]
        far = jnp.dot(
            jnp.concatenate(more, axis=1), weights[: 2 * channels, 2 * channels :], preferred_element_type=F32
        )
        right = far[: count * width, :channels] + far[width:, channels:]
        return (
            pltpu.roll(near[:, :channels], 1, 0)
            + near[:, channels:]
            + pltpu.roll(right, count * width - 1, 0)
        )

    at_row, at_col = lax.axis_index(("orbits", "rows")), lax.axis_index("cols")
    col = lax.broadcasted_iota(jnp.int32, (width, channels), 0)
    first_col = jnp.where(at_col > 0, PAD - 1, PAD)
    last_col = jnp.where(at_col < lax.axis_size("cols") - 1, PAD + TC, PAD + TC - 1)
    inside = (col >= first_col) & (col <= last_col)
    first_row = jnp.where(at_row > 0, 0, 1)
    last_row = jnp.where(at_row < lax.axis_size(("orbits", "rows")) - 1, SR + 1, SR)
    count = (SR + 2) // 2

    def first_rows(i, unused):
        value = silu(taps(x16_ref, i * count, count, wc1_ref) + b1_ref[...])
        for r in range(count):
            row = i * count + r
            keep = inside & (row >= first_row) & (row <= last_row)
            first_ref[row] = jnp.where(keep, value[r * width : (r + 1) * width], 0.0).astype(BF16)
        return unused

    lax.fori_loop(0, 2, first_rows, 0)
    again = PH

    def second_rows(i, band_ref):
        values = taps(first_ref, i * again, again, wc2_ref) + b2_ref[...]
        for r in range(again):
            row = i * again + r
            value = values[r * width + PAD : r * width + PAD + TC] + wide_ref[row + EDGE, body]
            out_ref[row] = value.astype(BF16)
            band_ref[r] = value.astype(BF16)

    second_rows(0, out0_ref)
    second_rows(1, out1_ref)


def arrives_last(patch):
    band = patch // ACROSS
    stripe = band // BANDS
    return jnp.where(lax.rem(band, BANDS) == 0, stripe == stripe_at(0, -1), stripe == stripe_at(0, 1))


def read_slot(grid_ref, weights_ref, slot, patch):
    at_row, at_col = place(jnp.maximum(patch, 0))
    values = grid_ref[at_row, at_col, :].reshape(PH * PW, grid_ref.shape[2])
    return jnp.dot(weights_ref[slot], values, preferred_element_type=F32).astype(BF16)


def read_kernel(orbits, most, patch_ref, weights_ref, *refs):
    count = orbits - 1
    up, down, (out_ref, list_ref, grid_ref) = refs[:count], refs[count : 2 * count], refs[2 * count :]
    size, slots = out_ref.shape[2], patch_ref.shape[0]
    grid_ref[...] = jnp.zeros(grid_ref.shape, BF16)
    for k in range(count):
        for piece_ref, way, band in ((up[k], 1, 0), (down[k], -1, 1)):
            grid_ref[pl.ds(stripe_at(orbits - 1 - k, -way) * SR + band * PH, PH)] = piece_ref[...]

    def tile(t, unused):
        for n in range(most):
            slot = t * most + n
            out_ref[t, n * size : (n + 1) * size, :] = read_slot(grid_ref, weights_ref, slot, patch_ref[slot])
        return unused

    lax.fori_loop(0, out_ref.shape[0], tile, 0)

    def look(slot, late):
        list_ref[late] = slot
        patch = patch_ref[slot]
        return late + jnp.where((patch >= 0) & arrives_last(jnp.maximum(patch, 0)), 1, 0)

    late = lax.fori_loop(0, slots, look, 0, unroll=8)
    for j in range(GROUP):
        list_ref[late + j] = 0
    list_ref[slots + GROUP] = late


def late_kernel(most, patch_ref, list_ref, weights_ref, up_ref, down_ref, _, out_hbm, grid_ref, result_ref, sems):
    size, slots = result_ref.shape[1], patch_ref.shape[0]
    grid_ref[0:PH], grid_ref[PH:] = up_ref[...], down_ref[...]
    late = list_ref[slots + GROUP]

    def give(i):
        slot = list_ref[i]
        rows = pl.ds(pl.multiple_of(lax.rem(slot, most) * size, size), size)
        return pltpu.make_async_copy(result_ref.at[i], out_hbm.at[slot // most, rows], sems.at[i])

    def some(c, unused):
        for j in range(GROUP):
            i = c * GROUP + j
            slot = list_ref[i]
            patch = lax.rem(jnp.maximum(patch_ref[slot], 0), BANDS * ACROSS)
            result_ref[i] = read_slot(grid_ref, weights_ref, slot, patch)
        for j in range(GROUP):
            i = c * GROUP + j

            @pl.when(i < late)
            def _():
                give(i).start()

        return unused

    def finish(i, unused):
        give(i).wait()
        return unused

    lax.fori_loop(0, (late + GROUP - 1) // GROUP, some, 0)
    lax.fori_loop(0, late, finish, 0)


def final_kernel(tile_ref, feat_ref, got_ref, out_hbm, out_ref, count_ref, sems):
    blocks, size, _ = feat_ref.shape
    chunks = sems.shape[0]
    per = blocks // chunks
    clear(count_ref)

    def give(c):
        at = pl.ds(c * per, per)
        return pltpu.make_async_copy(out_ref.at[at], out_hbm.at[at], sems.at[c])

    def chunk(c, unused):
        for k in range(per):
            b = c * per + k
            t, n = next_slot(tile_ref, count_ref, b)
            mine = got_ref[t, pl.ds(pl.multiple_of(n * size, size), size), :]
            out_ref[b] = (feat_ref[b].astype(F32) + mine.astype(F32)).astype(BF16)
        give(c).start()
        return unused

    lax.fori_loop(0, chunks, chunk, 0)
    for c in range(chunks):
        give(c).wait()


def shifts(axis):
    size = lax.axis_size(axis)
    up = [(i, i + 1) for i in range(size - 1)]
    return up, [(j, i) for i, j in up]


def halo(first, last, axis):
    up, down = shifts(axis)
    return lax.ppermute(last, axis, up), lax.ppermute(first, axis, down)


def turn(x, way):
    size = lax.axis_size("orbits")
    return lax.ppermute(x, "orbits", [(i, (i + way) % size) for i in range(size)])


TIES = {2: 1}


def ring_sums(leading, following):
    orbits = len(leading)
    first, second = leading[0], following[0]
    done = 0

    def step(total, stripes, k, way):
        total = turn(total, way)
        return total + stripes[k] if k < orbits - 1 else total

    for k in range(1, orbits):
        first = step(first, leading, k, 1)
        while done < TIES.get(k, 0):
            done += 1
            second = step(second, following, done, -1)
        if k in TIES:
            first, second = lax.optimization_barrier((first, second))
    while done < orbits - 1:
        done += 1
        second = step(second, following, done, -1)
    return first, second


def ring_gather(x, way):
    pieces = [x]
    for _ in range(lax.axis_size("orbits") - 1):
        pieces.append(turn(pieces[-1], way))
    return pieces


def local(
    obs_feat, obs_offset, obs_cells, block_tile, block_patch, w_embed, b_embed, w_proj, b_proj,
    density_weight, w_first, b_first, w_second, b_second,
):
    channels = obs_feat.shape[1]
    blocks = block_tile.shape[0]
    size = obs_feat.shape[0] // blocks
    plane = ("rows", "cols")
    tiles = lax.axis_size(plane)
    orbits = lax.axis_size("orbits")
    most = max(2, 2 * blocks // tiles)
    slots = tiles * most
    height = orbits * SR
    patches = height // PH * ACROSS
    length = most * size
    meta_rows = max(16, most * META)
    chunks = blocks // 8
    counts = pltpu.SMEM((tiles,), jnp.int32)
    shape = jax.ShapeDtypeStruct
    bias = lambda b: b.reshape(1, channels)
    exchange = lambda x: lax.all_to_all(x, plane, split_axis=0, concat_axis=0, tiled=True)
    vmem = lambda a: pltpu.VMEM(a.shape, a.dtype)

    b_embed, b_proj = bias(b_embed), bias(b_proj)
    features, send = call(
        embed_kernel,
        [HBM] * 9,
        [HBM] * 2,
        (shape((blocks, size, channels), BF16), shape((tiles, length + meta_rows, channels), BF16)),
        [
            pltpu.SMEM((blocks,), jnp.int32),
            pltpu.SMEM((blocks,), jnp.int32),
            vmem(obs_offset),
            pltpu.VMEM((8, obs_cells.shape[1]), jnp.int32),
            vmem(obs_feat),
            vmem(w_embed),
            vmem(b_embed),
            vmem(w_proj),
            vmem(b_proj),
            pltpu.VMEM((blocks, size, channels), BF16),
            pltpu.VMEM((size, channels), BF16),
            counts,
            pltpu.SMEM((blocks,), jnp.int32),
            pltpu.VMEM((slots * META, size), F32),
            pltpu.VMEM((tiles, meta_rows, size), BF16),
            pltpu.SemaphoreType.DMA((9,)),
            pltpu.SemaphoreType.DMA((chunks,)),
            pltpu.SemaphoreType.DMA((chunks,)),
            pltpu.SemaphoreType.DMA((slots,)),
        ],
        6 * obs_feat.size * channels,
        8 * obs_feat.size,
        block_tile, block_patch, obs_offset, obs_cells, obs_feat, w_embed, b_embed, w_proj, b_proj,
        limit=LARGE,
    )
    got = exchange(send)

    flops = 2 * slots * size * channels * PH * PW
    early_shape = shape((FULL + SR + CELLS, channels), BF16)
    late_shape = shape((len(LATE) * TC, channels), BF16)
    *bands, patch_of = call(
        functools.partial(spread_kernel, orbits, most),
        [VMEM],
        [VMEM] * (2 * orbits) + [SMEM],
        [early_shape] * orbits + [late_shape] * orbits + [shape((slots,), jnp.int32)],
        [pltpu.VMEM((height, TC, channels), F32), pltpu.VMEM((patches, PH, PW), F32)],
        flops,
        8 * slots * size * channels,
        got,
    )
    bands0, bands1 = bands[:orbits], bands[orbits:]
    sum0, sum1 = ring_sums(bands0, bands1)
    weights = call(
        functools.partial(weights_kernel, most),
        [VMEM],
        VMEM,
        shape((slots, size, PH * PW), BF16),
        [],
        flops,
        4 * slots * size * channels,
        got,
    )
    density_weight = bias(density_weight)
    rows_shape, cols_shape = shape((EDGE, TC, channels), BF16), shape((SR, EDGE, channels), BF16)
    top, bottom, left, right = call(
        edge_kernel,
        [VMEM] * 3,
        [VMEM] * 4,
        [rows_shape] * 2 + [cols_shape] * 2,
        [],
        10000000,
        4 * SR * TC * channels,
        bands0[-1], sum0, density_weight,
    )
    above, below = halo(top, bottom, ("orbits", "rows"))
    left = jnp.concatenate([above[:, :EDGE], left, below[:, :EDGE]], axis=0)
    right = jnp.concatenate([above[:, TC - EDGE :], right, below[:, TC - EDGE :]], axis=0)
    left, right = halo(left, right, "cols")
    sum1, weights = lax.optimization_barrier((sum1, weights))
    width = TC + 2 * PAD
    grid_out, band0, band1 = call(
        conv_kernel,
        [VMEM] * 13,
        [VMEM] * 3,
        [shape((SR, TC, channels), BF16)] + [shape((PH, TC, channels), BF16)] * 2,
        [
            pltpu.VMEM((SR + 4, width, channels), F32),
            pltpu.VMEM((SR + 4, width, channels), BF16),
            pltpu.VMEM((SR + 2, width, channels), BF16),
            pltpu.VMEM((3 * channels, 4 * channels), BF16),
            pltpu.VMEM((3 * channels, 4 * channels), BF16),
        ],
        4 * 9 * SR * TC * channels * channels,
        8 * SR * TC * channels,
        bands0[-1], sum0, bands1[-1], sum1, density_weight, above, below, left, right, w_first, bias(b_first), w_second, bias(b_second),
    )

    up, down = ring_gather(band0, 1), ring_gather(band1, -1)
    read_shape = shape((tiles, length, channels), BF16)
    readings, late = call(
        functools.partial(read_kernel, orbits, most),
        [SMEM] + [VMEM] * (2 * orbits - 1),
        [VMEM, SMEM],
        (read_shape, shape((slots + GROUP + 1,), jnp.int32)),
        [pltpu.VMEM((height, TC, channels), BF16)],
        flops,
        8 * slots * size * channels,
        patch_of, weights, *up[:-1], *down[:-1],
    )
    readings = call(
        functools.partial(late_kernel, most),
        [SMEM] * 2 + [VMEM] * 3 + [HBM],
        HBM,
        read_shape,
        [
            pltpu.VMEM((BANDS * PH, TC, channels), BF16),
            pltpu.VMEM((slots + GROUP, size, channels), BF16),
            pltpu.SemaphoreType.DMA((slots + GROUP,)),
        ],
        flops // 4,
        2 * slots * size * channels,
        patch_of, late, weights, up[-1], down[-1], readings,
        aliases={5: 0},
    )
    back = exchange(readings)
    obs_out = call(
        final_kernel,
        [SMEM] + [VMEM] * 2,
        HBM,
        shape((blocks, size, channels), BF16),
        [pltpu.VMEM((blocks, size, channels), BF16), counts, pltpu.SemaphoreType.DMA((chunks,))],
        1000000,
        8 * obs_feat.size,
        block_tile, features, back,
    )
    return obs_out.reshape(obs_feat.shape), grid_out


def solution(mesh):
    spread_out = ("orbits", "rows", "cols")
    in_specs = (
        P(spread_out, None),
        P(None, spread_out),
        P(None, spread_out),
        P(spread_out),
        P(spread_out),
    ) + (P(),) * 9
    out_specs = (P(spread_out, None), P(("orbits", "rows"), "cols", None))
    return jax.shard_map(local, mesh=mesh, in_specs=in_specs, out_specs=out_specs, check_vma=False)
```

```python
import functools

import jax
import jax.numpy as jnp
from jax import lax
from jax.experimental import pallas as pl
from jax.experimental.pallas import tpu as pltpu
from jax.sharding import PartitionSpec as P

KN = 16
PH = 8
PW = 32
SR = 16
TC = 128
SIDE = 4
PAD = 8
META = 4
BANDS = SR // PH
GROUP = 8
EDGE = 2
EARLY = (0, 1, SR - 2, SR - 1, 2, 3, 4)
LATE = tuple(r for r in range(SR) if r not in EARLY)
FULL = len(EARLY) * TC
CELLS = -(-len(LATE) * 2 * EDGE // 16) * 16
ACROSS = TC // PW
F32 = jnp.float32
BF16 = jnp.bfloat16

VMEM = pl.BlockSpec(memory_space=pltpu.VMEM)
SMEM = pl.BlockSpec(memory_space=pltpu.SMEM)
HBM = pl.BlockSpec(memory_space=pltpu.HBM)
LIMIT = 20 * 1024 * 1024
LARGE = 56 * 1024 * 1024


def call(kernel, in_specs, out_specs, out_shape, scratch, flops, moved, *args, limit=LIMIT, aliases={}):
    return pl.pallas_call(
        kernel,
        in_specs=in_specs,
        out_specs=out_specs,
        out_shape=out_shape,
        scratch_shapes=scratch,
        input_output_aliases=aliases,
        compiler_params=pltpu.CompilerParams(vmem_limit_bytes=limit),
        cost_estimate=pl.CostEstimate(flops=flops, bytes_accessed=moved, transcendentals=0),
    )(*args)


def silu(v):
    half = 0.5 * v
    return half + half * jnp.tanh(half)


def next_slot(tile_ref, count_ref, b):
    t = tile_ref[b]
    n = count_ref[t]
    count_ref[t] = n + 1
    return t, n


def clear(count_ref):
    for t in range(count_ref.shape[0]):
        count_ref[t] = 0


def embed_kernel(
    most, tile_hbm, patch_hbm, offset_hbm, cells_hbm, x_hbm, we_hbm, be_hbm, wp_hbm, bp_hbm,
    feat_hbm, send_hbm,
    tile_ref, patch_ref, offset_ref, cells_ref, x_ref, we_ref, be_ref, wp_ref, bp_ref, feat_ref,
    zero_ref, count_ref, slot_ref, meta_ref, meta16_ref, sems, x_sems, feat_sems, send_sems,
):
    blocks, size, channels = feat_ref.shape
    chunks = x_sems.shape[0]
    per = blocks // chunks
    tiles, meta_rows, base = meta16_ref.shape[0], most * META, most * size
    pairs = (
        (tile_hbm, tile_ref), (patch_hbm, patch_ref), (offset_hbm, offset_ref), (cells_hbm.at[0:8], cells_ref),
        (we_hbm, we_ref), (be_hbm, be_ref), (wp_hbm, wp_ref), (bp_hbm, bp_ref),
    )
    copies = [pltpu.make_async_copy(a, b, sems.at[i]) for i, (a, b) in enumerate(pairs)]

    def rows_of(c):
        return pl.ds(pl.multiple_of(c * per * size, per * size), per * size)

    def fetch(c):
        return pltpu.make_async_copy(x_hbm.at[rows_of(c)], x_ref.at[rows_of(c)], x_sems.at[c])

    def keep(c):
        at = pl.ds(c * per, per)
        return pltpu.make_async_copy(feat_ref.at[at], feat_hbm.at[at], feat_sems.at[c])

    def send(source, slot):
        rows = pl.ds(pl.multiple_of(lax.rem(slot, most) * size, size), size)
        return pltpu.make_async_copy(source, send_hbm.at[slot // most, rows], send_sems.at[slot])

    for copy in copies:
        copy.start()
    for c in range(chunks):
        fetch(c).start()
    zero_ref[...] = jnp.zeros(zero_ref.shape, BF16)
    clear(count_ref)
    row = lax.broadcasted_iota(jnp.int32, meta_ref.shape, 0) % META
    meta_ref[...] = jnp.where(row == 2, -65536.0, jnp.where(row == 3, -1.0, 0.0))
    copies[0].wait()
    for b in range(blocks):
        t, n = next_slot(tile_ref, count_ref, b)
        slot_ref[b] = t * most + n
    for t in range(tiles):
        for n in range(most):

            @pl.when(n >= count_ref[t])
            def _():
                send(zero_ref, t * most + n).start()

    for copy in copies[4:]:
        copy.wait()

    def chunk(c, unused):
        fetch(c).wait()
        hidden = silu(jnp.dot(x_ref[rows_of(c), :], we_ref[...], preferred_element_type=F32) + be_ref[...])
        out = jnp.dot(hidden.astype(BF16), wp_ref[...], preferred_element_type=F32) + bp_ref[...]
        feat_ref[pl.ds(c * per, per)] = out.astype(BF16).reshape(per, size, channels)
        keep(c).start()
        for k in range(per):
            b = c * per + k
            send(feat_ref.at[b], slot_ref[b]).start()
        return unused

    lax.fori_loop(0, chunks, chunk, 0)
    for copy in copies[1:4]:
        copy.wait()
    for b in range(blocks):
        first = slot_ref[b] * META
        obs = slice(b * size, (b + 1) * size)
        meta_ref[pl.ds(first, 2), :] = offset_ref[:, obs].astype(F32)
        meta_ref[pl.ds(first + 2, 1), :] = cells_ref[0:1, obs].astype(F32)
        meta_ref[pl.ds(first + 3, 1), :] = jnp.full((1, size), patch_ref[b], jnp.int32).astype(F32)
    extra = meta16_ref.shape[1] - meta_rows
    for t in range(tiles):
        rows = meta_ref[t * meta_rows : (t + 1) * meta_rows, :]
        if extra:
            rows = jnp.concatenate([rows, jnp.zeros((extra, size), F32)], axis=0)
        meta16_ref[t] = rows.astype(BF16)
    described = pltpu.make_async_copy(
        meta16_ref, send_hbm.at[:, pl.ds(base, meta16_ref.shape[1])], sems.at[len(copies)]
    )
    described.start()

    def finish(c, unused):
        keep(c).wait()
        return unused

    lax.fori_loop(0, chunks, finish, 0)
    for slot in range(tiles * most):
        send(zero_ref, slot).wait()
    described.wait()


def factors(meta, normal):
    off_row, off_col, corner = meta[0:1, :], meta[1:2, :], meta[2:3, :]
    first_row = jnp.floor(corner * (1.0 / PW))
    first_col = corner - first_row * PW

    def factor(count, start, off):
        at = lax.broadcasted_iota(jnp.int32, (count, meta.shape[1]), 0).astype(F32) - start
        delta = at - 1.5 - off
        value = jnp.exp(delta * delta * -0.5)
        return jnp.where((at >= 0.0) & (at < SIDE), value, 0.0)

    def total(off):
        at = lax.broadcasted_iota(jnp.int32, (SIDE, meta.shape[1]), 0).astype(F32)
        delta = at - 1.5 - off
        return jnp.sum(jnp.exp(delta * delta * -0.5), axis=0, keepdims=True)

    rows, cols = factor(PH, first_row, off_row), factor(PW, first_col, off_col)
    if normal:
        rows = rows / (total(off_row) * total(off_col))
    return rows, cols


def outer(rows, cols):
    return (rows[:, None, :] * cols[None, :, :]).reshape(PH * PW, rows.shape[1])


def place(patch):
    row, col = patch // ACROSS, lax.rem(patch, ACROSS)
    return pl.ds(pl.multiple_of(row * PH, PH), PH), pl.ds(pl.multiple_of(col * PW, PW), PW)


def stripe_at(k, way):
    orbits = lax.axis_size("orbits")
    return lax.rem(lax.axis_index("orbits") + way * (orbits - 1 - k) + orbits * orbits, orbits)


def spread_kernel(orbits, most, got_ref, *refs):
    up, down, (patch_ref, acc_ref, dens_ref) = refs[:orbits], refs[orbits : 2 * orbits], refs[2 * orbits :]
    size, channels = got_ref.shape[2], acc_ref.shape[2]
    acc_ref[...] = jnp.zeros(acc_ref.shape, F32)
    dens_ref[...] = jnp.zeros(dens_ref.shape, F32)
    base = most * size

    def tile(t, unused):
        metas = got_ref[t, base:, :].astype(F32)
        patches = [jnp.max(metas[n * META + 3 : n * META + 4, :]).astype(jnp.int32) for n in range(most)]
        for n in range(most):
            patch_ref[t * most + n] = patches[n]
            patch = jnp.maximum(patches[n], 0)
            rows, cols = factors(metas[n * META : (n + 1) * META], False)
            values = got_ref[t, n * size : (n + 1) * size, :]
            result = jnp.dot(outer(rows, cols).astype(BF16), values, preferred_element_type=F32)
            at_row, at_col = place(patch)
            acc_ref[at_row, at_col, :] += result.reshape(PH, PW, channels)
            dens_ref[patch] += lax.dot_general(
                rows.astype(BF16), cols.astype(BF16), (((1,), (1,)), ((), ())), preferred_element_type=F32
            )
        return unused

    lax.fori_loop(0, got_ref.shape[0], tile, 0, unroll=4)
    for k in range(orbits):
        for out_ref, way, rows in ((up[k], 1, EARLY), (down[k], -1, LATE)):
            first = stripe_at(k, way) * SR
            for i, r in enumerate(rows):
                out_ref[i * TC : (i + 1) * TC, :] = acc_ref[first + r].astype(BF16)
        first = stripe_at(k, 1) * SR
        bands = []
        for band in range(SR // PH):
            at = (stripe_at(k, 1) * (SR // PH) + band) * ACROSS
            bands.append(jnp.concatenate([dens_ref[at + c] for c in range(ACROSS)], axis=1))
        up[k][FULL : FULL + SR, :] = jnp.concatenate(bands, axis=0).astype(BF16)
        cells = [acc_ref[first + r, at] for r in LATE for at in (slice(0, EDGE), slice(TC - EDGE, TC))]
        spare = CELLS - len(LATE) * 2 * EDGE
        if spare:
            cells.append(jnp.zeros((spare, channels), F32))
        up[k][FULL + SR :, :] = jnp.concatenate(cells, axis=0).astype(BF16)


def weights_kernel(most, got_ref, out_ref):
    base = most * got_ref.shape[2]

    def tile(t, unused):
        metas = got_ref[t, base:, :].astype(F32)
        for n in range(most):
            rows, cols = factors(metas[n * META : (n + 1) * META], True)
            out_ref[t * most + n] = outer(rows, cols).T.astype(BF16)
        return unused

    lax.fori_loop(0, got_ref.shape[0], tile, 0)


def grid_values(spread, density, weight):
    return (spread / jnp.maximum(density, 1.0) + weight * (density / (1.0 + density))).astype(BF16)


def densities(own_ref, sum_ref):
    tail = slice(FULL, FULL + SR)
    columns = (own_ref[tail, :].astype(F32) + sum_ref[tail, :].astype(F32)).T
    return lambda r: jnp.broadcast_to(columns[:, r : r + 1], (TC, own_ref.shape[1]))


def edge_kernel(own_ref, sum_ref, weight_ref, top_ref, bottom_ref, left_ref, right_ref):
    density = densities(own_ref, sum_ref)
    weight = weight_ref[...]
    low, high = slice(0, EDGE), slice(TC - EDGE, TC)
    cells = own_ref[FULL + SR :, :].astype(F32) + sum_ref[FULL + SR :, :].astype(F32)
    for r in range(SR):
        d = density(r)
        if r in EARLY:
            at = slice(EARLY.index(r) * TC, (EARLY.index(r) + 1) * TC)
            spread = own_ref[at, :].astype(F32) + sum_ref[at, :].astype(F32)
            row = grid_values(spread, d, weight)
            if r < EDGE:
                top_ref[r] = row
            if r >= SR - EDGE:
                bottom_ref[r - (SR - EDGE)] = row
            left_ref[r], right_ref[r] = row[low], row[high]
        else:
            at = LATE.index(r) * 2 * EDGE
            left_ref[r] = grid_values(cells[at : at + EDGE], d[low], weight)
            right_ref[r] = grid_values(cells[at + EDGE : at + 2 * EDGE], d[high], weight)


def conv_kernel(
    own0_ref, sum0_ref, own1_ref, sum1_ref, weight_ref, up_ref, down_ref, left_ref, right_ref,
    w1_ref, b1_ref, w2_ref, b2_ref,
    out_ref, out0_ref, out1_ref, wide_ref, x16_ref, first_ref, wc1_ref, wc2_ref,
):
    channels = out_ref.shape[2]
    width = x16_ref.shape[1]
    for a in range(3):
        for b in range(3):
            at = (slice(a * channels, (a + 1) * channels), slice(b * channels, (b + 1) * channels))
            if a == 2 and b == 2:
                at = (slice(channels, 2 * channels), slice(3 * channels, None))
            wc1_ref[at] = w1_ref[a, b]
            wc2_ref[at] = w2_ref[a, b]
    spare = (slice(0, channels), slice(3 * channels, None))
    wc1_ref[spare] = jnp.zeros((channels, channels), BF16)
    wc2_ref[spare] = jnp.zeros((channels, channels), BF16)
    body = slice(PAD, PAD + TC)
    wide_ref[:, :PAD] = jnp.zeros((wide_ref.shape[0], PAD, channels), F32)
    wide_ref[:, PAD + TC :] = jnp.zeros((wide_ref.shape[0], PAD, channels), F32)
    density = densities(own0_ref, sum0_ref)
    for own_ref, sum_ref, rows in ((own0_ref, sum0_ref, EARLY), (own1_ref, sum1_ref, LATE)):
        for i, r in enumerate(rows):
            at = slice(i * TC, (i + 1) * TC)
            spread = own_ref[at, :].astype(F32) + sum_ref[at, :].astype(F32)
            wide_ref[EDGE + r, body] = grid_values(spread, density(r), weight_ref[...]).astype(F32)
    wide_ref[0:EDGE, body] = up_ref[...].astype(F32)
    wide_ref[EDGE + SR :, body] = down_ref[...].astype(F32)
    wide_ref[:, PAD - EDGE : PAD] = left_ref[...].astype(F32)
    wide_ref[:, PAD + TC : PAD + TC + EDGE] = right_ref[...].astype(F32)
    x16_ref[...] = wide_ref[...].astype(BF16)

    def taps(source, first, count, weights):
        rows = [source[pl.ds(first + a, count)].reshape(count * width, channels) for a in range(3)]
        near = jnp.dot(jnp.concatenate(rows, axis=1), weights[:, : 2 * channels], preferred_element_type=F32)
        more = [source[pl.ds(first + a, count + 1)].reshape((count + 1) * width, channels) for a in range(2)]
        far = jnp.dot(
            jnp.concatenate(more, axis=1), weights[: 2 * channels, 2 * channels :], preferred_element_type=F32
        )
        right = far[: count * width, :channels] + far[width:, channels:]
        return (
            pltpu.roll(near[:, :channels], 1, 0)
            + near[:, channels:]
            + pltpu.roll(right, count * width - 1, 0)
        )

    at_row, at_col = lax.axis_index(("orbits", "rows")), lax.axis_index("cols")
    col = lax.broadcasted_iota(jnp.int32, (width, channels), 0)
    first_col = jnp.where(at_col > 0, PAD - 1, PAD)
    last_col = jnp.where(at_col < lax.axis_size("cols") - 1, PAD + TC, PAD + TC - 1)
    inside = (col >= first_col) & (col <= last_col)
    first_row = jnp.where(at_row > 0, 0, 1)
    last_row = jnp.where(at_row < lax.axis_size(("orbits", "rows")) - 1, SR + 1, SR)
    count = (SR + 2) // 2

    def first_rows(i, unused):
        value = silu(taps(x16_ref, i * count, count, wc1_ref) + b1_ref[...])
        for r in range(count):
            row = i * count + r
            keep = inside & (row >= first_row) & (row <= last_row)
            first_ref[row] = jnp.where(keep, value[r * width : (r + 1) * width], 0.0).astype(BF16)
        return unused

    lax.fori_loop(0, 2, first_rows, 0)
    again = PH

    def second_rows(i, band_ref):
        values = taps(first_ref, i * again, again, wc2_ref) + b2_ref[...]
        for r in range(again):
            row = i * again + r
            value = values[r * width + PAD : r * width + PAD + TC] + wide_ref[row + EDGE, body]
            out_ref[row] = value.astype(BF16)
            band_ref[r] = value.astype(BF16)

    second_rows(0, out0_ref)
    second_rows(1, out1_ref)


def arrives_last(patch):
    band = patch // ACROSS
    stripe = band // BANDS
    return jnp.where(lax.rem(band, BANDS) == 0, stripe == stripe_at(0, -1), stripe == stripe_at(0, 1))


def read_slot(grid_ref, weights_ref, slot, patch):
    at_row, at_col = place(jnp.maximum(patch, 0))
    values = grid_ref[at_row, at_col, :].reshape(PH * PW, grid_ref.shape[2])
    return jnp.dot(weights_ref[slot], values, preferred_element_type=F32).astype(BF16)


def read_kernel(orbits, most, patch_ref, weights_ref, *refs):
    count = orbits - 1
    up, down, (out_ref, list_ref, grid_ref) = refs[:count], refs[count : 2 * count], refs[2 * count :]
    size, slots = out_ref.shape[2], patch_ref.shape[0]
    grid_ref[...] = jnp.zeros(grid_ref.shape, BF16)
    for k in range(count):
        for piece_ref, way, band in ((up[k], 1, 0), (down[k], -1, 1)):
            grid_ref[pl.ds(stripe_at(orbits - 1 - k, -way) * SR + band * PH, PH)] = piece_ref[...]

    def tile(t, unused):
        for n in range(most):
            slot = t * most + n
            out_ref[t, n * size : (n + 1) * size, :] = read_slot(grid_ref, weights_ref, slot, patch_ref[slot])
        return unused

    lax.fori_loop(0, out_ref.shape[0], tile, 0)

    def look(slot, late):
        list_ref[late] = slot
        patch = patch_ref[slot]
        return late + jnp.where((patch >= 0) & arrives_last(jnp.maximum(patch, 0)), 1, 0)

    late = lax.fori_loop(0, slots, look, 0, unroll=8)
    for j in range(GROUP):
        list_ref[late + j] = 0
    list_ref[slots + GROUP] = late


def late_kernel(most, patch_ref, list_ref, weights_ref, up_ref, down_ref, _, out_hbm, grid_ref, result_ref, sems):
    size, slots = result_ref.shape[1], patch_ref.shape[0]
    grid_ref[0:PH], grid_ref[PH:] = up_ref[...], down_ref[...]
    late = list_ref[slots + GROUP]

    def give(i):
        slot = list_ref[i]
        rows = pl.ds(pl.multiple_of(lax.rem(slot, most) * size, size), size)
        return pltpu.make_async_copy(result_ref.at[i], out_hbm.at[slot // most, rows], sems.at[i])

    def some(c, unused):
        for j in range(GROUP):
            i = c * GROUP + j
            slot = list_ref[i]
            patch = lax.rem(jnp.maximum(patch_ref[slot], 0), BANDS * ACROSS)
            result_ref[i] = read_slot(grid_ref, weights_ref, slot, patch)
        for j in range(GROUP):
            i = c * GROUP + j

            @pl.when(i < late)
            def _():
                give(i).start()

        return unused

    def finish(i, unused):
        give(i).wait()
        return unused

    lax.fori_loop(0, (late + GROUP - 1) // GROUP, some, 0)
    lax.fori_loop(0, late, finish, 0)


def final_kernel(tile_ref, feat_ref, got_ref, out_hbm, out_ref, count_ref, sems):
    blocks, size, _ = feat_ref.shape
    chunks = sems.shape[0]
    per = blocks // chunks
    clear(count_ref)

    def give(c):
        at = pl.ds(c * per, per)
        return pltpu.make_async_copy(out_ref.at[at], out_hbm.at[at], sems.at[c])

    def chunk(c, unused):
        for k in range(per):
            b = c * per + k
            t, n = next_slot(tile_ref, count_ref, b)
            mine = got_ref[t, pl.ds(pl.multiple_of(n * size, size), size), :]
            out_ref[b] = (feat_ref[b].astype(F32) + mine.astype(F32)).astype(BF16)
        give(c).start()
        return unused

    lax.fori_loop(0, chunks, chunk, 0)
    for c in range(chunks):
        give(c).wait()


def shifts(axis):
    size = lax.axis_size(axis)
    up = [(i, i + 1) for i in range(size - 1)]
    return up, [(j, i) for i, j in up]


def halo(first, last, axis):
    up, down = shifts(axis)
    return lax.ppermute(last, axis, up), lax.ppermute(first, axis, down)


def turn(x, way):
    size = lax.axis_size("orbits")
    return lax.ppermute(x, "orbits", [(i, (i + way) % size) for i in range(size)])


TIES = {2: 1}


def ring_sums(leading, following):
    orbits = len(leading)
    first, second = leading[0], following[0]
    done = 0

    def step(total, stripes, k, way):
        total = turn(total, way)
        return total + stripes[k] if k < orbits - 1 else total

    for k in range(1, orbits):
        first = step(first, leading, k, 1)
        while done < TIES.get(k, 0):
            done += 1
            second = step(second, following, done, -1)
        if k in TIES:
            first, second = lax.optimization_barrier((first, second))
    while done < orbits - 1:
        done += 1
        second = step(second, following, done, -1)
    return first, second


def ring_gather(x, way):
    pieces = [x]
    for _ in range(lax.axis_size("orbits") - 1):
        pieces.append(turn(pieces[-1], way))
    return pieces


def local(
    obs_feat, obs_offset, obs_cells, block_tile, block_patch, w_embed, b_embed, w_proj, b_proj,
    density_weight, w_first, b_first, w_second, b_second,
):
    channels = obs_feat.shape[1]
    blocks = block_tile.shape[0]
    size = obs_feat.shape[0] // blocks
    plane = ("rows", "cols")
    tiles = lax.axis_size(plane)
    orbits = lax.axis_size("orbits")
    most = max(2, 2 * blocks // tiles)
    slots = tiles * most
    height = orbits * SR
    patches = height // PH * ACROSS
    length = most * size
    meta_rows = max(16, most * META)
    chunks = blocks // 8
    counts = pltpu.SMEM((tiles,), jnp.int32)
    shape = jax.ShapeDtypeStruct
    bias = lambda b: b.reshape(1, channels)
    exchange = lambda x: lax.all_to_all(x, plane, split_axis=0, concat_axis=0, tiled=True)
    vmem = lambda a: pltpu.VMEM(a.shape, a.dtype)

    b_embed, b_proj = bias(b_embed), bias(b_proj)
    features, send = call(
        functools.partial(embed_kernel, most),
        [HBM] * 9,
        [HBM] * 2,
        (shape((blocks, size, channels), BF16), shape((tiles, length + meta_rows, channels), BF16)),
        [
            pltpu.SMEM((blocks,), jnp.int32),
            pltpu.SMEM((blocks,), jnp.int32),
            vmem(obs_offset),
            pltpu.VMEM((8, obs_cells.shape[1]), jnp.int32),
            vmem(obs_feat),
            vmem(w_embed),
            vmem(b_embed),
            vmem(w_proj),
            vmem(b_proj),
            pltpu.VMEM((blocks, size, channels), BF16),
            pltpu.VMEM((size, channels), BF16),
            counts,
            pltpu.SMEM((blocks,), jnp.int32),
            pltpu.VMEM((slots * META + 8, size), F32),
            pltpu.VMEM((tiles, meta_rows, size), BF16),
            pltpu.SemaphoreType.DMA((9,)),
            pltpu.SemaphoreType.DMA((chunks,)),
            pltpu.SemaphoreType.DMA((chunks,)),
            pltpu.SemaphoreType.DMA((slots,)),
        ],
        6 * obs_feat.size * channels,
        8 * obs_feat.size,
        block_tile, block_patch, obs_offset, obs_cells, obs_feat, w_embed, b_embed, w_proj, b_proj,
        limit=LARGE,
    )
    got = exchange(send)

    flops = 2 * slots * size * channels * PH * PW
    early_shape = shape((FULL + SR + CELLS, channels), BF16)
    late_shape = shape((len(LATE) * TC, channels), BF16)
    *bands, patch_of = call(
        functools.partial(spread_kernel, orbits, most),
        [VMEM],
        [VMEM] * (2 * orbits) + [SMEM],
        [early_shape] * orbits + [late_shape] * orbits + [shape((slots,), jnp.int32)],
        [pltpu.VMEM((height, TC, channels), F32), pltpu.VMEM((patches, PH, PW), F32)],
        flops,
        8 * slots * size * channels,
        got,
    )
    bands0, bands1 = bands[:orbits], bands[orbits:]
    sum0, sum1 = ring_sums(bands0, bands1)
    weights = call(
        functools.partial(weights_kernel, most),
        [VMEM],
        VMEM,
        shape((slots, size, PH * PW), BF16),
        [],
        flops,
        4 * slots * size * channels,
        got,
    )
    density_weight = bias(density_weight)
    rows_shape, cols_shape = shape((EDGE, TC, channels), BF16), shape((SR, EDGE, channels), BF16)
    top, bottom, left, right = call(
        edge_kernel,
        [VMEM] * 3,
        [VMEM] * 4,
        [rows_shape] * 2 + [cols_shape] * 2,
        [],
        10000000,
        4 * SR * TC * channels,
        bands0[-1], sum0, density_weight,
    )
    above, below = halo(top, bottom, ("orbits", "rows"))
    left = jnp.concatenate([above[:, :EDGE], left, below[:, :EDGE]], axis=0)
    right = jnp.concatenate([above[:, TC - EDGE :], right, below[:, TC - EDGE :]], axis=0)
    left, right = halo(left, right, "cols")
    sum1, weights = lax.optimization_barrier((sum1, weights))
    width = TC + 2 * PAD
    grid_out, band0, band1 = call(
        conv_kernel,
        [VMEM] * 13,
        [VMEM] * 3,
        [shape((SR, TC, channels), BF16)] + [shape((PH, TC, channels), BF16)] * 2,
        [
            pltpu.VMEM((SR + 4, width, channels), F32),
            pltpu.VMEM((SR + 4, width, channels), BF16),
            pltpu.VMEM((SR + 2, width, channels), BF16),
            pltpu.VMEM((3 * channels, 4 * channels), BF16),
            pltpu.VMEM((3 * channels, 4 * channels), BF16),
        ],
        4 * 9 * SR * TC * channels * channels,
        8 * SR * TC * channels,
        bands0[-1], sum0, bands1[-1], sum1, density_weight, above, below, left, right, w_first, bias(b_first), w_second, bias(b_second),
    )

    up, down = ring_gather(band0, 1), ring_gather(band1, -1)
    read_shape = shape((tiles, length, channels), BF16)
    readings, late = call(
        functools.partial(read_kernel, orbits, most),
        [SMEM] + [VMEM] * (2 * orbits - 1),
        [VMEM, SMEM],
        (read_shape, shape((slots + GROUP + 1,), jnp.int32)),
        [pltpu.VMEM((height, TC, channels), BF16)],
        flops,
        8 * slots * size * channels,
        patch_of, weights, *up[:-1], *down[:-1],
    )
    readings = call(
        functools.partial(late_kernel, most),
        [SMEM] * 2 + [VMEM] * 3 + [HBM],
        HBM,
        read_shape,
        [
            pltpu.VMEM((BANDS * PH, TC, channels), BF16),
            pltpu.VMEM((slots + GROUP, size, channels), BF16),
            pltpu.SemaphoreType.DMA((slots + GROUP,)),
        ],
        flops // 4,
        2 * slots * size * channels,
        patch_of, late, weights, up[-1], down[-1], readings,
        aliases={5: 0},
    )
    back = exchange(readings)
    obs_out = call(
        final_kernel,
        [SMEM] + [VMEM] * 2,
        HBM,
        shape((blocks, size, channels), BF16),
        [pltpu.VMEM((blocks, size, channels), BF16), counts, pltpu.SemaphoreType.DMA((chunks,))],
        1000000,
        8 * obs_feat.size,
        block_tile, features, back,
    )
    return obs_out.reshape(obs_feat.shape), grid_out


def solution(mesh):
    spread_out = ("orbits", "rows", "cols")
    in_specs = (
        P(spread_out, None),
        P(None, spread_out),
        P(None, spread_out),
        P(spread_out),
        P(spread_out),
    ) + (P(),) * 9
    out_specs = (P(spread_out, None), P(("orbits", "rows"), "cols", None))
    return jax.shard_map(local, mesh=mesh, in_specs=in_specs, out_specs=out_specs, check_vma=False)
```

```python
import functools

import jax
import jax.numpy as jnp
from jax import lax
from jax.experimental import pallas as pl
from jax.experimental.pallas import tpu as pltpu
from jax.sharding import PartitionSpec as P

KN = 16
PH = 8
PW = 32
SR = 16
TC = 128
SIDE = 4
PAD = 8
META = 4
BANDS = SR // PH
GROUP = 8
EDGE = 2
EARLY = (0, 1, SR - 2, SR - 1, 2, 3, 4)
LATE = tuple(r for r in range(SR) if r not in EARLY)
FULL = len(EARLY) * TC
CELLS = -(-len(LATE) * 2 * EDGE // 16) * 16
ACROSS = TC // PW
F32 = jnp.float32
BF16 = jnp.bfloat16

VMEM = pl.BlockSpec(memory_space=pltpu.VMEM)
SMEM = pl.BlockSpec(memory_space=pltpu.SMEM)
HBM = pl.BlockSpec(memory_space=pltpu.HBM)
LIMIT = 20 * 1024 * 1024
LARGE = 56 * 1024 * 1024


def call(kernel, in_specs, out_specs, out_shape, scratch, flops, moved, *args, limit=LIMIT, aliases={}):
    return pl.pallas_call(
        kernel,
        in_specs=in_specs,
        out_specs=out_specs,
        out_shape=out_shape,
        scratch_shapes=scratch,
        input_output_aliases=aliases,
        compiler_params=pltpu.CompilerParams(vmem_limit_bytes=limit),
        cost_estimate=pl.CostEstimate(flops=flops, bytes_accessed=moved, transcendentals=0),
    )(*args)


def silu(v):
    half = 0.5 * v
    return half + half * jnp.tanh(half)


def next_slot(tile_ref, count_ref, b):
    t = tile_ref[b]
    n = count_ref[t]
    count_ref[t] = n + 1
    return t, n


def clear(count_ref):
    for t in range(count_ref.shape[0]):
        count_ref[t] = 0


def embed_kernel(
    most, tile_hbm, patch_hbm, offset_hbm, cells_hbm, x_hbm, we_hbm, be_hbm, wp_hbm, bp_hbm,
    feat_hbm, send_hbm,
    tile_ref, patch_ref, offset_ref, cells_ref, x_ref, we_ref, be_ref, wp_ref, bp_ref, feat_ref,
    zero_ref, count_ref, slot_ref, meta_ref, meta16_ref, sems, x_sems, feat_sems, send_sems,
):
    blocks, size, channels = feat_ref.shape
    chunks = x_sems.shape[0]
    per = blocks // chunks
    tiles, meta_rows, base = meta16_ref.shape[0], most * META, most * size
    pairs = (
        (tile_hbm, tile_ref), (patch_hbm, patch_ref), (offset_hbm, offset_ref), (cells_hbm.at[0:8], cells_ref),
        (we_hbm, we_ref), (be_hbm, be_ref), (wp_hbm, wp_ref), (bp_hbm, bp_ref),
    )
    copies = [pltpu.make_async_copy(a, b, sems.at[i]) for i, (a, b) in enumerate(pairs)]

    def rows_of(c):
        return pl.ds(pl.multiple_of(c * per * size, per * size), per * size)

    def fetch(c):
        return pltpu.make_async_copy(x_hbm.at[rows_of(c)], x_ref.at[rows_of(c)], x_sems.at[c])

    def keep(c):
        at = pl.ds(c * per, per)
        return pltpu.make_async_copy(feat_ref.at[at], feat_hbm.at[at], feat_sems.at[c])

    def send(source, slot):
        rows = pl.ds(pl.multiple_of(lax.rem(slot, most) * size, size), size)
        return pltpu.make_async_copy(source, send_hbm.at[slot // most, rows], send_sems.at[slot])

    for copy in copies:
        copy.start()
    for c in range(chunks):
        fetch(c).start()
    zero_ref[...] = jnp.zeros(zero_ref.shape, BF16)
    clear(count_ref)
    row = lax.broadcasted_iota(jnp.int32, meta_ref.shape, 0) % META
    meta_ref[...] = jnp.where(row == 2, -65536.0, jnp.where(row == 3, -1.0, 0.0))
    copies[0].wait()
    for b in range(blocks):
        t, n = next_slot(tile_ref, count_ref, b)
        slot_ref[b] = t * most + n
    for t in range(tiles):
        for n in range(most):

            @pl.when(n >= count_ref[t])
            def _():
                send(zero_ref, t * most + n).start()

    for copy in copies[4:]:
        copy.wait()

    def chunk(c, unused):
        fetch(c).wait()
        hidden = silu(jnp.dot(x_ref[rows_of(c), :], we_ref[...], preferred_element_type=F32) + be_ref[...])
        out = jnp.dot(hidden.astype(BF16), wp_ref[...], preferred_element_type=F32) + bp_ref[...]
        feat_ref[pl.ds(c * per, per)] = out.astype(BF16).reshape(per, size, channels)
        keep(c).start()
        for k in range(per):
            b = c * per + k
            send(feat_ref.at[b], slot_ref[b]).start()
        return unused

    lax.fori_loop(0, chunks, chunk, 0)
    for copy in copies[1:4]:
        copy.wait()
    for b in range(blocks):
        first = slot_ref[b] * META
        obs = slice(b * size, (b + 1) * size)
        meta_ref[pl.ds(first, 2), :] = offset_ref[:, obs].astype(F32)
        meta_ref[pl.ds(first + 2, 1), :] = cells_ref[0:1, obs].astype(F32)
        meta_ref[pl.ds(first + 3, 1), :] = jnp.full((1, size), patch_ref[b], jnp.int32).astype(F32)
    extra = meta16_ref.shape[1] - meta_rows
    for t in range(tiles):
        rows = meta_ref[t * meta_rows : (t + 1) * meta_rows, :]
        if extra:
            rows = jnp.concatenate([rows, jnp.zeros((extra, size), F32)], axis=0)
        meta16_ref[t] = rows.astype(BF16)
    described = pltpu.make_async_copy(
        meta16_ref, send_hbm.at[:, pl.ds(base, meta16_ref.shape[1])], sems.at[len(copies)]
    )
    described.start()

    def finish(c, unused):
        keep(c).wait()
        return unused

    lax.fori_loop(0, chunks, finish, 0)
    for slot in range(tiles * most):
        send(zero_ref, slot).wait()
    described.wait()


def factors(meta, normal):
    off_row, off_col, corner = meta[0:1, :], meta[1:2, :], meta[2:3, :]
    first_row = jnp.floor(corner * (1.0 / PW))
    first_col = corner - first_row * PW

    def factor(count, start, off):
        at = lax.broadcasted_iota(jnp.int32, (count, meta.shape[1]), 0).astype(F32) - start
        delta = at - 1.5 - off
        value = jnp.exp(delta * delta * -0.5)
        return jnp.where((at >= 0.0) & (at < SIDE), value, 0.0)

    def total(off):
        at = lax.broadcasted_iota(jnp.int32, (SIDE, meta.shape[1]), 0).astype(F32)
        delta = at - 1.5 - off
        return jnp.sum(jnp.exp(delta * delta * -0.5), axis=0, keepdims=True)

    rows, cols = factor(PH, first_row, off_row), factor(PW, first_col, off_col)
    if normal:
        rows = rows / (total(off_row) * total(off_col))
    return rows, cols


def outer(rows, cols):
    return (rows[:, None, :] * cols[None, :, :]).reshape(PH * PW, rows.shape[1])


def place(patch):
    row, col = patch // ACROSS, lax.rem(patch, ACROSS)
    return pl.ds(pl.multiple_of(row * PH, PH), PH), pl.ds(pl.multiple_of(col * PW, PW), PW)


def stripe_at(k, way):
    orbits = lax.axis_size("orbits")
    return lax.rem(lax.axis_index("orbits") + way * (orbits - 1 - k) + orbits * orbits, orbits)


def spread_kernel(orbits, most, got_ref, *refs):
    up, down, (patch_ref, acc_ref, dens_ref) = refs[:orbits], refs[orbits : 2 * orbits], refs[2 * orbits :]
    size, channels = got_ref.shape[2], acc_ref.shape[2]
    acc_ref[...] = jnp.zeros(acc_ref.shape, F32)
    dens_ref[...] = jnp.zeros(dens_ref.shape, F32)
    base = most * size

    def tile(t, unused):
        metas = got_ref[t, base:, :].astype(F32)
        patches = [jnp.max(metas[n * META + 3 : n * META + 4, :]).astype(jnp.int32) for n in range(most)]
        for n in range(most):
            patch_ref[t * most + n] = patches[n]
            patch = jnp.maximum(patches[n], 0)
            rows, cols = factors(metas[n * META : (n + 1) * META], False)
            values = got_ref[t, n * size : (n + 1) * size, :]
            result = jnp.dot(outer(rows, cols).astype(BF16), values, preferred_element_type=F32)
            at_row, at_col = place(patch)
            acc_ref[at_row, at_col, :] += result.reshape(PH, PW, channels)
            dens_ref[patch] += lax.dot_general(
                rows.astype(BF16), cols.astype(BF16), (((1,), (1,)), ((), ())), preferred_element_type=F32
            )
        return unused

    lax.fori_loop(0, got_ref.shape[0], tile, 0, unroll=4)
    for k in range(orbits):
        for out_ref, way, rows in ((up[k], 1, EARLY), (down[k], -1, LATE)):
            first = stripe_at(k, way) * SR
            for i, r in enumerate(rows):
                out_ref[i * TC : (i + 1) * TC, :] = acc_ref[first + r].astype(BF16)
        first = stripe_at(k, 1) * SR
        bands = []
        for band in range(SR // PH):
            at = (stripe_at(k, 1) * (SR // PH) + band) * ACROSS
            bands.append(jnp.concatenate([dens_ref[at + c] for c in range(ACROSS)], axis=1))
        up[k][FULL : FULL + SR, :] = jnp.concatenate(bands, axis=0).astype(BF16)
        cells = [acc_ref[first + r, at] for r in LATE for at in (slice(0, EDGE), slice(TC - EDGE, TC))]
        spare = CELLS - len(LATE) * 2 * EDGE
        if spare:
            cells.append(jnp.zeros((spare, channels), F32))
        up[k][FULL + SR :, :] = jnp.concatenate(cells, axis=0).astype(BF16)


def weights_kernel(most, got_ref, out_ref):
    base = most * got_ref.shape[2]

    def tile(t, unused):
        metas = got_ref[t, base:, :].astype(F32)
        for n in range(most):
            rows, cols = factors(metas[n * META : (n + 1) * META], True)
            out_ref[t * most + n] = outer(rows, cols).T.astype(BF16)
        return unused

    lax.fori_loop(0, got_ref.shape[0], tile, 0)


def grid_values(spread, density, weight):
    return (spread / jnp.maximum(density, 1.0) + weight * (density / (1.0 + density))).astype(BF16)


def densities(own_ref, sum_ref):
    tail = slice(FULL, FULL + SR)
    columns = (own_ref[tail, :].astype(F32) + sum_ref[tail, :].astype(F32)).T
    return lambda r: jnp.broadcast_to(columns[:, r : r + 1], (TC, own_ref.shape[1]))


def edge_kernel(own_ref, sum_ref, weight_ref, top_ref, bottom_ref, left_ref, right_ref):
    density = densities(own_ref, sum_ref)
    weight = weight_ref[...]
    low, high = slice(0, EDGE), slice(TC - EDGE, TC)
    cells = own_ref[FULL + SR :, :].astype(F32) + sum_ref[FULL + SR :, :].astype(F32)
    for r in range(SR):
        d = density(r)
        if r in EARLY:
            at = slice(EARLY.index(r) * TC, (EARLY.index(r) + 1) * TC)
            spread = own_ref[at, :].astype(F32) + sum_ref[at, :].astype(F32)
            row = grid_values(spread, d, weight)
            if r < EDGE:
                top_ref[r] = row
            if r >= SR - EDGE:
                bottom_ref[r - (SR - EDGE)] = row
            left_ref[r], right_ref[r] = row[low], row[high]
        else:
            at = LATE.index(r) * 2 * EDGE
            left_ref[r] = grid_values(cells[at : at + EDGE], d[low], weight)
            right_ref[r] = grid_values(cells[at + EDGE : at + 2 * EDGE], d[high], weight)


def conv_kernel(
    own0_ref, sum0_ref, own1_ref, sum1_ref, weight_ref, up_ref, down_ref, left_ref, right_ref,
    w1_ref, b1_ref, w2_ref, b2_ref,
    out_ref, out0_ref, out1_ref, wide_ref, x16_ref, first_ref, wc1_ref, wc2_ref,
):
    channels = out_ref.shape[2]
    width = x16_ref.shape[1]
    for a in range(3):
        for b in range(3):
            at = (slice(a * channels, (a + 1) * channels), slice(b * channels, (b + 1) * channels))
            if a == 2 and b == 2:
                at = (slice(channels, 2 * channels), slice(3 * channels, None))
            wc1_ref[at] = w1_ref[a, b]
            wc2_ref[at] = w2_ref[a, b]
    spare = (slice(0, channels), slice(3 * channels, None))
    wc1_ref[spare] = jnp.zeros((channels, channels), BF16)
    wc2_ref[spare] = jnp.zeros((channels, channels), BF16)
    body = slice(PAD, PAD + TC)
    wide_ref[:, :PAD] = jnp.zeros((wide_ref.shape[0], PAD, channels), F32)
    wide_ref[:, PAD + TC :] = jnp.zeros((wide_ref.shape[0], PAD, channels), F32)
    density = densities(own0_ref, sum0_ref)
    for own_ref, sum_ref, rows in ((own0_ref, sum0_ref, EARLY), (own1_ref, sum1_ref, LATE)):
        for i, r in enumerate(rows):
            at = slice(i * TC, (i + 1) * TC)
            spread = own_ref[at, :].astype(F32) + sum_ref[at, :].astype(F32)
            wide_ref[EDGE + r, body] = grid_values(spread, density(r), weight_ref[...]).astype(F32)
    wide_ref[0:EDGE, body] = up_ref[...].astype(F32)
    wide_ref[EDGE + SR :, body] = down_ref[...].astype(F32)
    wide_ref[:, PAD - EDGE : PAD] = left_ref[...].astype(F32)
    wide_ref[:, PAD + TC : PAD + TC + EDGE] = right_ref[...].astype(F32)
    x16_ref[...] = wide_ref[...].astype(BF16)

    def taps(source, first, count, weights):
        rows = [source[pl.ds(first + a, count)].reshape(count * width, channels) for a in range(3)]
        near = jnp.dot(jnp.concatenate(rows, axis=1), weights[:, : 2 * channels], preferred_element_type=F32)
        more = [source[pl.ds(first + a, count + 1)].reshape((count + 1) * width, channels) for a in range(2)]
        far = jnp.dot(
            jnp.concatenate(more, axis=1), weights[: 2 * channels, 2 * channels :], preferred_element_type=F32
        )
        right = far[: count * width, :channels] + far[width:, channels:]
        return (
            pltpu.roll(near[:, :channels], 1, 0)
            + near[:, channels:]
            + pltpu.roll(right, count * width - 1, 0)
        )

    at_row, at_col = lax.axis_index(("orbits", "rows")), lax.axis_index("cols")
    col = lax.broadcasted_iota(jnp.int32, (width, channels), 0)
    first_col = jnp.where(at_col > 0, PAD - 1, PAD)
    last_col = jnp.where(at_col < lax.axis_size("cols") - 1, PAD + TC, PAD + TC - 1)
    inside = (col >= first_col) & (col <= last_col)
    first_row = jnp.where(at_row > 0, 0, 1)
    last_row = jnp.where(at_row < lax.axis_size(("orbits", "rows")) - 1, SR + 1, SR)
    count = (SR + 2) // 2

    def first_rows(i, unused):
        value = silu(taps(x16_ref, i * count, count, wc1_ref) + b1_ref[...])
        for r in range(count):
            row = i * count + r
            keep = inside & (row >= first_row) & (row <= last_row)
            first_ref[row] = jnp.where(keep, value[r * width : (r + 1) * width], 0.0).astype(BF16)
        return unused

    lax.fori_loop(0, 2, first_rows, 0, unroll=True)
    again = PH

    def second_rows(i, band_ref):
        values = taps(first_ref, i * again, again, wc2_ref) + b2_ref[...]
        for r in range(again):
            row = i * again + r
            value = values[r * width + PAD : r * width + PAD + TC] + wide_ref[row + EDGE, body]
            out_ref[row] = value.astype(BF16)
            band_ref[r] = value.astype(BF16)

    second_rows(0, out0_ref)
    second_rows(1, out1_ref)


def arrives_last(patch):
    band = patch // ACROSS
    stripe = band // BANDS
    return jnp.where(lax.rem(band, BANDS) == 0, stripe == stripe_at(0, -1), stripe == stripe_at(0, 1))


def read_slot(grid_ref, weights_ref, slot, patch):
    at_row, at_col = place(jnp.maximum(patch, 0))
    values = grid_ref[at_row, at_col, :].reshape(PH * PW, grid_ref.shape[2])
    return jnp.dot(weights_ref[slot], values, preferred_element_type=F32).astype(BF16)


def read_kernel(orbits, most, patch_ref, weights_ref, *refs):
    count = orbits - 1
    up, down, (out_ref, list_ref, grid_ref) = refs[:count], refs[count : 2 * count], refs[2 * count :]
    size, slots = out_ref.shape[2], patch_ref.shape[0]
    grid_ref[...] = jnp.zeros(grid_ref.shape, BF16)
    for k in range(count):
        for piece_ref, way, band in ((up[k], 1, 0), (down[k], -1, 1)):
            grid_ref[pl.ds(stripe_at(orbits - 1 - k, -way) * SR + band * PH, PH)] = piece_ref[...]

    def tile(t, unused):
        for n in range(most):
            slot = t * most + n
            out_ref[t, n * size : (n + 1) * size, :] = read_slot(grid_ref, weights_ref, slot, patch_ref[slot])
        return unused

    lax.fori_loop(0, out_ref.shape[0], tile, 0)

    def look(slot, late):
        list_ref[late] = slot
        patch = patch_ref[slot]
        return late + jnp.where((patch >= 0) & arrives_last(jnp.maximum(patch, 0)), 1, 0)

    late = lax.fori_loop(0, slots, look, 0, unroll=8)
    for j in range(GROUP):
        list_ref[late + j] = 0
    list_ref[slots + GROUP] = late


def late_kernel(most, patch_ref, list_ref, weights_ref, up_ref, down_ref, _, out_hbm, grid_ref, result_ref, sems):
    size, slots = result_ref.shape[1], patch_ref.shape[0]
    grid_ref[0:PH], grid_ref[PH:] = up_ref[...], down_ref[...]
    late = list_ref[slots + GROUP]

    def give(i):
        slot = list_ref[i]
        rows = pl.ds(pl.multiple_of(lax.rem(slot, most) * size, size), size)
        return pltpu.make_async_copy(result_ref.at[i], out_hbm.at[slot // most, rows], sems.at[i])

    def some(c, unused):
        for j in range(GROUP):
            i = c * GROUP + j
            slot = list_ref[i]
            patch = lax.rem(jnp.maximum(patch_ref[slot], 0), BANDS * ACROSS)
            result_ref[i] = read_slot(grid_ref, weights_ref, slot, patch)
        for j in range(GROUP):
            i = c * GROUP + j

            @pl.when(i < late)
            def _():
                give(i).start()

        return unused

    def finish(i, unused):
        give(i).wait()
        return unused

    lax.fori_loop(0, (late + GROUP - 1) // GROUP, some, 0)
    lax.fori_loop(0, late, finish, 0)


def final_kernel(tile_ref, feat_ref, got_ref, out_hbm, out_ref, count_ref, sems):
    blocks, size, _ = feat_ref.shape
    chunks = sems.shape[0]
    per = blocks // chunks
    clear(count_ref)

    def give(c):
        at = pl.ds(c * per, per)
        return pltpu.make_async_copy(out_ref.at[at], out_hbm.at[at], sems.at[c])

    def chunk(c, unused):
        for k in range(per):
            b = c * per + k
            t, n = next_slot(tile_ref, count_ref, b)
            mine = got_ref[t, pl.ds(pl.multiple_of(n * size, size), size), :]
            out_ref[b] = (feat_ref[b].astype(F32) + mine.astype(F32)).astype(BF16)
        give(c).start()
        return unused

    lax.fori_loop(0, chunks, chunk, 0)
    for c in range(chunks):
        give(c).wait()


def shifts(axis):
    size = lax.axis_size(axis)
    up = [(i, i + 1) for i in range(size - 1)]
    return up, [(j, i) for i, j in up]


def halo(first, last, axis):
    up, down = shifts(axis)
    return lax.ppermute(last, axis, up), lax.ppermute(first, axis, down)


def turn(x, way):
    size = lax.axis_size("orbits")
    return lax.ppermute(x, "orbits", [(i, (i + way) % size) for i in range(size)])


TIES = {2: 1}


def ring_sums(leading, following):
    orbits = len(leading)
    first, second = leading[0], following[0]
    done = 0

    def step(total, stripes, k, way):
        total = turn(total, way)
        return total + stripes[k] if k < orbits - 1 else total

    for k in range(1, orbits):
        first = step(first, leading, k, 1)
        while done < TIES.get(k, 0):
            done += 1
            second = step(second, following, done, -1)
        if k in TIES:
            first, second = lax.optimization_barrier((first, second))
    while done < orbits - 1:
        done += 1
        second = step(second, following, done, -1)
    return first, second


def ring_gather(x, way):
    pieces = [x]
    for _ in range(lax.axis_size("orbits") - 1):
        pieces.append(turn(pieces[-1], way))
    return pieces


def local(
    obs_feat, obs_offset, obs_cells, block_tile, block_patch, w_embed, b_embed, w_proj, b_proj,
    density_weight, w_first, b_first, w_second, b_second,
):
    channels = obs_feat.shape[1]
    blocks = block_tile.shape[0]
    size = obs_feat.shape[0] // blocks
    plane = ("rows", "cols")
    tiles = lax.axis_size(plane)
    orbits = lax.axis_size("orbits")
    most = max(2, 2 * blocks // tiles)
    slots = tiles * most
    height = orbits * SR
    patches = height // PH * ACROSS
    length = most * size
    meta_rows = max(16, most * META)
    chunks = blocks // 8
    counts = pltpu.SMEM((tiles,), jnp.int32)
    shape = jax.ShapeDtypeStruct
    bias = lambda b: b.reshape(1, channels)
    exchange = lambda x: lax.all_to_all(x, plane, split_axis=0, concat_axis=0, tiled=True)
    vmem = lambda a: pltpu.VMEM(a.shape, a.dtype)

    b_embed, b_proj = bias(b_embed), bias(b_proj)
    features, send = call(
        functools.partial(embed_kernel, most),
        [HBM] * 9,
        [HBM] * 2,
        (shape((blocks, size, channels), BF16), shape((tiles, length + meta_rows, channels), BF16)),
        [
            pltpu.SMEM((blocks,), jnp.int32),
            pltpu.SMEM((blocks,), jnp.int32),
            vmem(obs_offset),
            pltpu.VMEM((8, obs_cells.shape[1]), jnp.int32),
            vmem(obs_feat),
            vmem(w_embed),
            vmem(b_embed),
            vmem(w_proj),
            vmem(b_proj),
            pltpu.VMEM((blocks, size, channels), BF16),
            pltpu.VMEM((size, channels), BF16),
            counts,
            pltpu.SMEM((blocks,), jnp.int32),
            pltpu.VMEM((slots * META + 8, size), F32),
            pltpu.VMEM((tiles, meta_rows, size), BF16),
            pltpu.SemaphoreType.DMA((9,)),
            pltpu.SemaphoreType.DMA((chunks,)),
            pltpu.SemaphoreType.DMA((chunks,)),
            pltpu.SemaphoreType.DMA((slots,)),
        ],
        6 * obs_feat.size * channels,
        8 * obs_feat.size,
        block_tile, block_patch, obs_offset, obs_cells, obs_feat, w_embed, b_embed, w_proj, b_proj,
        limit=LARGE,
    )
    got = exchange(send)

    flops = 2 * slots * size * channels * PH * PW
    early_shape = shape((FULL + SR + CELLS, channels), BF16)
    late_shape = shape((len(LATE) * TC, channels), BF16)
    *bands, patch_of = call(
        functools.partial(spread_kernel, orbits, most),
        [VMEM],
        [VMEM] * (2 * orbits) + [SMEM],
        [early_shape] * orbits + [late_shape] * orbits + [shape((slots,), jnp.int32)],
        [pltpu.VMEM((height, TC, channels), F32), pltpu.VMEM((patches, PH, PW), F32)],
        flops,
        8 * slots * size * channels,
        got,
    )
    bands0, bands1 = bands[:orbits], bands[orbits:]
    sum0, sum1 = ring_sums(bands0, bands1)
    weights = call(
        functools.partial(weights_kernel, most),
        [VMEM],
        VMEM,
        shape((slots, size, PH * PW), BF16),
        [],
        flops,
        4 * slots * size * channels,
        got,
    )
    density_weight = bias(density_weight)
    rows_shape, cols_shape = shape((EDGE, TC, channels), BF16), shape((SR, EDGE, channels), BF16)
    top, bottom, left, right = call(
        edge_kernel,
        [VMEM] * 3,
        [VMEM] * 4,
        [rows_shape] * 2 + [cols_shape] * 2,
        [],
        10000000,
        4 * SR * TC * channels,
        bands0[-1], sum0, density_weight,
    )
    above, below = halo(top, bottom, ("orbits", "rows"))
    left = jnp.concatenate([above[:, :EDGE], left, below[:, :EDGE]], axis=0)
    right = jnp.concatenate([above[:, TC - EDGE :], right, below[:, TC - EDGE :]], axis=0)
    left, right = halo(left, right, "cols")
    sum1, weights = lax.optimization_barrier((sum1, weights))
    width = TC + 2 * PAD
    grid_out, band0, band1 = call(
        conv_kernel,
        [VMEM] * 13,
        [VMEM] * 3,
        [shape((SR, TC, channels), BF16)] + [shape((PH, TC, channels), BF16)] * 2,
        [
            pltpu.VMEM((SR + 4, width, channels), F32),
            pltpu.VMEM((SR + 4, width, channels), BF16),
            pltpu.VMEM((SR + 2, width, channels), BF16),
            pltpu.VMEM((3 * channels, 4 * channels), BF16),
            pltpu.VMEM((3 * channels, 4 * channels), BF16),
        ],
        4 * 9 * SR * TC * channels * channels,
        8 * SR * TC * channels,
        bands0[-1], sum0, bands1[-1], sum1, density_weight, above, below, left, right, w_first, bias(b_first), w_second, bias(b_second),
    )

    up, down = ring_gather(band0, 1), ring_gather(band1, -1)
    read_shape = shape((tiles, length, channels), BF16)
    readings, late = call(
        functools.partial(read_kernel, orbits, most),
        [SMEM] + [VMEM] * (2 * orbits - 1),
        [VMEM, SMEM],
        (read_shape, shape((slots + GROUP + 1,), jnp.int32)),
        [pltpu.VMEM((height, TC, channels), BF16)],
        flops,
        8 * slots * size * channels,
        patch_of, weights, *up[:-1], *down[:-1],
    )
    readings = call(
        functools.partial(late_kernel, most),
        [SMEM] * 2 + [VMEM] * 3 + [HBM],
        HBM,
        read_shape,
        [
            pltpu.VMEM((BANDS * PH, TC, channels), BF16),
            pltpu.VMEM((slots + GROUP, size, channels), BF16),
            pltpu.SemaphoreType.DMA((slots + GROUP,)),
        ],
        flops // 4,
        2 * slots * size * channels,
        patch_of, late, weights, up[-1], down[-1], readings,
        aliases={5: 0},
    )
    back = exchange(readings)
    obs_out = call(
        final_kernel,
        [SMEM] + [VMEM] * 2,
        HBM,
        shape((blocks, size, channels), BF16),
        [pltpu.VMEM((blocks, size, channels), BF16), counts, pltpu.SemaphoreType.DMA((chunks,))],
        1000000,
        8 * obs_feat.size,
        block_tile, features, back,
    )
    return obs_out.reshape(obs_feat.shape), grid_out


def solution(mesh):
    spread_out = ("orbits", "rows", "cols")
    in_specs = (
        P(spread_out, None),
        P(None, spread_out),
        P(None, spread_out),
        P(spread_out),
        P(spread_out),
    ) + (P(),) * 9
    out_specs = (P(spread_out, None), P(("orbits", "rows"), "cols", None))
    return jax.shard_map(local, mesh=mesh, in_specs=in_specs, out_specs=out_specs, check_vma=False)
```
